32 devices in a mesh: grp: 2 (over y), wide: 4 (over z), sec: 2 (over x), sub: 2 (over core).
Axes of the slice: x: 2, y: 2, z: 4, core: 2. Of those that a mesh axis runs over, the one named last changes fastest.
Arguments:
- tokens: bfloat16 [128, 4096], P(('grp', 'wide', 'sec', 'sub')), parts along dimension 0, may hold values from -6 to 6
- expert_ids: int32 [128, 8], P(('grp', 'wide', 'sec', 'sub')), parts along dimension 0, may hold values from 0 to 31, all different within a row; in each aligned block of 4 rows (0 to 3, 4 to 7, ...) at most 2 rows name the same one
- gate_numer: int32 [128, 8], P(('grp', 'wide', 'sec', 'sub')), parts along dimension 0, may hold values from 1 to 1024
- w_gate: bfloat16 [32, 1536, 4096], P('wide', ('sec', 'sub')), may hold values from -0.09375 to 0.09375
- w_up: bfloat16 [32, 1536, 4096], P('wide', ('sec', 'sub')), may hold values from -0.09375 to 0.09375
- w_down: bfloat16 [32, 1536, 4096], P('wide', ('sec', 'sub')), may hold values from -0.15625 to 0.15625
Outputs:
- mixed: bfloat16 [128, 4096], P(('grp', 'wide', 'sec', 'sub')), parts along dimension 0
The draws below stay inside these ranges and needn't reach their ends.
There are 2 independent parts, one for each index of `grp`. The reference program is written for one: setup_inputs(seed, part) draws one part's arguments, and reference() takes and returns one part's arrays. A program takes and returns all parts, laid end to end along the dimension named above; an argument that names none is the same for every part. Nothing has to cross between parts.
Inputs may be any that keep to these rules, and one draw needn't show every extreme that they name: `expert_ids`: each row names 8 different experts. In the 4 rows of one device no expert is named by more than 2 rows, a bound that some block reaches.
All inputs are finite; a program needn't handle non-finite values.
Results may differ from the reference program's by a relative error of at most 0.012.
Values may be sent and summed in bfloat16 or wider, within the bound.
No kernel may reach another device: no remote copies, remote signals or barrier semaphores. Data moves between devices by JAX's collectives and lax.ppermute only.
A program may use at most 192 MiB of HBM per device.

```python
import math
import jax
import jax.numpy as jnp
import numpy as np
from jax import lax

D = 4096
FF = 1536
TOP = 8
EXPERTS = 32
TOK_DEV = 4
CAP = 2
FF_DEV = 384
TOKENS = 64


def touch_ends(entries, rng, low, high):
    dims = entries.shape
    spot = [jax.random.randint(jax.random.fold_in(rng, axis), (), 0, dims[axis]) for axis in range(len(dims))]
    entries = entries.at[tuple(spot)].set(low)
    longest = dims.index(max(dims))
    spot[longest] = (spot[longest] + 1) % dims[longest]
    return entries.at[tuple(spot)].set(high)


def block_scale(key, shape, pieces, smallest, high):
    level = 1.0
    for dim, parts in pieces:
        heights = jax.random.uniform(jax.random.fold_in(jax.random.fold_in(key, 6), dim), (parts,), jnp.float32, smallest / len(pieces), high / len(pieces))
        level = level * jnp.repeat(jnp.exp(heights), shape[dim] // parts).reshape((-1,) + (1,) * (len(shape) - 1 - dim))
    return level


def deal_out(key, own, number, rows, number_of, top, bound, skew):
    ranking = jax.random.permutation(key, number_of)
    crowded, ordinary = shares(number_of, rows * top, bound, skew, True), shares(number_of, rows * top, bound, skew, False)
    places = jnp.arange(number_of)

    def named(sizes, turn):
        used = int((sizes > 0).sum())
        fixed = max(1, used // 4)
        passed = fixed + (places - fixed + turn * (used - fixed)) % max(1, number_of - fixed)
        return jnp.zeros((number_of,), jnp.int32).at[ranking[jnp.where(places < fixed, places, passed)]].set(jnp.asarray(sizes, jnp.int32))

    sizes = jnp.where(number % 4 == 0, named(crowded, number // 4), named(ordinary, number - number // 4 - 1))
    mixed = jax.random.permutation(jax.random.fold_in(own, 3), number_of)
    donor, sink = mixed[0:number_of // 2 * 2:2], mixed[1:number_of // 2 * 2:2]
    room = jnp.minimum(sizes[donor] - 1, bound - sizes[sink]) // 2
    room = jnp.where((donor == ranking[0]) | (sink == ranking[0]) | (sizes[sink] == 0), 0, jnp.maximum(room, 0))
    passed = jax.random.randint(jax.random.fold_in(own, 4), (number_of // 2,), 0, 1 << 20) % (room + 1)
    sizes = sizes.at[donor].add(-passed).at[sink].add(passed)
    members = jnp.searchsorted(jnp.cumsum(sizes), jnp.arange(rows * top), side="right").astype(jnp.int32)
    table = members.reshape(top, rows).T
    table = table[jax.random.permutation(jax.random.fold_in(own, 1), rows)]
    turn = jax.random.randint(jax.random.fold_in(own, 2), (rows, 1), 0, top)
    return jnp.take_along_axis(table, (jnp.arange(top)[None, :] + turn) % top, axis=1)


def shares(amount, total, reach, skew, full):
    loads = [(1 << 20) // math.isqrt(rank ** skew) + 1 for rank in range(1, amount + 1)]
    largest = reach if full else min(reach, max(-(-total // amount), total * loads[0] // sum(loads)))
    least = 1 if total - largest >= amount - 1 else 0
    holding, surplus = [largest] + [least] * (amount - 1), total - largest - least * (amount - 1)
    while surplus > 0:
        free = [i for i in range(1, amount) if holding[i] < largest] or [i for i in range(1, amount) if holding[i] < reach]
        mass, left = sum([loads[i] for i in free]), surplus
        for i in free:
            addition = min(reach - holding[i], max(1, left * loads[i] // mass), surplus)
            holding[i] = holding[i] + addition
            surplus = surplus - addition
    return np.array(holding)


def centred(rng, extent, spread, reach, cuts=(), kind=jnp.bfloat16):
    drawn = jax.random.normal(rng, extent, jnp.float32) * spread
    if len(cuts) > 0:
        drawn = block_scale(rng, extent, cuts, -0.22, 0.18) * drawn
    return jnp.clip(drawn, min=-reach, max=reach).astype(kind)


def setup_inputs(seed: int = 0, part: int = 0) -> dict:
    splits = jax.random.split(jax.random.key(seed), 7)
    own_keys = jax.random.split(jax.random.fold_in(splits[6], part), 7)
    tokens = centred(own_keys[0], (TOKENS, D), 1.0, 6.0, ((0, 16),))
    expert_ids_keys = jax.random.split(jax.random.fold_in(own_keys[1], 1), TOKENS // TOK_DEV)
    expert_ids_turns = jax.random.permutation(jax.random.fold_in(own_keys[1], 3), TOKENS // TOK_DEV)
    expert_ids = jax.vmap(lambda own, number: deal_out(jax.random.fold_in(own_keys[1], 2), own, number, TOK_DEV, EXPERTS, TOP, CAP, 2))(expert_ids_keys, expert_ids_turns).reshape((TOKENS, TOP))
    gate_numer = touch_ends(jax.random.randint(own_keys[2], (TOKENS, TOP), 1, 1025), jax.random.fold_in(own_keys[2], 1), 1, 1024).astype(jnp.int32)
    w_gate = centred(splits[3], (EXPERTS, FF, D), D ** -0.5, 0.09375, ((0, 4), (1, 4)))
    w_up = centred(splits[4], (EXPERTS, FF, D), D ** -0.5, 0.09375, ((0, 4), (1, 4)))
    w_down = centred(splits[5], (EXPERTS, FF, D), FF ** -0.5, 0.15625, ((0, 4), (1, 4)))
    return {"tokens": tokens, "expert_ids": expert_ids, "gate_numer": gate_numer, "w_gate": w_gate, "w_up": w_up, "w_down": w_down}


def block_slots(block_ids):
    onehot = (block_ids[:, :, None] == jnp.arange(EXPERTS, dtype=jnp.int32)).astype(jnp.int32)
    per_row = jnp.sum(onehot, axis=1)
    before = jnp.cumsum(per_row, axis=0) - per_row
    return jnp.sum(onehot * before[:, None, :], axis=-1).astype(jnp.int32)


def reference(tokens, expert_ids, gate_numer, w_gate, w_up, w_down):
    blocks = TOKENS // TOK_DEV
    block_ids = expert_ids.reshape(blocks, TOK_DEV, TOP)
    slot_of = jax.vmap(block_slots)(block_ids)
    token_rows = tokens.reshape(blocks, TOK_DEV, D).astype(jnp.float32)
    slot_range = jnp.arange(CAP, dtype=jnp.int32)
    sections = FF // FF_DEV

    def one_expert(expert):
        chosen = (block_ids == expert)[..., None] & (slot_of[..., None] == slot_range)
        select = jnp.sum(chosen.astype(jnp.float32), axis=2)
        buffer = jnp.einsum('brc,brd->bcd', select, token_rows).astype(jnp.bfloat16).reshape(blocks * CAP, D)
        gate_out = jnp.dot(buffer, w_gate[expert].T, preferred_element_type=jnp.float32)
        up_out = jnp.dot(buffer, w_up[expert].T, preferred_element_type=jnp.float32)
        hidden = (jax.nn.silu(gate_out) * up_out).astype(jnp.bfloat16)
        down_rows = w_down[expert]
        summed = jnp.zeros((blocks * CAP, D), jnp.float32)
        for section in range(sections):
            lower = section * FF_DEV
            partial_value = jnp.dot(hidden[:, lower:lower + FF_DEV], down_rows[lower:lower + FF_DEV],
                              preferred_element_type=jnp.float32).astype(jnp.bfloat16)
            partial_value = lax.optimization_barrier(partial_value)
            summed = summed + partial_value.astype(jnp.float32)
        return summed.astype(jnp.bfloat16).reshape(blocks, CAP, D)

    results = lax.map(one_expert, jnp.arange(EXPERTS, dtype=jnp.int32))
    numer = gate_numer.astype(jnp.float32)
    weight = (numer / jnp.sum(numer, axis=-1, keepdims=True)).reshape(blocks, TOK_DEV, TOP)
    block_index = jnp.broadcast_to(jnp.arange(blocks, dtype=jnp.int32)[:, None, None], block_ids.shape)
    picked = results[block_ids, block_index, slot_of]
    mixed = jnp.sum(weight[..., None] * picked.astype(jnp.float32), axis=2)
    return mixed.reshape(TOKENS, D).astype(jnp.bfloat16)
```

```python
import jax
import jax.numpy as jnp
from jax import lax
from jax.sharding import PartitionSpec as P

EXPERTS = 32
PART = ("wide", "sec", "sub")


def row_weights(expert_ids, gate_numer):
    numer = gate_numer.astype(jnp.float32)
    weight = numer / jnp.sum(numer, axis=-1, keepdims=True)
    chosen = expert_ids[:, :, None] == jnp.arange(EXPERTS, dtype=jnp.int32)
    return jnp.sum(jnp.where(chosen, weight[:, :, None], 0.0), axis=1)


def local(tokens, expert_ids, gate_numer, w_gate, w_up, w_down):
    local_count, ff_dev, depth = w_gate.shape
    weight = row_weights(expert_ids, gate_numer)
    high = weight.astype(jnp.bfloat16)
    low = (weight - high.astype(jnp.float32)).astype(jnp.bfloat16)
    pad = jnp.zeros((tokens.shape[0], 128 - 2 * EXPERTS), jnp.bfloat16)
    row = jnp.concatenate([tokens, high, low, pad], axis=1)
    rows = lax.all_gather(row, PART, axis=0, tiled=True)
    x = rows[:, :depth]
    both = rows[:, depth:depth + EXPERTS].astype(jnp.float32) + rows[
        :, depth + EXPERTS:depth + 2 * EXPERTS
    ].astype(jnp.float32)
    first = lax.axis_index("wide") * local_count
    mine = lax.dynamic_slice_in_dim(both, first, local_count, axis=1)
    gate_out = jnp.einsum("nd,jfd->njf", x, w_gate, preferred_element_type=jnp.float32)
    up_out = jnp.einsum("nd,jfd->njf", x, w_up, preferred_element_type=jnp.float32)
    hidden = (jax.nn.silu(gate_out) * up_out * mine[:, :, None]).astype(jnp.bfloat16)
    share = jnp.einsum("njf,jfd->nd", hidden, w_down, preferred_element_type=jnp.float32)
    return lax.psum_scatter(
        share.astype(jnp.bfloat16), PART, scatter_dimension=0, tiled=True
    )


def solution(mesh):
    rows = P(("grp", "wide", "sec", "sub"), None)
    weights = P("wide", ("sec", "sub"), None)
    return jax.shard_map(
        local,
        mesh=mesh,
        in_specs=(rows, rows, rows, weights, weights, weights),
        out_specs=rows,
        check_vma=False,
    )
```

```python
import jax
import jax.numpy as jnp
from jax import lax
from jax.sharding import PartitionSpec as P

EXPERTS = 32


def row_weights(expert_ids, gate_numer):
    numer = gate_numer.astype(jnp.float32)
    weight = numer / jnp.sum(numer, axis=-1, keepdims=True)
    chosen = expert_ids[:, :, None] == jnp.arange(EXPERTS, dtype=jnp.int32)
    return jnp.sum(jnp.where(chosen, weight[:, :, None], 0.0), axis=1)


def shift(x, axis, size, by):
    return lax.ppermute(x, axis, [(i, (i + by) % size) for i in range(size)])


def gather(x, axis, size):
    return jnp.concatenate([x] + [shift(x, axis, size, -s) for s in range(1, size)], axis=0)


def scatter(total, axis, size):
    blocks = total.reshape(size, total.shape[0] // size, total.shape[1])
    arrived = [
        shift(blocks[s].astype(jnp.bfloat16), axis, size, s).astype(jnp.float32)
        for s in range(1, size)
    ]
    return sum(arrived, blocks[0])


def build(axes):
    def local(tokens, expert_ids, gate_numer, w_gate, w_up, w_down):
        local_count, ff_dev, depth = w_gate.shape
        weight = row_weights(expert_ids, gate_numer)
        high = weight.astype(jnp.bfloat16)
        low = (weight - high.astype(jnp.float32)).astype(jnp.bfloat16)
        pad = jnp.zeros((tokens.shape[0], 128 - 2 * EXPERTS), jnp.bfloat16)
        rows = jnp.concatenate([tokens, high, low, pad], axis=1)
        for axis in axes:
            rows = gather(rows, *axis)
        x = rows[:, :depth]
        both = rows[:, depth:depth + EXPERTS].astype(jnp.float32) + rows[
            :, depth + EXPERTS:depth + 2 * EXPERTS
        ].astype(jnp.float32)
        first = lax.axis_index("wide") * local_count
        mine = lax.dynamic_slice_in_dim(both, first, local_count, axis=1)
        gate_out = jnp.einsum("nd,jfd->njf", x, w_gate, preferred_element_type=jnp.float32)
        up_out = jnp.einsum("nd,jfd->njf", x, w_up, preferred_element_type=jnp.float32)
        hidden = (jax.nn.silu(gate_out) * up_out * mine[:, :, None]).astype(jnp.bfloat16)
        total = jnp.einsum("njf,jfd->nd", hidden, w_down, preferred_element_type=jnp.float32)
        for axis in reversed(axes):
            total = scatter(total, *axis)
        return total.astype(jnp.bfloat16)

    return local


def solution(mesh):
    rows = P(("grp", "wide", "sec", "sub"), None)
    weights = P("wide", ("sec", "sub"), None)
    axes = [(name, mesh.shape[name]) for name in ("wide", "sec", "sub")]
    return jax.shard_map(
        build(axes),
        mesh=mesh,
        in_specs=(rows, rows, rows, weights, weights, weights),
        out_specs=rows,
        check_vma=False,
    )
```

```python
import functools

import jax
import jax.numpy as jnp
from jax import lax
from jax.experimental import pallas as pl
from jax.experimental.pallas import tpu as pltpu
from jax.sharding import PartitionSpec as P

EXPERTS = 32
SIDE = 128
SLOTS = 4


def shift(x, axis, size, by):
    return lax.ppermute(x, axis, [(i, (i + by) % size) for i in range(size)])


def gather(x, axis, size):
    return jnp.concatenate([x] + [shift(x, axis, size, -s) for s in range(1, size)], axis=0)


def scatter(total, axis, size):
    blocks = total.reshape(size, total.shape[0] // size, total.shape[1])
    arrived = [
        shift(blocks[s].astype(jnp.bfloat16), axis, size, s).astype(jnp.float32)
        for s in range(1, size)
    ]
    return sum(arrived, blocks[0])


def with_routing(tokens, expert_ids, gate_numer):
    side = jnp.concatenate([expert_ids, gate_numer >> 5, gate_numer & 31], axis=1)
    pad = jnp.zeros((tokens.shape[0], SIDE - side.shape[1]), jnp.bfloat16)
    return jnp.concatenate([tokens, side.astype(jnp.bfloat16), pad], axis=1)


def dense_weights(side, top):
    ids = side[:, :top]
    numer = side[:, top:2 * top] * 32.0 + side[:, 2 * top:3 * top]
    weight = numer / jnp.sum(numer, axis=-1, keepdims=True)
    lane = lax.broadcasted_iota(jnp.int32, (side.shape[0], SIDE), 1)
    expert = jnp.where(lane < EXPERTS, lane, lane - EXPERTS).astype(jnp.float32)
    full = jnp.zeros((side.shape[0], SIDE), jnp.float32)
    for k in range(top):
        full = full + jnp.where(expert == ids[:, k:k + 1], weight[:, k:k + 1], 0.0)
    high = full.astype(jnp.bfloat16).astype(jnp.float32)
    return jnp.where(lane < EXPERTS, high, full - high).astype(jnp.bfloat16)


def layer(top, ff_dev, row_block, rows_ref, gate_ref, up_ref, down_ref, out_ref,
          gates, ups, downs, weights, hidden, sem):
    units, depth = down_ref.shape
    step_units = gates.shape[1]
    steps = units // step_units
    count = rows_ref.shape[0]

    def copies(step, slot):
        span = pl.ds(pl.multiple_of(step * step_units, step_units), step_units)
        return [
            pltpu.make_async_copy(src.at[span], dst.at[slot], sem.at[i, slot])
            for i, (src, dst) in enumerate(
                [(gate_ref, gates), (up_ref, ups), (down_ref, downs)]
            )
        ]

    for step in range(min(SLOTS - 1, steps)):
        for copy in copies(step, step):
            copy.start()

    first = lax.axis_index("wide") * (units // ff_dev)

    def each_block(body):
        if count == row_block:
            body(pl.ds(0, row_block))
        else:
            @pl.loop(0, count // row_block)
            def _(b):
                body(pl.ds(pl.multiple_of(b * row_block, row_block), row_block))

    def prepare(block):
        side = rows_ref[block, depth:depth + SIDE].astype(jnp.float32)
        weights[block, :] = dense_weights(side, top)
        out_ref[block, :] = jnp.zeros((row_block, depth), jnp.float32)

    each_block(prepare)

    @pl.loop(0, steps)
    def _(step):
        slot = lax.rem(step, SLOTS)

        @pl.when(step + SLOTS - 1 < steps)
        def _():
            for copy in copies(step + SLOTS - 1, lax.rem(step + SLOTS - 1, SLOTS)):
                copy.start()

        expert = lax.broadcasted_iota(jnp.int32, (SIDE, step_units), 0)
        place = jnp.where(expert < EXPERTS, expert, expert - EXPERTS) - first
        unit = step * step_units + lax.broadcasted_iota(jnp.int32, (SIDE, step_units), 1)
        low = place * ff_dev
        pick = ((unit >= low) & (unit < low + ff_dev) & (expert < 2 * EXPERTS))
        pick = jnp.where(pick, 1.0, 0.0).astype(jnp.bfloat16)
        now = copies(step, slot)
        now[0].wait()
        now[1].wait()

        def first_half(block):
            x = rows_ref[block, :depth]
            last = (((1,), (1,)), ((), ()))
            g = lax.dot_general(x, gates[slot], last, preferred_element_type=jnp.float32)
            u = lax.dot_general(x, ups[slot], last, preferred_element_type=jnp.float32)
            scale = jnp.dot(weights[block, :], pick, preferred_element_type=jnp.float32)
            hidden[block, :] = (g / (1.0 + jnp.exp(-g)) * u * scale).astype(jnp.bfloat16)

        each_block(first_half)
        now[2].wait()

        def second_half(block):
            out_ref[block, :] += jnp.dot(
                hidden[block, :], downs[slot], preferred_element_type=jnp.float32
            )

        each_block(second_half)


def build(axes):
    def local(tokens, expert_ids, gate_numer, w_gate, w_up, w_down):
        local_count, ff_dev, depth = w_gate.shape
        units = local_count * ff_dev
        step_units = next(n for n in range(256, 0, -16) if units % n == 0)
        rows = with_routing(tokens, expert_ids, gate_numer)
        for axis in axes:
            rows = gather(rows, *axis)
        count = rows.shape[0]
        total = pl.pallas_call(
            functools.partial(layer, expert_ids.shape[1], ff_dev, min(count, 64)),
            out_shape=jax.ShapeDtypeStruct((count, depth), jnp.float32),
            in_specs=[pl.BlockSpec(memory_space=pltpu.VMEM)]
            + [pl.BlockSpec(memory_space=pl.ANY)] * 3,
            out_specs=pl.BlockSpec(memory_space=pltpu.VMEM),
            scratch_shapes=[pltpu.VMEM((SLOTS, step_units, depth), jnp.bfloat16)] * 3
            + [
                pltpu.VMEM((count, SIDE), jnp.bfloat16),
                pltpu.VMEM((count, step_units), jnp.bfloat16),
                pltpu.SemaphoreType.DMA((3, SLOTS)),
            ],
            compiler_params=pltpu.CompilerParams(vmem_limit_bytes=56 << 20),
            cost_estimate=pl.CostEstimate(
                flops=6 * count * units * depth,
                bytes_accessed=6 * units * depth,
                transcendentals=count * units,
            ),
            name="expert_layer",
        )(
            rows,
            w_gate.reshape(units, depth),
            w_up.reshape(units, depth),
            w_down.reshape(units, depth),
        )
        for axis in reversed(axes):
            total = scatter(total, *axis)
        return total.astype(jnp.bfloat16)

    return local


def solution(mesh):
    rows = P(("grp", "wide", "sec", "sub"), None)
    weights = P("wide", ("sec", "sub"), None)
    axes = [(name, mesh.shape[name]) for name in ("wide", "sec", "sub")]
    return jax.shard_map(
        build(axes),
        mesh=mesh,
        in_specs=(rows, rows, rows, weights, weights, weights),
        out_specs=rows,
        check_vma=False,
    )
```

```python
import functools

import jax
import jax.numpy as jnp
from jax import lax
from jax.experimental import pallas as pl
from jax.experimental.pallas import tpu as pltpu
from jax.sharding import PartitionSpec as P

EXPERTS = 32
SIDE = 128
SLOTS = 3
TILE = 1024
EARLY = (2, 1, 1)
GRANT = 22 << 20


def swap(x, axis, size, by):
    return lax.ppermute(x, axis, [(i, i ^ by) for i in range(size)])


def with_routing(tokens_ref, ids_ref, numer_ref, out_ref):
    rows, depth = tokens_ref.shape
    top = ids_ref.shape[1]
    out_ref[:, :depth] = tokens_ref[...]
    ids, numer = ids_ref[...], numer_ref[...]
    pad = jnp.zeros((rows, SIDE - 3 * top), jnp.int32)
    side = jnp.concatenate([ids, numer >> 5, numer & 31, pad], axis=1)
    out_ref[:, depth:] = side.astype(jnp.float32).astype(jnp.bfloat16)


def dense_weights(side, top):
    ids = side[:, :top]
    numer = side[:, top:2 * top] * 32.0 + side[:, 2 * top:3 * top]
    weight = numer / jnp.sum(numer, axis=-1, keepdims=True)
    lane = lax.broadcasted_iota(jnp.int32, (side.shape[0], SIDE), 1)
    expert = jnp.where(lane < EXPERTS, lane, lane - EXPERTS).astype(jnp.float32)
    full = jnp.zeros((side.shape[0], SIDE), jnp.float32)
    for k in range(top):
        full = full + jnp.where(expert == ids[:, k:k + 1], weight[:, k:k + 1], 0.0)
    high = full.astype(jnp.bfloat16).astype(jnp.float32)
    return jnp.where(lane < EXPERTS, high, full - high).astype(jnp.bfloat16)


def bring(at, gate_ref, up_ref, down_ref, after_ref, gates, ups, downs, end_ref, sem):
    pieces = sem.shape[1]
    size = gates.shape[0] // pieces
    started = []
    for p in range(pieces):
        for i, (ref, held) in enumerate([(gate_ref, gates), (up_ref, ups), (down_ref, downs)]):
            started.append(
                pltpu.make_async_copy(
                    ref.at[pl.ds(at + p * size, size)], held.at[pl.ds(p * size, size)], sem.at[i, p]
                )
            )
    for copy in started:
        copy.start()
    end_ref[...] = jnp.zeros_like(end_ref)
    for copy in started:
        copy.wait()


def layer(top, ff_dev, row_block, step_units, parts, rows_ref, *refs):
    held, refs = refs[:3 * parts], refs[3 * parts:]
    (gate_ref, up_ref, down_ref, out_ref, gates, ups, downs, weights, hidden, sem) = refs
    units, depth = down_ref.shape
    steps = units // step_units
    count = rows_ref.shape[0]
    early = sum(held[3 * p].shape[0] for p in range(parts)) // step_units

    def copies(step, slot):
        span = pl.ds(pl.multiple_of(step * step_units, step_units), step_units)
        return [
            pltpu.make_async_copy(src.at[span], dst.at[slot], sem.at[i, slot])
            for i, (src, dst) in enumerate(
                [(gate_ref, gates), (up_ref, ups), (down_ref, downs)]
            )
        ]

    for step in range(early, min(early + SLOTS - 1, steps)):
        for copy in copies(step, step - early):
            copy.start()

    first = lax.axis_index("wide") * (units // ff_dev)

    def each_block(body):
        if count == row_block:
            body(pl.ds(0, row_block))
        else:
            @pl.loop(0, count // row_block)
            def _(b):
                body(pl.ds(pl.multiple_of(b * row_block, row_block), row_block))

    def prepare(block):
        side = rows_ref[block, depth:depth + SIDE].astype(jnp.float32)
        weights[block, :] = dense_weights(side, top)
        out_ref[block, :] = jnp.zeros((row_block, depth), jnp.float32)

    each_block(prepare)

    def work(step, gate, up, down, ready=None):
        expert = lax.broadcasted_iota(jnp.int32, (SIDE, step_units), 0)
        place = jnp.where(expert < EXPERTS, expert, expert - EXPERTS) - first
        unit = step * step_units + lax.broadcasted_iota(jnp.int32, (SIDE, step_units), 1)
        low = place * ff_dev
        pick = (unit >= low) & (unit < low + ff_dev) & (expert < 2 * EXPERTS)
        pick = jnp.where(pick, 1.0, 0.0).astype(jnp.bfloat16)
        if ready is not None:
            ready[0].wait()
            ready[1].wait()

        def first_half(block):
            def add(c, sums):
                cols = pl.ds(pl.multiple_of(c * TILE, TILE), TILE)
                x = rows_ref[block, cols]
                last = (((1,), (1,)), ((), ()))
                return tuple(
                    total + lax.dot_general(x, w[:, cols], last, preferred_element_type=jnp.float32)
                    for total, w in zip(sums, (gate, up))
                )

            zero = jnp.zeros((row_block, step_units), jnp.float32)
            g, u = lax.fori_loop(0, depth // TILE, add, (zero, zero))
            scale = jnp.dot(weights[block, :], pick, preferred_element_type=jnp.float32)
            hidden[block, :] = (g / (1.0 + jnp.exp(-g)) * u * scale).astype(jnp.bfloat16)

        each_block(first_half)
        if ready is not None:
            ready[2].wait()

        def second_half(block):
            h = hidden[block, :]

            @pl.loop(0, depth // TILE)
            def _(c):
                cols = pl.ds(pl.multiple_of(c * TILE, TILE), TILE)
                out_ref[block, cols] += jnp.dot(h, down[:, cols], preferred_element_type=jnp.float32)

        each_block(second_half)

    done = 0
    for p in range(parts):
        inside = held[3 * p].shape[0] // step_units

        @pl.loop(0, inside)
        def _(s):
            span = pl.ds(pl.multiple_of(s * step_units, step_units), step_units)
            work(done + s, *[ref.at[span] for ref in held[3 * p:3 * p + 3]])

        done += inside

    @pl.loop(early, steps)
    def _(step):
        slot = lax.rem(step - early, SLOTS)

        @pl.when(step + SLOTS - 1 < steps)
        def _():
            for copy in copies(step + SLOTS - 1, lax.rem(step - early + SLOTS - 1, SLOTS)):
                copy.start()

        work(step, gates.at[slot], ups.at[slot], downs.at[slot], copies(step, slot))


def build(axes):
    def local(tokens, expert_ids, gate_numer, w_gate, w_up, w_down):
        local_count, ff_dev, depth = w_gate.shape
        units = local_count * ff_dev
        step_units = next(n for n in range(256, 0, -16) if units % n == 0)
        weights = [w.reshape(units, depth) for w in (w_gate, w_up, w_down)]
        weights = [pltpu.with_memory_space_constraint(w, pltpu.HBM) for w in weights]
        rows = pl.pallas_call(
            with_routing,
            out_shape=jax.ShapeDtypeStruct((tokens.shape[0], depth + SIDE), jnp.bfloat16),
            in_specs=[pl.BlockSpec(memory_space=pltpu.VMEM)] * 3,
            out_specs=pl.BlockSpec(memory_space=pltpu.VMEM),
            compiler_params=pltpu.CompilerParams(vmem_limit_bytes=2 << 20),
            name="with_routing",
        )(tokens, expert_ids, gate_numer)
        hops = []
        for axis, size in axes:
            by = size // 2
            while by:
                hops.append((axis, size, by))
                by //= 2
        held = []
        at = 0
        for number, hop in enumerate(hops):
            theirs = swap(rows, *hop)
            steps = EARLY[number] if number < len(EARLY) and units >= 8 * step_units else 0
            if steps:
                span = steps * step_units
                *brought, end = pl.pallas_call(
                    functools.partial(bring, at),
                    out_shape=[pltpu.VMEM((span, depth), jnp.bfloat16)] * 3
                    + [jax.ShapeDtypeStruct((8, 128), jnp.float32)],
                    in_specs=[pl.BlockSpec(memory_space=pltpu.HBM)] * 3
                    + [pl.BlockSpec(memory_space=pl.ANY)],
                    out_specs=[pl.BlockSpec(memory_space=pltpu.VMEM)] * 4,
                    scratch_shapes=[pltpu.SemaphoreType.DMA((3, 2 * steps))],
                    compiler_params=pltpu.CompilerParams(vmem_limit_bytes=1 << 20),
                    cost_estimate=pl.CostEstimate(
                        flops=0, bytes_accessed=6 * span * depth, transcendentals=0
                    ),
                    name="bring_weights",
                )(*weights, rows)
                held += brought
                at += span
                theirs = theirs + end[0, 0].astype(jnp.bfloat16)
            rows = jnp.concatenate([rows, theirs], axis=0)
        count = rows.shape[0]
        total = pl.pallas_call(
            functools.partial(
                layer, expert_ids.shape[1], ff_dev, min(count, 64), step_units, len(held) // 3
            ),
            out_shape=jax.ShapeDtypeStruct((count, depth), jnp.float32),
            in_specs=[pl.BlockSpec(memory_space=pltpu.VMEM)] * (1 + len(held))
            + [pl.BlockSpec(memory_space=pltpu.HBM)] * 3,
            out_specs=pl.BlockSpec(memory_space=pltpu.VMEM),
            scratch_shapes=[pltpu.VMEM((SLOTS, step_units, depth), jnp.bfloat16)] * 3
            + [
                pltpu.VMEM((count, SIDE), jnp.bfloat16),
                pltpu.VMEM((count, step_units), jnp.bfloat16),
                pltpu.SemaphoreType.DMA((3, SLOTS)),
            ],
            compiler_params=pltpu.CompilerParams(vmem_limit_bytes=GRANT),
            cost_estimate=pl.CostEstimate(
                flops=6 * count * units * depth,
                bytes_accessed=6 * units * depth,
                transcendentals=count * units,
            ),
            name="expert_layer",
        )(rows, *held, *weights)
        for hop in reversed(hops):
            half = total.shape[0] // 2
            theirs = swap(total[half:].astype(jnp.bfloat16), *hop)
            total = total[:half] + theirs.astype(jnp.float32)
        return total.astype(jnp.bfloat16)

    return local


def solution(mesh):
    rows = P(("grp", "wide", "sec", "sub"), None)
    weights = P("wide", ("sec", "sub"), None)
    axes = [(name, mesh.shape[name]) for name in ("wide", "sec", "sub")]
    return jax.shard_map(
        build(axes),
        mesh=mesh,
        in_specs=(rows, rows, rows, weights, weights, weights),
        out_specs=rows,
        check_vma=False,
    )
```

```python
import functools

import jax
import jax.numpy as jnp
from jax import lax
from jax.experimental import pallas as pl
from jax.experimental.pallas import tpu as pltpu
from jax.sharding import PartitionSpec as P

EXPERTS = 32
SIDE = 128
SLOTS = 2
EARLY = (2, 2, 1)
GRANT = 19 << 20

VMEM = pl.BlockSpec(memory_space=pltpu.VMEM)
HBM = pl.BlockSpec(memory_space=pltpu.HBM)
LAST = (((1,), (1,)), ((), ()))


def swap(x, axis, size, by):
    return lax.ppermute(x, axis, [(i, i ^ by) for i in range(size)])


def with_routing(tokens_ref, ids_ref, numer_ref, out_ref, ids, numer, sem):
    rows, depth = tokens_ref.shape
    top = ids_ref.shape[1]
    pairs = [(tokens_ref, out_ref.at[:, pl.ds(0, depth)]), (ids_ref, ids), (numer_ref, numer)]
    started = [pltpu.make_async_copy(a, b, sem.at[i]) for i, (a, b) in enumerate(pairs)]
    for copy in started:
        copy.start()
    for copy in started:
        copy.wait()
    pad = jnp.zeros((rows, SIDE - 3 * top), jnp.int32)
    side = jnp.concatenate([ids[...], numer[...] >> 5, numer[...] & 31, pad], axis=1)
    out_ref[:, depth:] = side.astype(jnp.float32).astype(jnp.bfloat16)


def join(mine_ref, theirs_ref, *refs):
    out_ref = refs[-1]
    count = mine_ref.shape[0]
    out_ref[:count, :] = mine_ref[...]
    out_ref[count:, :] = theirs_ref[...]


def bring(at, gate_ref, up_ref, down_ref, after_ref, gates, ups, downs, end_ref, sem):
    pieces = sem.shape[1]
    size = gates.shape[0] // pieces
    started = []
    for p in range(pieces):
        for i, (ref, held) in enumerate([(gate_ref, gates), (up_ref, ups), (down_ref, downs)]):
            started.append(
                pltpu.make_async_copy(
                    ref.at[pl.ds(at + p * size, size)], held.at[pl.ds(p * size, size)], sem.at[i, p]
                )
            )
    for copy in started:
        copy.start()
    end_ref[...] = jnp.zeros_like(end_ref)
    for copy in started:
        copy.wait()


def dense_weights(side, top):
    ids = side[:, :top]
    numer = side[:, top:2 * top] * 32.0 + side[:, 2 * top:3 * top]
    weight = numer / jnp.sum(numer, axis=-1, keepdims=True)
    lane = lax.broadcasted_iota(jnp.int32, (side.shape[0], SIDE), 1)
    expert = jnp.where(lane < EXPERTS, lane, lane - EXPERTS).astype(jnp.float32)
    full = jnp.zeros((side.shape[0], SIDE), jnp.float32)
    for k in range(top):
        full = full + jnp.where(expert == ids[:, k:k + 1], weight[:, k:k + 1], 0.0)
    high = full.astype(jnp.bfloat16).astype(jnp.float32)
    return jnp.where(lane < EXPERTS, high, full - high).astype(jnp.bfloat16)


def layer(top, ff_dev, row_block, step_units, parts, mine_ref, theirs_ref, *refs):
    held, refs = refs[:3 * parts], refs[3 * parts:]
    (gate_ref, up_ref, down_ref, keep_ref, send_ref,
     rows_ref, total, gates, ups, downs, weights, hidden, sem) = refs
    units, depth = down_ref.shape
    steps = units // step_units
    count = rows_ref.shape[0]
    half = count // 2
    early = sum(held[3 * p].shape[0] for p in range(parts)) // step_units

    def copies(step, slot):
        span = pl.ds(pl.multiple_of(step * step_units, step_units), step_units)
        return [
            pltpu.make_async_copy(src.at[span], dst.at[slot], sem.at[i, slot])
            for i, (src, dst) in enumerate(
                [(gate_ref, gates), (up_ref, ups), (down_ref, downs)]
            )
        ]

    for step in range(early, min(early + SLOTS - 1, steps)):
        for copy in copies(step, step - early):
            copy.start()

    first = lax.axis_index("wide") * (units // ff_dev)

    def each_block(body):
        if count == row_block:
            body(pl.ds(0, row_block))
        else:
            @pl.loop(0, count // row_block)
            def _(b):
                body(pl.ds(pl.multiple_of(b * row_block, row_block), row_block))

    rows_ref[:half, :] = mine_ref[...]
    rows_ref[half:, :] = theirs_ref[...]

    def prepare(block):
        side = rows_ref[block, depth:depth + SIDE].astype(jnp.float32)
        weights[block, :] = dense_weights(side, top)
        total[block, :] = jnp.zeros((row_block, depth), jnp.float32)

    each_block(prepare)

    def work(step, gate, up, down, ready=None):
        expert = lax.broadcasted_iota(jnp.int32, (SIDE, step_units), 0)
        place = jnp.where(expert < EXPERTS, expert, expert - EXPERTS) - first
        unit = step * step_units + lax.broadcasted_iota(jnp.int32, (SIDE, step_units), 1)
        low = place * ff_dev
        pick = (unit >= low) & (unit < low + ff_dev) & (expert < 2 * EXPERTS)
        pick = jnp.where(pick, 1.0, 0.0).astype(jnp.bfloat16)
        if ready is not None:
            ready[0].wait()
            ready[1].wait()

        def first_half(block):
            x = rows_ref[block, :depth]
            g = lax.dot_general(x, gate[...], LAST, preferred_element_type=jnp.float32)
            u = lax.dot_general(x, up[...], LAST, preferred_element_type=jnp.float32)
            scale = jnp.dot(weights[block, :], pick, preferred_element_type=jnp.float32)
            hidden[block, :] = (g / (1.0 + jnp.exp(-g)) * u * scale).astype(jnp.bfloat16)

        each_block(first_half)
        if ready is not None:
            ready[2].wait()

        def second_half(block):
            total[block, :] += jnp.dot(
                hidden[block, :], down[...], preferred_element_type=jnp.float32
            )

        each_block(second_half)

    done = 0
    for p in range(parts):
        inside = held[3 * p].shape[0] // step_units

        @pl.loop(0, inside)
        def _(s):
            span = pl.ds(pl.multiple_of(s * step_units, step_units), step_units)
            work(done + s, *[ref.at[span] for ref in held[3 * p:3 * p + 3]])

        done += inside

    @pl.loop(early, steps)
    def _(step):
        slot = lax.rem(step - early, SLOTS)

        @pl.when(step + SLOTS - 1 < steps)
        def _():
            for copy in copies(step + SLOTS - 1, lax.rem(step - early + SLOTS - 1, SLOTS)):
                copy.start()

        work(step, gates.at[slot], ups.at[slot], downs.at[slot], copies(step, slot))

    keep_ref[...] = total[:half, :]
    send_ref[...] = total[half:, :].astype(jnp.bfloat16)


def build(axes):
    def local(tokens, expert_ids, gate_numer, w_gate, w_up, w_down):
        local_count, ff_dev, depth = w_gate.shape
        units = local_count * ff_dev
        top = expert_ids.shape[1]
        step_units = next(n for n in range(256, 0, -16) if units % n == 0)
        weights = [w.reshape(units, depth) for w in (w_gate, w_up, w_down)]
        weights = [pltpu.with_memory_space_constraint(w, pltpu.HBM) for w in weights]
        small = pltpu.CompilerParams(vmem_limit_bytes=2 << 20)
        own = (tokens, expert_ids, gate_numer)
        own = [pltpu.with_memory_space_constraint(a, pltpu.HBM) for a in own]
        rows = pl.pallas_call(
            with_routing,
            out_shape=jax.ShapeDtypeStruct((tokens.shape[0], depth + SIDE), jnp.bfloat16),
            in_specs=[HBM] * 3,
            out_specs=VMEM,
            scratch_shapes=[
                pltpu.VMEM(expert_ids.shape, jnp.int32),
                pltpu.VMEM(gate_numer.shape, jnp.int32),
                pltpu.SemaphoreType.DMA((3,)),
            ],
            compiler_params=small,
            name="with_routing",
        )(*own)
        hops = []
        for axis, size in axes:
            by = size // 2
            while by:
                hops.append((axis, size, by))
                by //= 2
        held = []
        at = 0
        for number, hop in enumerate(hops):
            theirs = swap(rows, *hop)
            steps = EARLY[number] if number < len(EARLY) and units >= 8 * step_units else 0
            ends = []
            if steps:
                span = steps * step_units
                *brought, end = pl.pallas_call(
                    functools.partial(bring, at),
                    out_shape=[pltpu.VMEM((span, depth), jnp.bfloat16)] * 3
                    + [jax.ShapeDtypeStruct((8, 128), jnp.float32)],
                    in_specs=[HBM] * 3 + [pl.BlockSpec(memory_space=pl.ANY)],
                    out_specs=[VMEM] * 4,
                    scratch_shapes=[pltpu.SemaphoreType.DMA((3, 2 * steps))],
                    compiler_params=small,
                    cost_estimate=pl.CostEstimate(
                        flops=0, bytes_accessed=6 * span * depth, transcendentals=0
                    ),
                    name="bring_weights",
                )(*weights, rows)
                held += brought
                at += span
                ends = [end]
            if hop is hops[-1]:
                break
            count = rows.shape[0]
            if count <= 64:
                rows = pl.pallas_call(
                    join,
                    out_shape=jax.ShapeDtypeStruct((2 * count, depth + SIDE), jnp.bfloat16),
                    in_specs=[VMEM] * 2 + [pl.BlockSpec(memory_space=pl.ANY)] * len(ends),
                    out_specs=VMEM,
                    compiler_params=small,
                    name="join",
                )(rows, theirs, *ends)
            else:
                rows = jnp.concatenate([rows, theirs], axis=0)
        half = rows.shape[0]
        count = 2 * half
        keep, send = pl.pallas_call(
            functools.partial(layer, top, ff_dev, min(count, 64), step_units, len(held) // 3),
            out_shape=[
                jax.ShapeDtypeStruct((half, depth), jnp.float32),
                jax.ShapeDtypeStruct((half, depth), jnp.bfloat16),
            ],
            in_specs=[VMEM] * (2 + len(held)) + [HBM] * 3,
            out_specs=[VMEM] * 2,
            scratch_shapes=[
                pltpu.VMEM((count, depth + SIDE), jnp.bfloat16),
                pltpu.VMEM((count, depth), jnp.float32),
            ]
            + [pltpu.VMEM((SLOTS, step_units, depth), jnp.bfloat16)] * 3
            + [
                pltpu.VMEM((count, SIDE), jnp.bfloat16),
                pltpu.VMEM((count, step_units), jnp.bfloat16),
                pltpu.SemaphoreType.DMA((3, SLOTS)),
            ],
            compiler_params=pltpu.CompilerParams(
                vmem_limit_bytes=GRANT if count == 64 else 60 << 20
            ),
            cost_estimate=pl.CostEstimate(
                flops=6 * count * units * depth,
                bytes_accessed=6 * (units - at) * depth,
                transcendentals=count * units,
            ),
            name="expert_layer",
        )(rows, theirs, *held, *weights)
        total = keep + swap(send, *hops[-1]).astype(jnp.float32)
        for hop in reversed(hops[:-1]):
            half = total.shape[0] // 2
            theirs = swap(total[half:].astype(jnp.bfloat16), *hop)
            total = total[:half] + theirs.astype(jnp.float32)
        return total.astype(jnp.bfloat16)

    return local


def solution(mesh):
    rows = P(("grp", "wide", "sec", "sub"), None)
    weights = P("wide", ("sec", "sub"), None)
    axes = [(name, mesh.shape[name]) for name in ("wide", "sec", "sub")]
    return jax.shard_map(
        build(axes),
        mesh=mesh,
        in_specs=(rows, rows, rows, weights, weights, weights),
        out_specs=rows,
        check_vma=False,
    )
```

```python
import functools

import jax
import jax.numpy as jnp
from jax import lax
from jax.experimental import pallas as pl
from jax.experimental.pallas import tpu as pltpu
from jax.sharding import PartitionSpec as P

EXPERTS = 32
SIDE = 128
SLOTS = 2
EARLY = (2, 2, 1)
GRANT = 19 << 20

VMEM = pl.BlockSpec(memory_space=pltpu.VMEM)
HBM = pl.BlockSpec(memory_space=pltpu.HBM)
LAST = (((1,), (1,)), ((), ()))


def swap(x, axis, size, by):
    return lax.ppermute(x, axis, [(i, i ^ by) for i in range(size)])


def with_routing(tokens_ref, ids_ref, numer_ref, out_ref, ids, numer, sem):
    rows, depth = tokens_ref.shape
    top = ids_ref.shape[1]
    pairs = [(tokens_ref, out_ref.at[:, pl.ds(0, depth)]), (ids_ref, ids), (numer_ref, numer)]
    started = [pltpu.make_async_copy(a, b, sem.at[i]) for i, (a, b) in enumerate(pairs)]
    for copy in started:
        copy.start()
    for copy in started:
        copy.wait()
    pad = jnp.zeros((rows, SIDE - 3 * top), jnp.int32)
    side = jnp.concatenate([ids[...], numer[...] >> 5, numer[...] & 31, pad], axis=1)
    out_ref[:, depth:] = side.astype(jnp.float32).astype(jnp.bfloat16)


def join(mine_ref, theirs_ref, *refs):
    out_ref = refs[-1]
    count = mine_ref.shape[0]
    out_ref[:count, :] = mine_ref[...]
    out_ref[count:, :] = theirs_ref[...]


def bring(at, gate_ref, up_ref, down_ref, after_ref, gates, ups, downs, end_ref, sem):
    pieces = sem.shape[1]
    size = gates.shape[0] // pieces
    started = []
    for p in range(pieces):
        for i, (ref, held) in enumerate([(gate_ref, gates), (up_ref, ups), (down_ref, downs)]):
            started.append(
                pltpu.make_async_copy(
                    ref.at[pl.ds(at + p * size, size)], held.at[pl.ds(p * size, size)], sem.at[i, p]
                )
            )
    for copy in started:
        copy.start()
    end_ref[...] = jnp.zeros_like(end_ref)
    for copy in started:
        copy.wait()


def dense_weights(side, top):
    ids = side[:, :top]
    numer = side[:, top:2 * top] * 32.0 + side[:, 2 * top:3 * top]
    weight = numer / jnp.sum(numer, axis=-1, keepdims=True)
    lane = lax.broadcasted_iota(jnp.int32, (side.shape[0], SIDE), 1)
    expert = jnp.where(lane < EXPERTS, lane, lane - EXPERTS).astype(jnp.float32)
    full = jnp.zeros((side.shape[0], SIDE), jnp.float32)
    for k in range(top):
        full = full + jnp.where(expert == ids[:, k:k + 1], weight[:, k:k + 1], 0.0)
    high = full.astype(jnp.bfloat16).astype(jnp.float32)
    return jnp.where(lane < EXPERTS, high, full - high).astype(jnp.bfloat16)


def layer(top, ff_dev, row_block, step_units, parts, mine_ref, theirs_ref, *refs):
    held, refs = refs[:3 * parts], refs[3 * parts:]
    (gate_ref, up_ref, down_ref, keep_ref, send_ref,
     rows_ref, total, gates, ups, downs, weights, hidden, sem) = refs
    units, depth = down_ref.shape
    steps = units // step_units
    count = rows_ref.shape[0]
    half = count // 2
    early = sum(held[3 * p].shape[0] for p in range(parts)) // step_units

    def copies(step, slot):
        span = pl.ds(pl.multiple_of(step * step_units, step_units), step_units)
        return [
            pltpu.make_async_copy(src.at[span], dst.at[slot], sem.at[i, slot])
            for i, (src, dst) in enumerate(
                [(gate_ref, gates), (up_ref, ups), (down_ref, downs)]
            )
        ]

    for step in range(early, min(early + SLOTS - 1, steps)):
        for copy in copies(step, step - early):
            copy.start()

    first = lax.axis_index("wide") * (units // ff_dev)

    def each_block(body):
        if count == row_block:
            body(pl.ds(0, row_block))
        else:
            @pl.loop(0, count // row_block)
            def _(b):
                body(pl.ds(pl.multiple_of(b * row_block, row_block), row_block))

    rows_ref[:half, :] = mine_ref[...]
    rows_ref[half:, :] = theirs_ref[...]

    def prepare(block):
        side = rows_ref[block, depth:depth + SIDE].astype(jnp.float32)
        weights[block, :] = dense_weights(side, top)
        total[block, :] = jnp.zeros((row_block, depth), jnp.float32)

    each_block(prepare)

    def work(step, gate, up, down, ready=None):
        expert = lax.broadcasted_iota(jnp.int32, (step_units, SIDE), 1)
        place = jnp.where(expert < EXPERTS, expert, expert - EXPERTS) - first
        unit = step * step_units + lax.broadcasted_iota(jnp.int32, (step_units, SIDE), 0)
        low = place * ff_dev
        pick = (unit >= low) & (unit < low + ff_dev) & (expert < 2 * EXPERTS)
        pick = jnp.where(pick, 1.0, 0.0).astype(jnp.bfloat16)
        if ready is not None:
            ready[0].wait()
            ready[1].wait()

        def first_half(block):
            x = rows_ref[block, :depth]
            g = lax.dot_general(gate[...], x, LAST, preferred_element_type=jnp.float32)
            u = lax.dot_general(up[...], x, LAST, preferred_element_type=jnp.float32)
            scale = lax.dot_general(
                pick, weights[block, :], LAST, preferred_element_type=jnp.float32
            )
            h = g / (1.0 + jnp.exp(-g)) * u * scale
            hidden[block, :] = jnp.transpose(h).astype(jnp.bfloat16)

        each_block(first_half)
        if ready is not None:
            ready[2].wait()

        def second_half(block):
            total[block, :] += jnp.dot(
                hidden[block, :], down[...], preferred_element_type=jnp.float32
            )

        each_block(second_half)

    done = 0
    for p in range(parts):
        inside = held[3 * p].shape[0] // step_units

        @pl.loop(0, inside)
        def _(s):
            span = pl.ds(pl.multiple_of(s * step_units, step_units), step_units)
            work(done + s, *[ref.at[span] for ref in held[3 * p:3 * p + 3]])

        done += inside

    @pl.loop(early, steps)
    def _(step):
        slot = lax.rem(step - early, SLOTS)

        @pl.when(step + SLOTS - 1 < steps)
        def _():
            for copy in copies(step + SLOTS - 1, lax.rem(step - early + SLOTS - 1, SLOTS)):
                copy.start()

        work(step, gates.at[slot], ups.at[slot], downs.at[slot], copies(step, slot))

    keep_ref[...] = total[:half, :]
    send_ref[...] = total[half:, :].astype(jnp.bfloat16)


def build(axes):
    def local(tokens, expert_ids, gate_numer, w_gate, w_up, w_down):
        local_count, ff_dev, depth = w_gate.shape
        units = local_count * ff_dev
        top = expert_ids.shape[1]
        step_units = next(n for n in range(256, 0, -16) if units % n == 0)
        weights = [w.reshape(units, depth) for w in (w_gate, w_up, w_down)]
        weights = [pltpu.with_memory_space_constraint(w, pltpu.HBM) for w in weights]
        small = pltpu.CompilerParams(vmem_limit_bytes=2 << 20)
        own = (tokens, expert_ids, gate_numer)
        own = [pltpu.with_memory_space_constraint(a, pltpu.HBM) for a in own]
        rows = pl.pallas_call(
            with_routing,
            out_shape=jax.ShapeDtypeStruct((tokens.shape[0], depth + SIDE), jnp.bfloat16),
            in_specs=[HBM] * 3,
            out_specs=VMEM,
            scratch_shapes=[
                pltpu.VMEM(expert_ids.shape, jnp.int32),
                pltpu.VMEM(gate_numer.shape, jnp.int32),
                pltpu.SemaphoreType.DMA((3,)),
            ],
            compiler_params=small,
            name="with_routing",
        )(*own)
        hops = []
        for axis, size in axes:
            by = size // 2
            while by:
                hops.append((axis, size, by))
                by //= 2
        held = []
        at = 0
        for number, hop in enumerate(hops):
            theirs = swap(rows, *hop)
            steps = EARLY[number] if number < len(EARLY) and units >= 8 * step_units else 0
            ends = []
            if steps:
                span = steps * step_units
                *brought, end = pl.pallas_call(
                    functools.partial(bring, at),
                    out_shape=[pltpu.VMEM((span, depth), jnp.bfloat16)] * 3
                    + [jax.ShapeDtypeStruct((8, 128), jnp.float32)],
                    in_specs=[HBM] * 3 + [pl.BlockSpec(memory_space=pl.ANY)],
                    out_specs=[VMEM] * 4,
                    scratch_shapes=[pltpu.SemaphoreType.DMA((3, 2 * steps))],
                    compiler_params=small,
                    cost_estimate=pl.CostEstimate(
                        flops=0, bytes_accessed=6 * span * depth, transcendentals=0
                    ),
                    name="bring_weights",
                )(*weights, rows)
                held += brought
                at += span
                ends = [end]
            if hop is hops[-1]:
                break
            count = rows.shape[0]
            if count <= 64:
                rows = pl.pallas_call(
                    join,
                    out_shape=jax.ShapeDtypeStruct((2 * count, depth + SIDE), jnp.bfloat16),
                    in_specs=[VMEM] * 2 + [pl.BlockSpec(memory_space=pl.ANY)] * len(ends),
                    out_specs=VMEM,
                    compiler_params=small,
                    name="join",
                )(rows, theirs, *ends)
            else:
                rows = jnp.concatenate([rows, theirs], axis=0)
        half = rows.shape[0]
        count = 2 * half
        keep, send = pl.pallas_call(
            functools.partial(layer, top, ff_dev, min(count, 64), step_units, len(held) // 3),
            out_shape=[
                jax.ShapeDtypeStruct((half, depth), jnp.float32),
                jax.ShapeDtypeStruct((half, depth), jnp.bfloat16),
            ],
            in_specs=[VMEM] * (2 + len(held)) + [HBM] * 3,
            out_specs=[VMEM] * 2,
            scratch_shapes=[
                pltpu.VMEM((count, depth + SIDE), jnp.bfloat16),
                pltpu.VMEM((count, depth), jnp.float32),
            ]
            + [pltpu.VMEM((SLOTS, step_units, depth), jnp.bfloat16)] * 3
            + [
                pltpu.VMEM((count, SIDE), jnp.bfloat16),
                pltpu.VMEM((count, step_units), jnp.bfloat16),
                pltpu.SemaphoreType.DMA((3, SLOTS)),
            ],
            compiler_params=pltpu.CompilerParams(
                vmem_limit_bytes=GRANT if count == 64 else 60 << 20
            ),
            cost_estimate=pl.CostEstimate(
                flops=6 * count * units * depth,
                bytes_accessed=6 * (units - at) * depth,
                transcendentals=count * units,
            ),
            name="expert_layer",
        )(rows, theirs, *held, *weights)
        total = keep + swap(send, *hops[-1]).astype(jnp.float32)
        for hop in reversed(hops[:-1]):
            half = total.shape[0] // 2
            theirs = swap(total[half:].astype(jnp.bfloat16), *hop)
            total = total[:half] + theirs.astype(jnp.float32)
        return total.astype(jnp.bfloat16)

    return local


def solution(mesh):
    rows = P(("grp", "wide", "sec", "sub"), None)
    weights = P("wide", ("sec", "sub"), None)
    axes = [(name, mesh.shape[name]) for name in ("wide", "sec", "sub")]
    return jax.shard_map(
        build(axes),
        mesh=mesh,
        in_specs=(rows, rows, rows, weights, weights, weights),
        out_specs=rows,
        check_vma=False,
    )
```

```python
import functools

import jax
import jax.numpy as jnp
from jax import lax
from jax.experimental import pallas as pl
from jax.experimental.pallas import tpu as pltpu
from jax.sharding import PartitionSpec as P

EXPERTS = 32
SIDE = 128
SLOTS = 3
EARLY = (0, 1, 1)
GRANT = 8 << 20

VMEM = pl.BlockSpec(memory_space=pltpu.VMEM)
HBM = pl.BlockSpec(memory_space=pltpu.HBM)
LAST = (((1,), (1,)), ((), ()))


def swap(x, axis, size, by):
    return lax.ppermute(x, axis, [(i, i ^ by) for i in range(size)])


def with_routing(tokens_ref, ids_ref, numer_ref, out_ref, ids, numer, sem):
    rows, depth = tokens_ref.shape
    top = ids_ref.shape[1]
    pairs = [(tokens_ref, out_ref.at[:, pl.ds(0, depth)]), (ids_ref, ids), (numer_ref, numer)]
    started = [pltpu.make_async_copy(a, b, sem.at[i]) for i, (a, b) in enumerate(pairs)]
    for copy in started:
        copy.start()
    for copy in started:
        copy.wait()
    pad = jnp.zeros((rows, SIDE - 3 * top), jnp.int32)
    side = jnp.concatenate([ids[...], numer[...] >> 5, numer[...] & 31, pad], axis=1)
    out_ref[:, depth:] = side.astype(jnp.float32).astype(jnp.bfloat16)


def join(mine_ref, theirs_ref, *refs):
    out_ref = refs[-1]
    count = mine_ref.shape[0]
    out_ref[:count, :] = mine_ref[...]
    out_ref[count:, :] = theirs_ref[...]


def bring(first, count, gate_ref, up_ref, down_ref, after_ref, *refs):
    gates, ups, downs, end_ref, sem = refs[-5:]
    size = gates.shape[1]
    started = []
    for step in range(first, first + count):
        for i, (ref, ring) in enumerate([(gate_ref, gates), (up_ref, ups), (down_ref, downs)]):
            for part in range(2):
                half = size // 2
                started.append(
                    pltpu.make_async_copy(
                        ref.at[pl.ds(step * size + part * half, half)],
                        ring.at[step, pl.ds(part * half, half)],
                        sem.at[i, step - first, part],
                    )
                )
    for copy in started:
        copy.start()
    end_ref[...] = jnp.zeros_like(end_ref)
    for copy in started:
        copy.wait()


def dense_weights(side, top):
    ids = side[:, :top]
    numer = side[:, top:2 * top] * 32.0 + side[:, 2 * top:3 * top]
    weight = numer / jnp.sum(numer, axis=-1, keepdims=True)
    lane = lax.broadcasted_iota(jnp.int32, (side.shape[0], SIDE), 1)
    expert = jnp.where(lane < EXPERTS, lane, lane - EXPERTS).astype(jnp.float32)
    full = jnp.zeros((side.shape[0], SIDE), jnp.float32)
    for k in range(top):
        full = full + jnp.where(expert == ids[:, k:k + 1], weight[:, k:k + 1], 0.0)
    high = full.astype(jnp.bfloat16).astype(jnp.float32)
    return jnp.where(lane < EXPERTS, high, full - high).astype(jnp.bfloat16)


def layer(top, ff_dev, row_block, step_units, early, mine_ref, theirs_ref, gate_ref, up_ref,
          down_ref, *refs):
    if early:
        refs = refs[3:]
    keep_ref, send_ref, gates, ups, downs, rows_ref, total, weights, hidden, sem = refs
    units, depth = down_ref.shape
    steps = units // step_units
    count = rows_ref.shape[0]
    half = count // 2
    slots = gates.shape[0]

    def copy_of(i, step):
        src, ring = [(gate_ref, gates), (up_ref, ups), (down_ref, downs)][i]
        slot = lax.rem(step, ring.shape[0])
        span = pl.ds(pl.multiple_of(step * step_units, step_units), step_units)
        return pltpu.make_async_copy(src.at[span], ring.at[slot], sem.at[i, slot])

    def start(step):
        for i in range(3):
            copy_of(i, step).start()

    def wait(i, step):
        if isinstance(step, int):
            if step >= early:
                copy_of(i, jnp.int32(step)).wait()
        else:
            @pl.when(step >= early)
            def _():
                copy_of(i, step).wait()

    for step in range(early, min(slots, steps)):
        start(jnp.int32(step))

    first = lax.axis_index("wide") * (units // ff_dev)

    def each_block(body):
        if count == row_block:
            body(pl.ds(0, row_block))
        else:
            @pl.loop(0, count // row_block)
            def _(b):
                body(pl.ds(pl.multiple_of(b * row_block, row_block), row_block))

    rows_ref[:half, :] = mine_ref[...]
    rows_ref[half:, :] = theirs_ref[...]

    def prepare(block):
        side = rows_ref[block, depth:depth + SIDE].astype(jnp.float32)
        weights[block, :] = dense_weights(side, top)
        total[block, :] = jnp.zeros((row_block, depth), jnp.float32)

    each_block(prepare)

    def products(step, block):
        x = rows_ref[block, :depth]
        gate, up = [ring.at[lax.rem(step, ring.shape[0])] for ring in (gates, ups)]
        g = lax.dot_general(gate[...], x, LAST, preferred_element_type=jnp.float32)
        u = lax.dot_general(up[...], x, LAST, preferred_element_type=jnp.float32)
        return g, u

    def activate(step, block, g, u):
        expert = lax.broadcasted_iota(jnp.int32, (step_units, SIDE), 1)
        place = jnp.where(expert < EXPERTS, expert, expert - EXPERTS) - first
        unit = step * step_units + lax.broadcasted_iota(jnp.int32, (step_units, SIDE), 0)
        low = place * ff_dev
        pick = (unit >= low) & (unit < low + ff_dev) & (expert < 2 * EXPERTS)
        pick = jnp.where(pick, 1.0, 0.0).astype(jnp.bfloat16)
        scale = lax.dot_general(pick, weights[block, :], LAST, preferred_element_type=jnp.float32)
        h = g / (1.0 + jnp.exp(-g)) * u * scale
        hidden[lax.rem(step, 2), block, :] = jnp.transpose(h).astype(jnp.bfloat16)

    def down_product(step, block):
        down = downs.at[lax.rem(step, downs.shape[0])]
        total[block, :] += jnp.dot(
            hidden[lax.rem(step, 2), block, :], down[...], preferred_element_type=jnp.float32
        )

    wait(0, 0)
    wait(1, 0)
    each_block(lambda block: activate(0, block, *products(jnp.int32(0), block)))

    @pl.loop(1, steps)
    def _(step):
        @pl.when(step - 1 + slots < steps)
        def _():
            start(step - 1 + slots)

        wait(0, step)
        wait(1, step)
        wait(2, step - 1)

        def both(block):
            g, u = products(step, block)
            down_product(step - 1, block)
            activate(step, block, g, u)

        each_block(both)

    wait(2, steps - 1)
    each_block(lambda block: down_product(jnp.int32(steps - 1), block))
    keep_ref[...] = total[:half, :]
    send_ref[...] = total[half:, :].astype(jnp.bfloat16)


def build(axes):
    def local(tokens, expert_ids, gate_numer, w_gate, w_up, w_down):
        local_count, ff_dev, depth = w_gate.shape
        units = local_count * ff_dev
        top = expert_ids.shape[1]
        step_units = next(n for n in range(256, 0, -16) if units % n == 0)
        weights = [w.reshape(units, depth) for w in (w_gate, w_up, w_down)]
        weights = [pltpu.with_memory_space_constraint(w, pltpu.HBM) for w in weights]
        small = pltpu.CompilerParams(vmem_limit_bytes=2 << 20)
        own = (tokens, expert_ids, gate_numer)
        own = [pltpu.with_memory_space_constraint(a, pltpu.HBM) for a in own]
        rows = pl.pallas_call(
            with_routing,
            out_shape=jax.ShapeDtypeStruct((tokens.shape[0], depth + SIDE), jnp.bfloat16),
            in_specs=[HBM] * 3,
            out_specs=VMEM,
            scratch_shapes=[
                pltpu.VMEM(expert_ids.shape, jnp.int32),
                pltpu.VMEM(gate_numer.shape, jnp.int32),
                pltpu.SemaphoreType.DMA((3,)),
            ],
            compiler_params=small,
            name="with_routing",
        )(*own)
        hops = []
        for axis, size in axes:
            by = size // 2
            while by:
                hops.append((axis, size, by))
                by //= 2
        slots = min(SLOTS, units // step_units)
        ring_shapes = [
            pltpu.VMEM((n, step_units, depth), jnp.bfloat16) for n in (slots, slots, slots + 1)
        ]
        ring = []
        early = 0
        for number, hop in enumerate(hops):
            theirs = swap(rows, *hop)
            steps = EARLY[number] if number < len(EARLY) and units >= 8 * step_units else 0
            ends = []
            if steps:
                *ring, end = pl.pallas_call(
                    functools.partial(bring, early, steps),
                    out_shape=ring_shapes + [jax.ShapeDtypeStruct((8, 128), jnp.float32)],
                    in_specs=[HBM] * 3 + [pl.BlockSpec(memory_space=pl.ANY)] + [VMEM] * len(ring),
                    out_specs=[VMEM] * 4,
                    scratch_shapes=[pltpu.SemaphoreType.DMA((3, steps, 2))],
                    input_output_aliases={4 + i: i for i in range(len(ring))},
                    compiler_params=small,
                    cost_estimate=pl.CostEstimate(
                        flops=0,
                        bytes_accessed=6 * steps * step_units * depth,
                        transcendentals=0,
                    ),
                    name="bring_weights",
                )(*weights, rows, *ring)
                early += steps
                ends = [end]
            if hop is hops[-1]:
                break
            count = rows.shape[0]
            if count <= 64:
                rows = pl.pallas_call(
                    join,
                    out_shape=jax.ShapeDtypeStruct((2 * count, depth + SIDE), jnp.bfloat16),
                    in_specs=[VMEM] * 2 + [pl.BlockSpec(memory_space=pl.ANY)] * len(ends),
                    out_specs=VMEM,
                    compiler_params=small,
                    name="join",
                )(rows, theirs, *ends)
            else:
                rows = jnp.concatenate([rows, theirs], axis=0)
        half = rows.shape[0]
        count = 2 * half
        row_block = min(count, 64)
        keep, send, *_ = pl.pallas_call(
            functools.partial(layer, top, ff_dev, row_block, step_units, early),
            out_shape=[
                jax.ShapeDtypeStruct((half, depth), jnp.float32),
                jax.ShapeDtypeStruct((half, depth), jnp.bfloat16),
            ]
            + (ring_shapes if early else []),
            in_specs=[VMEM] * 2 + [HBM] * 3 + [VMEM] * len(ring),
            out_specs=[VMEM] * (5 if early else 2),
            scratch_shapes=([] if early else ring_shapes)
            + [
                pltpu.VMEM((count, depth + SIDE), jnp.bfloat16),
                pltpu.VMEM((count, depth), jnp.float32),
                pltpu.VMEM((count, SIDE), jnp.bfloat16),
                pltpu.VMEM((2, count, step_units), jnp.bfloat16),
                pltpu.SemaphoreType.DMA((3, slots + 1)),
            ],
            input_output_aliases={5 + i: 2 + i for i in range(len(ring))},
            compiler_params=pltpu.CompilerParams(
                vmem_limit_bytes=GRANT if early else 60 << 20
            ),
            cost_estimate=pl.CostEstimate(
                flops=6 * count * units * depth,
                bytes_accessed=6 * (units - early * step_units) * depth,
                transcendentals=count * units,
            ),
            name="expert_layer",
        )(rows, theirs, *weights, *ring)
        total = keep + swap(send, *hops[-1]).astype(jnp.float32)
        for hop in reversed(hops[:-1]):
            half = total.shape[0] // 2
            theirs = swap(total[half:].astype(jnp.bfloat16), *hop)
            total = total[:half] + theirs.astype(jnp.float32)
        return total.astype(jnp.bfloat16)

    return local


def solution(mesh):
    rows = P(("grp", "wide", "sec", "sub"), None)
    weights = P("wide", ("sec", "sub"), None)
    axes = [(name, mesh.shape[name]) for name in ("wide", "sec", "sub")]
    return jax.shard_map(
        build(axes),
        mesh=mesh,
        in_specs=(rows, rows, rows, weights, weights, weights),
        out_specs=rows,
        check_vma=False,
    )
```

```python
import functools

import jax
import jax.numpy as jnp
from jax import lax
from jax.experimental import pallas as pl
from jax.experimental.pallas import tpu as pltpu
from jax.sharding import PartitionSpec as P

EXPERTS = 32
SIDE = 128
SLOTS = 4
EARLY = (1, 1, 2)
GRANT = 8 << 20

VMEM = pl.BlockSpec(memory_space=pltpu.VMEM)
HBM = pl.BlockSpec(memory_space=pltpu.HBM)
LAST = (((1,), (1,)), ((), ()))


def swap(x, axis, size, by):
    return lax.ppermute(x, axis, [(i, i ^ by) for i in range(size)])


def with_routing(tokens_ref, ids_ref, numer_ref, out_ref, ids, numer, sem):
    rows, depth = tokens_ref.shape
    top = ids_ref.shape[1]
    pairs = [(tokens_ref, out_ref.at[:, pl.ds(0, depth)]), (ids_ref, ids), (numer_ref, numer)]
    started = [pltpu.make_async_copy(a, b, sem.at[i]) for i, (a, b) in enumerate(pairs)]
    for copy in started:
        copy.start()
    for copy in started:
        copy.wait()
    pad = jnp.zeros((rows, SIDE - 3 * top), jnp.int32)
    side = jnp.concatenate([ids[...], numer[...] >> 5, numer[...] & 31, pad], axis=1)
    out_ref[:, depth:] = side.astype(jnp.float32).astype(jnp.bfloat16)


def join(mine_ref, theirs_ref, *refs):
    out_ref = refs[-1]
    count = mine_ref.shape[0]
    out_ref[:count, :] = mine_ref[...]
    out_ref[count:, :] = theirs_ref[...]


def bring(first, count, gate_ref, up_ref, down_ref, after_ref, *refs):
    gates, ups, downs, end_ref, sem = refs[-5:]
    size = gates.shape[1]
    started = []
    for step in range(first, first + count):
        for i, (ref, ring) in enumerate([(gate_ref, gates), (up_ref, ups), (down_ref, downs)]):
            for part in range(2):
                half = size // 2
                started.append(
                    pltpu.make_async_copy(
                        ref.at[pl.ds(step * size + part * half, half)],
                        ring.at[step, pl.ds(part * half, half)],
                        sem.at[i, step - first, part],
                    )
                )
    for copy in started:
        copy.start()
    end_ref[...] = jnp.zeros_like(end_ref)
    for copy in started:
        copy.wait()


def dense_weights(side, top):
    ids = side[:, :top]
    numer = side[:, top:2 * top] * 32.0 + side[:, 2 * top:3 * top]
    weight = numer / jnp.sum(numer, axis=-1, keepdims=True)
    lane = lax.broadcasted_iota(jnp.int32, (side.shape[0], SIDE), 1)
    expert = jnp.where(lane < EXPERTS, lane, lane - EXPERTS).astype(jnp.float32)
    full = jnp.zeros((side.shape[0], SIDE), jnp.float32)
    for k in range(top):
        full = full + jnp.where(expert == ids[:, k:k + 1], weight[:, k:k + 1], 0.0)
    high = full.astype(jnp.bfloat16).astype(jnp.float32)
    return jnp.where(lane < EXPERTS, high, full - high).astype(jnp.bfloat16)


def layer(top, ff_dev, row_block, step_units, early, mine_ref, theirs_ref, gate_ref, up_ref,
          down_ref, *refs):
    if early:
        refs = refs[3:]
    keep_ref, send_ref, gates, ups, downs, rows_ref, total, weights, hidden, sem = refs
    units, depth = down_ref.shape
    steps = units // step_units
    count = rows_ref.shape[0]
    half = count // 2
    slots = gates.shape[0]

    def copy_of(i, step):
        src, ring = [(gate_ref, gates), (up_ref, ups), (down_ref, downs)][i]
        slot = lax.rem(step, ring.shape[0])
        span = pl.ds(pl.multiple_of(step * step_units, step_units), step_units)
        return pltpu.make_async_copy(src.at[span], ring.at[slot], sem.at[i, slot])

    def start(step):
        for i in range(3):
            copy_of(i, step).start()

    def wait(i, step):
        if isinstance(step, int):
            if step >= early:
                copy_of(i, jnp.int32(step)).wait()
        else:
            @pl.when(step >= early)
            def _():
                copy_of(i, step).wait()

    for step in range(early, min(slots, steps)):
        start(jnp.int32(step))

    first = lax.axis_index("wide") * (units // ff_dev)

    def each_block(body):
        if count == row_block:
            body(pl.ds(0, row_block))
        else:
            @pl.loop(0, count // row_block)
            def _(b):
                body(pl.ds(pl.multiple_of(b * row_block, row_block), row_block))

    rows_ref[:half, :] = mine_ref[...]
    rows_ref[half:, :] = theirs_ref[...]

    def prepare(block):
        side = rows_ref[block, depth:depth + SIDE].astype(jnp.float32)
        weights[block, :] = dense_weights(side, top)
        total[block, :] = jnp.zeros((row_block, depth), jnp.float32)

    each_block(prepare)

    def products(step, block):
        x = rows_ref[block, :depth]
        gate, up = [ring.at[lax.rem(step, ring.shape[0])] for ring in (gates, ups)]
        g = lax.dot_general(gate[...], x, LAST, preferred_element_type=jnp.float32)
        u = lax.dot_general(up[...], x, LAST, preferred_element_type=jnp.float32)
        return g, u

    def activate(step, block, g, u):
        expert = lax.broadcasted_iota(jnp.int32, (step_units, SIDE), 1)
        place = jnp.where(expert < EXPERTS, expert, expert - EXPERTS) - first
        unit = step * step_units + lax.broadcasted_iota(jnp.int32, (step_units, SIDE), 0)
        low = place * ff_dev
        pick = (unit >= low) & (unit < low + ff_dev) & (expert < 2 * EXPERTS)
        pick = jnp.where(pick, 1.0, 0.0).astype(jnp.bfloat16)
        scale = lax.dot_general(pick, weights[block, :], LAST, preferred_element_type=jnp.float32)
        h = g / (1.0 + jnp.exp(-g)) * u * scale
        hidden[lax.rem(step, 2), block, :] = jnp.transpose(h).astype(jnp.bfloat16)

    def down_product(step, block):
        down = downs.at[lax.rem(step, downs.shape[0])]
        total[block, :] += jnp.dot(
            hidden[lax.rem(step, 2), block, :], down[...], preferred_element_type=jnp.float32
        )

    wait(0, 0)
    wait(1, 0)
    each_block(lambda block: activate(0, block, *products(jnp.int32(0), block)))

    @pl.loop(1, steps)
    def _(step):
        @pl.when(step - 1 + slots < steps)
        def _():
            start(step - 1 + slots)

        wait(0, step)
        wait(1, step)
        wait(2, step - 1)

        def both(block):
            g, u = products(step, block)
            down_product(step - 1, block)
            activate(step, block, g, u)

        each_block(both)

    wait(2, steps - 1)
    each_block(lambda block: down_product(jnp.int32(steps - 1), block))
    keep_ref[...] = total[:half, :]
    send_ref[...] = total[half:, :].astype(jnp.bfloat16)


def build(axes):
    def local(tokens, expert_ids, gate_numer, w_gate, w_up, w_down):
        local_count, ff_dev, depth = w_gate.shape
        units = local_count * ff_dev
        top = expert_ids.shape[1]
        step_units = next(n for n in range(256, 0, -16) if units % n == 0)
        weights = [w.reshape(units, depth) for w in (w_gate, w_up, w_down)]
        weights = [pltpu.with_memory_space_constraint(w, pltpu.HBM) for w in weights]
        small = pltpu.CompilerParams(vmem_limit_bytes=2 << 20)
        own = (tokens, expert_ids, gate_numer)
        own = [pltpu.with_memory_space_constraint(a, pltpu.HBM) for a in own]
        rows = pl.pallas_call(
            with_routing,
            out_shape=jax.ShapeDtypeStruct((tokens.shape[0], depth + SIDE), jnp.bfloat16),
            in_specs=[HBM] * 3,
            out_specs=VMEM,
            scratch_shapes=[
                pltpu.VMEM(expert_ids.shape, jnp.int32),
                pltpu.VMEM(gate_numer.shape, jnp.int32),
                pltpu.SemaphoreType.DMA((3,)),
            ],
            compiler_params=small,
            name="with_routing",
        )(*own)
        hops = []
        for axis, size in axes:
            by = size // 2
            while by:
                hops.append((axis, size, by))
                by //= 2
        slots = min(SLOTS, units // step_units)
        ring_shapes = [
            pltpu.VMEM((n, step_units, depth), jnp.bfloat16) for n in (slots, slots, slots + 1)
        ]
        ring = []
        early = 0
        for number, hop in enumerate(hops):
            theirs = swap(rows, *hop)
            steps = EARLY[number] if number < len(EARLY) and units >= 8 * step_units else 0
            ends = []
            if steps:
                *ring, end = pl.pallas_call(
                    functools.partial(bring, early, steps),
                    out_shape=ring_shapes + [jax.ShapeDtypeStruct((8, 128), jnp.float32)],
                    in_specs=[HBM] * 3 + [pl.BlockSpec(memory_space=pl.ANY)] + [VMEM] * len(ring),
                    out_specs=[VMEM] * 4,
                    scratch_shapes=[pltpu.SemaphoreType.DMA((3, steps, 2))],
                    input_output_aliases={4 + i: i for i in range(len(ring))},
                    compiler_params=small,
                    cost_estimate=pl.CostEstimate(
                        flops=0,
                        bytes_accessed=6 * steps * step_units * depth,
                        transcendentals=0,
                    ),
                    name="bring_weights",
                )(*weights, rows, *ring)
                early += steps
                ends = [end]
            if hop is hops[-1]:
                break
            count = rows.shape[0]
            if count <= 64:
                rows = pl.pallas_call(
                    join,
                    out_shape=jax.ShapeDtypeStruct((2 * count, depth + SIDE), jnp.bfloat16),
                    in_specs=[VMEM] * 2 + [pl.BlockSpec(memory_space=pl.ANY)] * len(ends),
                    out_specs=VMEM,
                    compiler_params=small,
                    name="join",
                )(rows, theirs, *ends)
            else:
                rows = jnp.concatenate([rows, theirs], axis=0)
        half = rows.shape[0]
        count = 2 * half
        row_block = min(count, 64)
        keep, send, *_ = pl.pallas_call(
            functools.partial(layer, top, ff_dev, row_block, step_units, early),
            out_shape=[
                jax.ShapeDtypeStruct((half, depth), jnp.float32),
                jax.ShapeDtypeStruct((half, depth), jnp.bfloat16),
            ]
            + (ring_shapes if early else []),
            in_specs=[VMEM] * 2 + [HBM] * 3 + [VMEM] * len(ring),
            out_specs=[VMEM] * (5 if early else 2),
            scratch_shapes=([] if early else ring_shapes)
            + [
                pltpu.VMEM((count, depth + SIDE), jnp.bfloat16),
                pltpu.VMEM((count, depth), jnp.float32),
                pltpu.VMEM((count, SIDE), jnp.bfloat16),
                pltpu.VMEM((2, count, step_units), jnp.bfloat16),
                pltpu.SemaphoreType.DMA((3, slots + 1)),
            ],
            input_output_aliases={5 + i: 2 + i for i in range(len(ring))},
            compiler_params=pltpu.CompilerParams(
                vmem_limit_bytes=GRANT if early else 60 << 20
            ),
            cost_estimate=pl.CostEstimate(
                flops=6 * count * units * depth,
                bytes_accessed=6 * (units - early * step_units) * depth,
                transcendentals=count * units,
            ),
            name="expert_layer",
        )(rows, theirs, *weights, *ring)
        total = keep + swap(send, *hops[-1]).astype(jnp.float32)
        for hop in reversed(hops[:-1]):
            half = total.shape[0] // 2
            theirs = swap(total[half:].astype(jnp.bfloat16), *hop)
            total = total[:half] + theirs.astype(jnp.float32)
        return total.astype(jnp.bfloat16)

    return local


def solution(mesh):
    rows = P(("grp", "wide", "sec", "sub"), None)
    weights = P("wide", ("sec", "sub"), None)
    axes = [(name, mesh.shape[name]) for name in ("wide", "sec", "sub")]
    return jax.shard_map(
        build(axes),
        mesh=mesh,
        in_specs=(rows, rows, rows, weights, weights, weights),
        out_specs=rows,
        check_vma=False,
    )
```

```python
import functools

import jax
import jax.numpy as jnp
from jax import lax
from jax.experimental import pallas as pl
from jax.experimental.pallas import tpu as pltpu
from jax.sharding import PartitionSpec as P

EXPERTS = 32
SIDE = 128
SLOTS = 3
EARLY = (0, 1, 1)
GRANT = 8 << 20

VMEM = pl.BlockSpec(memory_space=pltpu.VMEM)
HBM = pl.BlockSpec(memory_space=pltpu.HBM)
LAST = (((1,), (1,)), ((), ()))


def swap(x, axis, size, by):
    if axis == "sub":
        return [lax.ppermute(x, axis, [(i, i ^ by) for i in range(size)])]
    return [
        lax.ppermute(x, axis, [(i, i ^ by) for i in range(size) if i & by == way])
        for way in (0, by)
    ]


def received(theirs):
    return sum(t.astype(jnp.float32) for t in theirs)


def with_routing(tokens_ref, ids_ref, numer_ref, out_ref, ids, numer, sem):
    rows, depth = tokens_ref.shape
    top = ids_ref.shape[1]
    pairs = [(tokens_ref, out_ref.at[:, pl.ds(0, depth)]), (ids_ref, ids), (numer_ref, numer)]
    started = [pltpu.make_async_copy(a, b, sem.at[i]) for i, (a, b) in enumerate(pairs)]
    for copy in started:
        copy.start()
    for copy in started:
        copy.wait()
    pad = jnp.zeros((rows, SIDE - 3 * top), jnp.int32)
    side = jnp.concatenate([ids[...], numer[...] >> 5, numer[...] & 31, pad], axis=1)
    out_ref[:, depth:] = side.astype(jnp.float32).astype(jnp.bfloat16)


def join(mine_ref, up_ref, down_ref, *refs):
    out_ref = refs[-1]
    count = mine_ref.shape[0]
    out_ref[:count, :] = mine_ref[...]
    out_ref[count:, :] = up_ref[...] + down_ref[...]


def bring(first, count, gate_ref, up_ref, down_ref, after_ref, *refs):
    gates, ups, downs, end_ref, sem = refs[-5:]
    size = gates.shape[1]
    started = []
    for step in range(first, first + count):
        for i, (ref, ring) in enumerate([(gate_ref, gates), (up_ref, ups), (down_ref, downs)]):
            for part in range(2):
                half = size // 2
                started.append(
                    pltpu.make_async_copy(
                        ref.at[pl.ds(step * size + part * half, half)],
                        ring.at[step, pl.ds(part * half, half)],
                        sem.at[i, step - first, part],
                    )
                )
    for copy in started:
        copy.start()
    end_ref[...] = jnp.zeros_like(end_ref)
    for copy in started:
        copy.wait()


def dense_weights(side, top):
    ids = side[:, :top]
    numer = side[:, top:2 * top] * 32.0 + side[:, 2 * top:3 * top]
    weight = numer / jnp.sum(numer, axis=-1, keepdims=True)
    lane = lax.broadcasted_iota(jnp.int32, (side.shape[0], SIDE), 1)
    expert = jnp.where(lane < EXPERTS, lane, lane - EXPERTS).astype(jnp.float32)
    full = jnp.zeros((side.shape[0], SIDE), jnp.float32)
    for k in range(top):
        full = full + jnp.where(expert == ids[:, k:k + 1], weight[:, k:k + 1], 0.0)
    high = full.astype(jnp.bfloat16).astype(jnp.float32)
    return jnp.where(lane < EXPERTS, high, full - high).astype(jnp.bfloat16)


def layer(top, ff_dev, row_block, step_units, early, mine_ref, theirs_ref, gate_ref, up_ref,
          down_ref, *refs):
    if early:
        refs = refs[3:]
    keep_ref, send_ref, gates, ups, downs, rows_ref, total, weights, hidden, sem = refs
    units, depth = down_ref.shape
    steps = units // step_units
    count = rows_ref.shape[0]
    half = count // 2
    slots = gates.shape[0]

    def copy_of(i, step):
        src, ring = [(gate_ref, gates), (up_ref, ups), (down_ref, downs)][i]
        slot = lax.rem(step, ring.shape[0])
        span = pl.ds(pl.multiple_of(step * step_units, step_units), step_units)
        return pltpu.make_async_copy(src.at[span], ring.at[slot], sem.at[i, slot])

    def start(step):
        for i in range(3):
            copy_of(i, step).start()

    def wait(i, step):
        if isinstance(step, int):
            if step >= early:
                copy_of(i, jnp.int32(step)).wait()
        else:
            @pl.when(step >= early)
            def _():
                copy_of(i, step).wait()

    for step in range(early, min(slots, steps)):
        start(jnp.int32(step))

    first = lax.axis_index("wide") * (units // ff_dev)

    def each_block(body):
        if count == row_block:
            body(pl.ds(0, row_block))
        else:
            @pl.loop(0, count // row_block)
            def _(b):
                body(pl.ds(pl.multiple_of(b * row_block, row_block), row_block))

    rows_ref[:half, :] = mine_ref[...]
    rows_ref[half:, :] = theirs_ref[...]

    def prepare(block):
        side = rows_ref[block, depth:depth + SIDE].astype(jnp.float32)
        weights[block, :] = dense_weights(side, top)
        total[block, :] = jnp.zeros((row_block, depth), jnp.float32)

    each_block(prepare)

    def products(step, block):
        x = rows_ref[block, :depth]
        gate, up = [ring.at[lax.rem(step, ring.shape[0])] for ring in (gates, ups)]
        g = lax.dot_general(gate[...], x, LAST, preferred_element_type=jnp.float32)
        u = lax.dot_general(up[...], x, LAST, preferred_element_type=jnp.float32)
        return g, u

    def activate(step, block, g, u):
        expert = lax.broadcasted_iota(jnp.int32, (step_units, SIDE), 1)
        place = jnp.where(expert < EXPERTS, expert, expert - EXPERTS) - first
        unit = step * step_units + lax.broadcasted_iota(jnp.int32, (step_units, SIDE), 0)
        low = place * ff_dev
        pick = (unit >= low) & (unit < low + ff_dev) & (expert < 2 * EXPERTS)
        pick = jnp.where(pick, 1.0, 0.0).astype(jnp.bfloat16)
        scale = lax.dot_general(pick, weights[block, :], LAST, preferred_element_type=jnp.float32)
        h = g / (1.0 + jnp.exp(-g)) * u * scale
        hidden[lax.rem(step, 2), block, :] = jnp.transpose(h).astype(jnp.bfloat16)

    def down_product(step, block):
        down = downs.at[lax.rem(step, downs.shape[0])]
        total[block, :] += jnp.dot(
            hidden[lax.rem(step, 2), block, :], down[...], preferred_element_type=jnp.float32
        )

    wait(0, 0)
    wait(1, 0)
    each_block(lambda block: activate(0, block, *products(jnp.int32(0), block)))

    @pl.loop(1, steps)
    def _(step):
        @pl.when(step - 1 + slots < steps)
        def _():
            start(step - 1 + slots)

        wait(0, step)
        wait(1, step)
        wait(2, step - 1)

        def both(block):
            g, u = products(step, block)
            down_product(step - 1, block)
            activate(step, block, g, u)

        each_block(both)

    wait(2, steps - 1)
    each_block(lambda block: down_product(jnp.int32(steps - 1), block))
    keep_ref[...] = total[:half, :]
    send_ref[...] = total[half:, :].astype(jnp.bfloat16)


def build(axes):
    def local(tokens, expert_ids, gate_numer, w_gate, w_up, w_down):
        local_count, ff_dev, depth = w_gate.shape
        units = local_count * ff_dev
        top = expert_ids.shape[1]
        step_units = next(n for n in range(256, 0, -16) if units % n == 0)
        weights = [w.reshape(units, depth) for w in (w_gate, w_up, w_down)]
        weights = [pltpu.with_memory_space_constraint(w, pltpu.HBM) for w in weights]
        small = pltpu.CompilerParams(vmem_limit_bytes=2 << 20)
        own = (tokens, expert_ids, gate_numer)
        own = [pltpu.with_memory_space_constraint(a, pltpu.HBM) for a in own]
        rows = pl.pallas_call(
            with_routing,
            out_shape=jax.ShapeDtypeStruct((tokens.shape[0], depth + SIDE), jnp.bfloat16),
            in_specs=[HBM] * 3,
            out_specs=VMEM,
            scratch_shapes=[
                pltpu.VMEM(expert_ids.shape, jnp.int32),
                pltpu.VMEM(gate_numer.shape, jnp.int32),
                pltpu.SemaphoreType.DMA((3,)),
            ],
            compiler_params=small,
            name="with_routing",
        )(*own)
        hops = []
        for axis, size in axes:
            by = size // 2
            while by:
                hops.append((axis, size, by))
                by //= 2
        slots = min(SLOTS, units // step_units)
        ring_shapes = [
            pltpu.VMEM((n, step_units, depth), jnp.bfloat16) for n in (slots, slots, slots + 1)
        ]
        ring = []
        early = 0
        for number, hop in enumerate(hops):
            theirs = swap(rows, *hop)
            steps = EARLY[number] if number < len(EARLY) and units >= 8 * step_units else 0
            ends = []
            if steps:
                *ring, end = pl.pallas_call(
                    functools.partial(bring, early, steps),
                    out_shape=ring_shapes + [jax.ShapeDtypeStruct((8, 128), jnp.float32)],
                    in_specs=[HBM] * 3 + [pl.BlockSpec(memory_space=pl.ANY)] + [VMEM] * len(ring),
                    out_specs=[VMEM] * 4,
                    scratch_shapes=[pltpu.SemaphoreType.DMA((3, steps, 2))],
                    input_output_aliases={4 + i: i for i in range(len(ring))},
                    compiler_params=small,
                    cost_estimate=pl.CostEstimate(
                        flops=0,
                        bytes_accessed=6 * steps * step_units * depth,
                        transcendentals=0,
                    ),
                    name="bring_weights",
                )(*weights, rows, *ring)
                early += steps
                ends = [end]
            if hop is hops[-1]:
                break
            count = rows.shape[0]
            if count <= 64:
                rows = pl.pallas_call(
                    join,
                    out_shape=jax.ShapeDtypeStruct((2 * count, depth + SIDE), jnp.bfloat16),
                    in_specs=[VMEM] * 3 + [pl.BlockSpec(memory_space=pl.ANY)] * len(ends),
                    out_specs=VMEM,
                    compiler_params=small,
                    name="join",
                )(rows, *theirs, *ends)
            else:
                rows = jnp.concatenate([rows, sum(theirs)], axis=0)
        half = rows.shape[0]
        count = 2 * half
        row_block = min(count, 64)
        keep, send, *_ = pl.pallas_call(
            functools.partial(layer, top, ff_dev, row_block, step_units, early),
            out_shape=[
                jax.ShapeDtypeStruct((half, depth), jnp.float32),
                jax.ShapeDtypeStruct((half, depth), jnp.bfloat16),
            ]
            + (ring_shapes if early else []),
            in_specs=[VMEM] * 2 + [HBM] * 3 + [VMEM] * len(ring),
            out_specs=[VMEM] * (5 if early else 2),
            scratch_shapes=([] if early else ring_shapes)
            + [
                pltpu.VMEM((count, depth + SIDE), jnp.bfloat16),
                pltpu.VMEM((count, depth), jnp.float32),
                pltpu.VMEM((count, SIDE), jnp.bfloat16),
                pltpu.VMEM((2, count, step_units), jnp.bfloat16),
                pltpu.SemaphoreType.DMA((3, slots + 1)),
            ],
            input_output_aliases={5 + i: 2 + i for i in range(len(ring))},
            compiler_params=pltpu.CompilerParams(
                vmem_limit_bytes=GRANT if early else 60 << 20
            ),
            cost_estimate=pl.CostEstimate(
                flops=6 * count * units * depth,
                bytes_accessed=6 * (units - early * step_units) * depth,
                transcendentals=count * units,
            ),
            name="expert_layer",
        )(rows, *theirs, *weights, *ring)
        total = keep + received(swap(send, *hops[-1]))
        for hop in reversed(hops[:-1]):
            half = total.shape[0] // 2
            theirs = swap(total[half:].astype(jnp.bfloat16), *hop)
            total = total[:half] + received(theirs)
        return total.astype(jnp.bfloat16)

    return local


def solution(mesh):
    rows = P(("grp", "wide", "sec", "sub"), None)
    weights = P("wide", ("sec", "sub"), None)
    axes = [(name, mesh.shape[name]) for name in ("wide", "sec", "sub")]
    return jax.shard_map(
        build(axes),
        mesh=mesh,
        in_specs=(rows, rows, rows, weights, weights, weights),
        out_specs=rows,
        check_vma=False,
    )
```

```python
import functools

import jax
import jax.numpy as jnp
from jax import lax
from jax.experimental import pallas as pl
from jax.experimental.pallas import tpu as pltpu
from jax.sharding import PartitionSpec as P

EXPERTS = 32
SIDE = 128
SLOTS = 3
EARLY = (0, 1, 1)
GRANT = 8 << 20

VMEM = pl.BlockSpec(memory_space=pltpu.VMEM)
HBM = pl.BlockSpec(memory_space=pltpu.HBM)
LAST = (((1,), (1,)), ((), ()))


def swap(x, axis, size, by):
    return lax.ppermute(x, axis, [(i, i ^ by) for i in range(size)])


def with_routing(tokens_ref, ids_ref, numer_ref, out_ref, ids, numer, sem):
    rows, depth = tokens_ref.shape
    top = ids_ref.shape[1]
    pairs = [(tokens_ref, out_ref.at[:, pl.ds(0, depth)]), (ids_ref, ids), (numer_ref, numer)]
    started = [pltpu.make_async_copy(a, b, sem.at[i]) for i, (a, b) in enumerate(pairs)]
    for copy in started:
        copy.start()
    for copy in started:
        copy.wait()
    pad = jnp.zeros((rows, SIDE - 3 * top), jnp.int32)
    side = jnp.concatenate([ids[...], numer[...] >> 5, numer[...] & 31, pad], axis=1)
    out_ref[:, depth:] = side.astype(jnp.float32).astype(jnp.bfloat16)


def join(mine_ref, theirs_ref, *refs):
    out_ref = refs[-1]
    count = mine_ref.shape[0]
    out_ref[:count, :] = mine_ref[...]
    out_ref[count:, :] = theirs_ref[...]


def bring(first, count, gate_ref, up_ref, down_ref, after_ref, *refs):
    gates, ups, downs, end_ref, sem = refs[-5:]
    size = gates.shape[1]
    started = []
    for step in range(first, first + count):
        for i, (ref, ring) in enumerate([(gate_ref, gates), (up_ref, ups), (down_ref, downs)]):
            for part in range(2):
                half = size // 2
                started.append(
                    pltpu.make_async_copy(
                        ref.at[pl.ds(step * size + part * half, half)],
                        ring.at[step, pl.ds(part * half, half)],
                        sem.at[i, step - first, part],
                    )
                )
    for copy in started:
        copy.start()
    end_ref[...] = jnp.zeros_like(end_ref)
    for copy in started:
        copy.wait()


def dense_weights(side, top):
    ids = side[:, :top]
    numer = side[:, top:2 * top] * 32.0 + side[:, 2 * top:3 * top]
    weight = numer / jnp.sum(numer, axis=-1, keepdims=True)
    lane = lax.broadcasted_iota(jnp.int32, (side.shape[0], SIDE), 1)
    expert = jnp.where(lane < EXPERTS, lane, lane - EXPERTS).astype(jnp.float32)
    full = jnp.zeros((side.shape[0], SIDE), jnp.float32)
    for k in range(top):
        full = full + jnp.where(expert == ids[:, k:k + 1], weight[:, k:k + 1], 0.0)
    high = full.astype(jnp.bfloat16).astype(jnp.float32)
    return jnp.where(lane < EXPERTS, high, full - high).astype(jnp.bfloat16)


def layer(top, ff_dev, row_block, step_units, early, places, mine_ref, theirs_ref, gate_ref, up_ref,
          down_ref, *refs):
    if early:
        refs = refs[3:]
    keep_ref, send_ref, gates, ups, downs, rows_ref, total, weights, hidden, sem = refs
    units, depth = down_ref.shape
    steps = units // step_units
    count = rows_ref.shape[0]
    half = count // 2
    slots = gates.shape[0]

    def copy_of(i, step):
        src, ring = [(gate_ref, gates), (up_ref, ups), (down_ref, downs)][i]
        slot = lax.rem(step, ring.shape[0])
        span = pl.ds(pl.multiple_of(step * step_units, step_units), step_units)
        return pltpu.make_async_copy(src.at[span], ring.at[slot], sem.at[i, slot])

    def start(step):
        for i in range(3):
            copy_of(i, step).start()

    def wait(i, step):
        if isinstance(step, int):
            if step >= early:
                copy_of(i, jnp.int32(step)).wait()
        else:
            @pl.when(step >= early)
            def _():
                copy_of(i, step).wait()

    for step in range(early, min(slots, steps)):
        start(jnp.int32(step))

    first = lax.axis_index("wide") * (units // ff_dev)

    def each_block(body):
        if count == row_block:
            body(pl.ds(0, row_block))
        else:
            @pl.loop(0, count // row_block)
            def _(b):
                body(pl.ds(pl.multiple_of(b * row_block, row_block), row_block))

    rows_ref[:half, :] = mine_ref[...]
    rows_ref[half:, :] = theirs_ref[...]

    def prepare(block):
        side = rows_ref[block, depth:depth + SIDE].astype(jnp.float32)
        weights[block, :] = dense_weights(side, top)
        total[block, :] = jnp.zeros((row_block, depth), jnp.float32)

    each_block(prepare)

    def products(step, block):
        x = rows_ref[block, :depth]
        gate, up = [ring.at[lax.rem(step, ring.shape[0])] for ring in (gates, ups)]
        g = lax.dot_general(gate[...], x, LAST, preferred_element_type=jnp.float32)
        u = lax.dot_general(up[...], x, LAST, preferred_element_type=jnp.float32)
        return g, u

    def activate(step, block, g, u):
        expert = lax.broadcasted_iota(jnp.int32, (step_units, SIDE), 1)
        place = jnp.where(expert < EXPERTS, expert, expert - EXPERTS) - first
        unit = step * step_units + lax.broadcasted_iota(jnp.int32, (step_units, SIDE), 0)
        low = place * ff_dev
        pick = (unit >= low) & (unit < low + ff_dev) & (expert < 2 * EXPERTS)
        pick = jnp.where(pick, 1.0, 0.0).astype(jnp.bfloat16)
        scale = lax.dot_general(pick, weights[block, :], LAST, preferred_element_type=jnp.float32)
        h = g / (1.0 + jnp.exp(-g)) * u * scale
        hidden[lax.rem(step, 2), block, :] = jnp.transpose(h).astype(jnp.bfloat16)

    def down_product(step, block):
        down = downs.at[lax.rem(step, downs.shape[0])]
        total[block, :] += jnp.dot(
            hidden[lax.rem(step, 2), block, :], down[...], preferred_element_type=jnp.float32
        )

    wait(0, 0)
    wait(1, 0)
    each_block(lambda block: activate(0, block, *products(jnp.int32(0), block)))

    @pl.loop(1, steps)
    def _(step):
        @pl.when(step - 1 + slots < steps)
        def _():
            start(step - 1 + slots)

        wait(0, step)
        wait(1, step)
        wait(2, step - 1)

        def both(block):
            g, u = products(step, block)
            down_product(step - 1, block)
            activate(step, block, g, u)

        each_block(both)

    wait(2, steps - 1)
    each_block(lambda block: down_product(jnp.int32(steps - 1), block))
    tok = half // len(places)
    me = [lax.axis_index(name) for name in ("wide", "sec")]
    sections = lax.axis_size("sec")
    for block, (wide, sec) in enumerate(places):
        place = (me[0] ^ wide) * sections + (me[1] ^ sec)
        low = block * tok
        keep_ref[place] = total[low:low + tok, :]
        send_ref[place] = total[half + low:half + low + tok, :].astype(jnp.bfloat16)


def build(axes):
    def local(tokens, expert_ids, gate_numer, w_gate, w_up, w_down):
        local_count, ff_dev, depth = w_gate.shape
        units = local_count * ff_dev
        top = expert_ids.shape[1]
        step_units = next(n for n in range(256, 0, -16) if units % n == 0)
        weights = [w.reshape(units, depth) for w in (w_gate, w_up, w_down)]
        weights = [pltpu.with_memory_space_constraint(w, pltpu.HBM) for w in weights]
        small = pltpu.CompilerParams(vmem_limit_bytes=2 << 20)
        own = (tokens, expert_ids, gate_numer)
        own = [pltpu.with_memory_space_constraint(a, pltpu.HBM) for a in own]
        rows = pl.pallas_call(
            with_routing,
            out_shape=jax.ShapeDtypeStruct((tokens.shape[0], depth + SIDE), jnp.bfloat16),
            in_specs=[HBM] * 3,
            out_specs=VMEM,
            scratch_shapes=[
                pltpu.VMEM(expert_ids.shape, jnp.int32),
                pltpu.VMEM(gate_numer.shape, jnp.int32),
                pltpu.SemaphoreType.DMA((3,)),
            ],
            compiler_params=small,
            name="with_routing",
        )(*own)
        hops = []
        for axis, size in axes:
            by = size // 2
            while by:
                hops.append((axis, size, by))
                by //= 2
        slots = min(SLOTS, units // step_units)
        ring_shapes = [
            pltpu.VMEM((n, step_units, depth), jnp.bfloat16) for n in (slots, slots, slots + 1)
        ]
        ring = []
        early = 0
        for number, hop in enumerate(hops):
            theirs = swap(rows, *hop)
            steps = EARLY[number] if number < len(EARLY) and units >= 8 * step_units else 0
            ends = []
            if steps:
                *ring, end = pl.pallas_call(
                    functools.partial(bring, early, steps),
                    out_shape=ring_shapes + [jax.ShapeDtypeStruct((8, 128), jnp.float32)],
                    in_specs=[HBM] * 3 + [pl.BlockSpec(memory_space=pl.ANY)] + [VMEM] * len(ring),
                    out_specs=[VMEM] * 4,
                    scratch_shapes=[pltpu.SemaphoreType.DMA((3, steps, 2))],
                    input_output_aliases={4 + i: i for i in range(len(ring))},
                    compiler_params=small,
                    cost_estimate=pl.CostEstimate(
                        flops=0,
                        bytes_accessed=6 * steps * step_units * depth,
                        transcendentals=0,
                    ),
                    name="bring_weights",
                )(*weights, rows, *ring)
                early += steps
                ends = [end]
            if hop is hops[-1]:
                break
            count = rows.shape[0]
            if count <= 64:
                rows = pl.pallas_call(
                    join,
                    out_shape=jax.ShapeDtypeStruct((2 * count, depth + SIDE), jnp.bfloat16),
                    in_specs=[VMEM] * 2 + [pl.BlockSpec(memory_space=pl.ANY)] * len(ends),
                    out_specs=VMEM,
                    compiler_params=small,
                    name="join",
                )(rows, theirs, *ends)
            else:
                rows = jnp.concatenate([rows, theirs], axis=0)
        half = rows.shape[0]
        count = 2 * half
        tok = tokens.shape[0]
        places = [(0, 0)]
        for axis, _, by in hops[:-1]:
            places += [(w ^ by, c) if axis == "wide" else (w, c ^ by) for w, c in places]
        blocks = (len(places), tok, depth)
        row_block = min(count, 64)
        keep, send, *_ = pl.pallas_call(
            functools.partial(layer, top, ff_dev, row_block, step_units, early, places),
            out_shape=[
                jax.ShapeDtypeStruct(blocks, jnp.float32),
                jax.ShapeDtypeStruct(blocks, jnp.bfloat16),
            ]
            + (ring_shapes if early else []),
            in_specs=[VMEM] * 2 + [HBM] * 3 + [VMEM] * len(ring),
            out_specs=[VMEM] * (5 if early else 2),
            scratch_shapes=([] if early else ring_shapes)
            + [
                pltpu.VMEM((count, depth + SIDE), jnp.bfloat16),
                pltpu.VMEM((count, depth), jnp.float32),
                pltpu.VMEM((count, SIDE), jnp.bfloat16),
                pltpu.VMEM((2, count, step_units), jnp.bfloat16),
                pltpu.SemaphoreType.DMA((3, slots + 1)),
            ],
            input_output_aliases={5 + i: 2 + i for i in range(len(ring))},
            compiler_params=pltpu.CompilerParams(
                vmem_limit_bytes=GRANT if early else 60 << 20
            ),
            cost_estimate=pl.CostEstimate(
                flops=6 * count * units * depth,
                bytes_accessed=6 * (units - early * step_units) * depth,
                transcendentals=count * units,
            ),
            name="expert_layer",
        )(rows, theirs, *weights, *ring)
        total = keep + swap(send, *hops[-1]).astype(jnp.float32)
        arrived = lax.all_to_all(
            total.astype(jnp.bfloat16), ("wide", "sec"), split_axis=0, concat_axis=0, tiled=True
        )
        return jnp.sum(arrived.astype(jnp.float32), axis=0).astype(jnp.bfloat16)

    return local


def solution(mesh):
    rows = P(("grp", "wide", "sec", "sub"), None)
    weights = P("wide", ("sec", "sub"), None)
    axes = [(name, mesh.shape[name]) for name in ("wide", "sec", "sub")]
    return jax.shard_map(
        build(axes),
        mesh=mesh,
        in_specs=(rows, rows, rows, weights, weights, weights),
        out_specs=rows,
        check_vma=False,
    )
```

```python
import functools

import jax
import jax.numpy as jnp
from jax import lax
from jax.experimental import pallas as pl
from jax.experimental.pallas import tpu as pltpu
from jax.sharding import PartitionSpec as P

EXPERTS = 32
SIDE = 128
SLOTS = 3
EARLY = (0, 1, 1)
GRANT = 8 << 20

VMEM = pl.BlockSpec(memory_space=pltpu.VMEM)
HBM = pl.BlockSpec(memory_space=pltpu.HBM)
LAST = (((1,), (1,)), ((), ()))


def swap(x, axis, size, by):
    return lax.ppermute(x, axis, [(i, i ^ by) for i in range(size)])


def with_routing(tokens_ref, ids_ref, numer_ref, out_ref, ids, numer, sem):
    rows, depth = tokens_ref.shape
    top = ids_ref.shape[1]
    pairs = [(tokens_ref, out_ref.at[:, pl.ds(0, depth)]), (ids_ref, ids), (numer_ref, numer)]
    started = [pltpu.make_async_copy(a, b, sem.at[i]) for i, (a, b) in enumerate(pairs)]
    for copy in started:
        copy.start()
    for copy in started:
        copy.wait()
    pad = jnp.zeros((rows, SIDE - 3 * top), jnp.int32)
    side = jnp.concatenate([ids[...], numer[...] >> 5, numer[...] & 31, pad], axis=1)
    out_ref[:, depth:] = side.astype(jnp.float32).astype(jnp.bfloat16)


def join(mine_ref, theirs_ref, *refs):
    out_ref = refs[-1]
    count = mine_ref.shape[0]
    out_ref[:count, :] = mine_ref[...]
    out_ref[count:, :] = theirs_ref[...]


def bring(first, count, gate_ref, up_ref, down_ref, after_ref, *refs):
    gates, ups, downs, end_ref, sem = refs[-5:]
    size = gates.shape[1]
    started = []
    for step in range(first, first + count):
        for i, (ref, ring) in enumerate([(gate_ref, gates), (up_ref, ups), (down_ref, downs)]):
            for part in range(2):
                half = size // 2
                started.append(
                    pltpu.make_async_copy(
                        ref.at[pl.ds(step * size + part * half, half)],
                        ring.at[step, pl.ds(part * half, half)],
                        sem.at[i, step - first, part],
                    )
                )
    for copy in started:
        copy.start()
    end_ref[...] = jnp.zeros_like(end_ref)
    for copy in started:
        copy.wait()


def dense_weights(side, top):
    ids = side[:, :top]
    numer = side[:, top:2 * top] * 32.0 + side[:, 2 * top:3 * top]
    weight = numer / jnp.sum(numer, axis=-1, keepdims=True)
    lane = lax.broadcasted_iota(jnp.int32, (side.shape[0], SIDE), 1)
    expert = jnp.where(lane < EXPERTS, lane, lane - EXPERTS).astype(jnp.float32)
    full = jnp.zeros((side.shape[0], SIDE), jnp.float32)
    for k in range(top):
        full = full + jnp.where(expert == ids[:, k:k + 1], weight[:, k:k + 1], 0.0)
    high = full.astype(jnp.bfloat16).astype(jnp.float32)
    return jnp.where(lane < EXPERTS, high, full - high).astype(jnp.bfloat16)


def layer(top, ff_dev, row_block, step_units, early, places, mine_ref, theirs_ref, gate_ref, up_ref,
          down_ref, *refs):
    if early:
        refs = refs[3:]
    keep_ref, send_ref, gates, ups, downs, rows_ref, total, weights, hidden, sem = refs
    units, depth = down_ref.shape
    steps = units // step_units
    count = rows_ref.shape[0]
    half = count // 2
    slots = gates.shape[0]

    def copy_of(i, step):
        src, ring = [(gate_ref, gates), (up_ref, ups), (down_ref, downs)][i]
        slot = lax.rem(step, ring.shape[0])
        span = pl.ds(pl.multiple_of(step * step_units, step_units), step_units)
        return pltpu.make_async_copy(src.at[span], ring.at[slot], sem.at[i, slot])

    def start(step):
        for i in range(3):
            copy_of(i, step).start()

    def wait(i, step):
        if isinstance(step, int):
            if step >= early:
                copy_of(i, jnp.int32(step)).wait()
        else:
            @pl.when(step >= early)
            def _():
                copy_of(i, step).wait()

    for step in range(early, min(slots, steps)):
        start(jnp.int32(step))

    first = lax.axis_index("wide") * (units // ff_dev)

    def each_block(body):
        if count == row_block:
            body(pl.ds(0, row_block))
        else:
            @pl.loop(0, count // row_block)
            def _(b):
                body(pl.ds(pl.multiple_of(b * row_block, row_block), row_block))

    rows_ref[:half, :] = mine_ref[...]
    rows_ref[half:, :] = theirs_ref[...]

    def prepare(block):
        side = rows_ref[block, depth:depth + SIDE].astype(jnp.float32)
        weights[block, :] = dense_weights(side, top)
        total[block, :] = jnp.zeros((row_block, depth), jnp.float32)

    each_block(prepare)

    def products(step, block):
        x = rows_ref[block, :depth]
        gate, up = [ring.at[lax.rem(step, ring.shape[0])] for ring in (gates, ups)]
        g = lax.dot_general(gate[...], x, LAST, preferred_element_type=jnp.float32)
        u = lax.dot_general(up[...], x, LAST, preferred_element_type=jnp.float32)
        return g, u

    def activate(step, block, g, u):
        expert = lax.broadcasted_iota(jnp.int32, (step_units, SIDE), 1)
        place = jnp.where(expert < EXPERTS, expert, expert - EXPERTS) - first
        unit = step * step_units + lax.broadcasted_iota(jnp.int32, (step_units, SIDE), 0)
        low = place * ff_dev
        pick = (unit >= low) & (unit < low + ff_dev) & (expert < 2 * EXPERTS)
        pick = jnp.where(pick, 1.0, 0.0).astype(jnp.bfloat16)
        scale = lax.dot_general(pick, weights[block, :], LAST, preferred_element_type=jnp.float32)
        h = g / (1.0 + jnp.exp(-g)) * u * scale
        hidden[lax.rem(step, 2), block, :] = jnp.transpose(h).astype(jnp.bfloat16)

    def down_product(step, block):
        down = downs.at[lax.rem(step, downs.shape[0])]
        total[block, :] += jnp.dot(
            hidden[lax.rem(step, 2), block, :], down[...], preferred_element_type=jnp.float32
        )

    wait(0, 0)
    wait(1, 0)
    each_block(lambda block: activate(0, block, *products(jnp.int32(0), block)))

    @pl.loop(1, steps)
    def _(step):
        @pl.when(step - 1 + slots < steps)
        def _():
            start(step - 1 + slots)

        wait(0, step)
        wait(1, step)
        wait(2, step - 1)

        def both(block):
            g, u = products(step, block)
            down_product(step - 1, block)
            activate(step, block, g, u)

        each_block(both)

    wait(2, steps - 1)
    each_block(lambda block: down_product(jnp.int32(steps - 1), block))
    tok = half // (keep_ref.shape[0] * len(places))
    me = lax.axis_index("wide")
    for block in range(half // tok):
        place = (block // len(places), me ^ places[block % len(places)])
        low = block * tok
        keep_ref[place] = total[low:low + tok, :]
        send_ref[place] = total[half + low:half + low + tok, :].astype(jnp.bfloat16)


def build(axes):
    def local(tokens, expert_ids, gate_numer, w_gate, w_up, w_down):
        local_count, ff_dev, depth = w_gate.shape
        units = local_count * ff_dev
        top = expert_ids.shape[1]
        step_units = next(n for n in range(256, 0, -16) if units % n == 0)
        weights = [w.reshape(units, depth) for w in (w_gate, w_up, w_down)]
        weights = [pltpu.with_memory_space_constraint(w, pltpu.HBM) for w in weights]
        small = pltpu.CompilerParams(vmem_limit_bytes=2 << 20)
        own = (tokens, expert_ids, gate_numer)
        own = [pltpu.with_memory_space_constraint(a, pltpu.HBM) for a in own]
        rows = pl.pallas_call(
            with_routing,
            out_shape=jax.ShapeDtypeStruct((tokens.shape[0], depth + SIDE), jnp.bfloat16),
            in_specs=[HBM] * 3,
            out_specs=VMEM,
            scratch_shapes=[
                pltpu.VMEM(expert_ids.shape, jnp.int32),
                pltpu.VMEM(gate_numer.shape, jnp.int32),
                pltpu.SemaphoreType.DMA((3,)),
            ],
            compiler_params=small,
            name="with_routing",
        )(*own)
        hops = []
        for axis, size in axes:
            by = size // 2
            while by:
                hops.append((axis, size, by))
                by //= 2
        slots = min(SLOTS, units // step_units)
        ring_shapes = [
            pltpu.VMEM((n, step_units, depth), jnp.bfloat16) for n in (slots, slots, slots + 1)
        ]
        ring = []
        early = 0
        for number, hop in enumerate(hops):
            theirs = swap(rows, *hop)
            steps = EARLY[number] if number < len(EARLY) and units >= 8 * step_units else 0
            ends = []
            if steps:
                *ring, end = pl.pallas_call(
                    functools.partial(bring, early, steps),
                    out_shape=ring_shapes + [jax.ShapeDtypeStruct((8, 128), jnp.float32)],
                    in_specs=[HBM] * 3 + [pl.BlockSpec(memory_space=pl.ANY)] + [VMEM] * len(ring),
                    out_specs=[VMEM] * 4,
                    scratch_shapes=[pltpu.SemaphoreType.DMA((3, steps, 2))],
                    input_output_aliases={4 + i: i for i in range(len(ring))},
                    compiler_params=small,
                    cost_estimate=pl.CostEstimate(
                        flops=0,
                        bytes_accessed=6 * steps * step_units * depth,
                        transcendentals=0,
                    ),
                    name="bring_weights",
                )(*weights, rows, *ring)
                early += steps
                ends = [end]
            if hop is hops[-1]:
                break
            count = rows.shape[0]
            if count <= 64:
                rows = pl.pallas_call(
                    join,
                    out_shape=jax.ShapeDtypeStruct((2 * count, depth + SIDE), jnp.bfloat16),
                    in_specs=[VMEM] * 2 + [pl.BlockSpec(memory_space=pl.ANY)] * len(ends),
                    out_specs=VMEM,
                    compiler_params=small,
                    name="join",
                )(rows, theirs, *ends)
            else:
                rows = jnp.concatenate([rows, theirs], axis=0)
        half = rows.shape[0]
        count = 2 * half
        tok = tokens.shape[0]
        places = [0]
        for axis, _, by in hops:
            if axis == "wide":
                places += [w ^ by for w in places]
        blocks = (half // (tok * len(places)), len(places), tok, depth)
        row_block = min(count, 64)
        keep, send, *_ = pl.pallas_call(
            functools.partial(layer, top, ff_dev, row_block, step_units, early, places),
            out_shape=[
                jax.ShapeDtypeStruct(blocks, jnp.float32),
                jax.ShapeDtypeStruct(blocks, jnp.bfloat16),
            ]
            + (ring_shapes if early else []),
            in_specs=[VMEM] * 2 + [HBM] * 3 + [VMEM] * len(ring),
            out_specs=[VMEM] * (5 if early else 2),
            scratch_shapes=([] if early else ring_shapes)
            + [
                pltpu.VMEM((count, depth + SIDE), jnp.bfloat16),
                pltpu.VMEM((count, depth), jnp.float32),
                pltpu.VMEM((count, SIDE), jnp.bfloat16),
                pltpu.VMEM((2, count, step_units), jnp.bfloat16),
                pltpu.SemaphoreType.DMA((3, slots + 1)),
            ],
            input_output_aliases={5 + i: 2 + i for i in range(len(ring))},
            compiler_params=pltpu.CompilerParams(
                vmem_limit_bytes=GRANT if early else 60 << 20
            ),
            cost_estimate=pl.CostEstimate(
                flops=6 * count * units * depth,
                bytes_accessed=6 * (units - early * step_units) * depth,
                transcendentals=count * units,
            ),
            name="expert_layer",
        )(rows, theirs, *weights, *ring)
        total = keep + swap(send, *hops[-1]).astype(jnp.float32)
        for hop in reversed(hops[:-1]):
            if hop[0] != "wide":
                left = total.shape[0] // 2
                theirs = swap(total[left:].astype(jnp.bfloat16), *hop)
                total = total[:left] + theirs.astype(jnp.float32)
        arrived = lax.all_to_all(
            total[0].astype(jnp.bfloat16), "wide", split_axis=0, concat_axis=0, tiled=True
        )
        return jnp.sum(arrived.astype(jnp.float32), axis=0).astype(jnp.bfloat16)

    return local


def solution(mesh):
    rows = P(("grp", "wide", "sec", "sub"), None)
    weights = P("wide", ("sec", "sub"), None)
    axes = [(name, mesh.shape[name]) for name in ("wide", "sec", "sub")]
    return jax.shard_map(
        build(axes),
        mesh=mesh,
        in_specs=(rows, rows, rows, weights, weights, weights),
        out_specs=rows,
        check_vma=False,
    )
```

```python
import functools

import jax
import jax.numpy as jnp
from jax import lax
from jax.experimental import pallas as pl
from jax.experimental.pallas import tpu as pltpu
from jax.sharding import PartitionSpec as P

EXPERTS = 32
SIDE = 128
SLOTS = 3
EARLY = (1, 1)
GRANT = 8 << 20

VMEM = pl.BlockSpec(memory_space=pltpu.VMEM)
HBM = pl.BlockSpec(memory_space=pltpu.HBM)
LAST = (((1,), (1,)), ((), ()))


def swap(x, axis, size, by):
    return lax.ppermute(x, axis, [(i, i ^ by) for i in range(size)])


def shift(x, axis, size, by):
    return lax.ppermute(x, axis, [(i, (i + by) % size) for i in range(size)])


def with_routing(tokens_ref, ids_ref, numer_ref, out_ref, ids, numer, sem):
    rows, depth = tokens_ref.shape
    top = ids_ref.shape[1]
    pairs = [(tokens_ref, out_ref.at[:, pl.ds(0, depth)]), (ids_ref, ids), (numer_ref, numer)]
    started = [pltpu.make_async_copy(a, b, sem.at[i]) for i, (a, b) in enumerate(pairs)]
    for copy in started:
        copy.start()
    for copy in started:
        copy.wait()
    pad = jnp.zeros((rows, SIDE - 3 * top), jnp.int32)
    side = jnp.concatenate([ids[...], numer[...] >> 5, numer[...] & 31, pad], axis=1)
    out_ref[:, depth:] = side.astype(jnp.float32).astype(jnp.bfloat16)


def join(parts, *refs):
    out_ref = refs[-1]
    count = refs[0].shape[0]
    for part in range(parts):
        out_ref[part * count:(part + 1) * count, :] = refs[part][...]


def bring(first, count, gate_ref, up_ref, down_ref, after_ref, *refs):
    gates, ups, downs, end_ref, sem = refs[-5:]
    size = gates.shape[1]
    started = []
    for step in range(first, first + count):
        for i, (ref, ring) in enumerate([(gate_ref, gates), (up_ref, ups), (down_ref, downs)]):
            for part in range(2):
                half = size // 2
                started.append(
                    pltpu.make_async_copy(
                        ref.at[pl.ds(step * size + part * half, half)],
                        ring.at[step, pl.ds(part * half, half)],
                        sem.at[i, step - first, part],
                    )
                )
    for copy in started:
        copy.start()
    end_ref[...] = jnp.zeros_like(end_ref)
    for copy in started:
        copy.wait()


def dense_weights(side, top):
    ids = side[:, :top]
    numer = side[:, top:2 * top] * 32.0 + side[:, 2 * top:3 * top]
    weight = numer / jnp.sum(numer, axis=-1, keepdims=True)
    lane = lax.broadcasted_iota(jnp.int32, (side.shape[0], SIDE), 1)
    expert = jnp.where(lane < EXPERTS, lane, lane - EXPERTS).astype(jnp.float32)
    full = jnp.zeros((side.shape[0], SIDE), jnp.float32)
    for k in range(top):
        full = full + jnp.where(expert == ids[:, k:k + 1], weight[:, k:k + 1], 0.0)
    high = full.astype(jnp.bfloat16).astype(jnp.float32)
    return jnp.where(lane < EXPERTS, high, full - high).astype(jnp.bfloat16)


def layer(top, ff_dev, row_block, step_units, early, mine_ref, theirs_ref, gate_ref, up_ref,
          down_ref, *refs):
    if early:
        refs = refs[3:]
    keep_ref, send_ref, gates, ups, downs, rows_ref, total, weights, hidden, sem = refs
    units, depth = down_ref.shape
    steps = units // step_units
    count = rows_ref.shape[0]
    half = count // 2
    slots = gates.shape[0]

    def copy_of(i, step):
        src, ring = [(gate_ref, gates), (up_ref, ups), (down_ref, downs)][i]
        slot = lax.rem(step, ring.shape[0])
        span = pl.ds(pl.multiple_of(step * step_units, step_units), step_units)
        return pltpu.make_async_copy(src.at[span], ring.at[slot], sem.at[i, slot])

    def start(step):
        for i in range(3):
            copy_of(i, step).start()

    def wait(i, step):
        if isinstance(step, int):
            if step >= early:
                copy_of(i, jnp.int32(step)).wait()
        else:
            @pl.when(step >= early)
            def _():
                copy_of(i, step).wait()

    for step in range(early, min(slots, steps)):
        start(jnp.int32(step))

    first = lax.axis_index("wide") * (units // ff_dev)

    def each_block(body):
        if count == row_block:
            body(pl.ds(0, row_block))
        else:
            @pl.loop(0, count // row_block)
            def _(b):
                body(pl.ds(pl.multiple_of(b * row_block, row_block), row_block))

    rows_ref[:half, :] = mine_ref[...]
    rows_ref[half:, :] = theirs_ref[...]

    def prepare(block):
        side = rows_ref[block, depth:depth + SIDE].astype(jnp.float32)
        weights[block, :] = dense_weights(side, top)
        total[block, :] = jnp.zeros((row_block, depth), jnp.float32)

    each_block(prepare)

    def products(step, block):
        x = rows_ref[block, :depth]
        gate, up = [ring.at[lax.rem(step, ring.shape[0])] for ring in (gates, ups)]
        g = lax.dot_general(gate[...], x, LAST, preferred_element_type=jnp.float32)
        u = lax.dot_general(up[...], x, LAST, preferred_element_type=jnp.float32)
        return g, u

    def activate(step, block, g, u):
        expert = lax.broadcasted_iota(jnp.int32, (step_units, SIDE), 1)
        place = jnp.where(expert < EXPERTS, expert, expert - EXPERTS) - first
        unit = step * step_units + lax.broadcasted_iota(jnp.int32, (step_units, SIDE), 0)
        low = place * ff_dev
        pick = (unit >= low) & (unit < low + ff_dev) & (expert < 2 * EXPERTS)
        pick = jnp.where(pick, 1.0, 0.0).astype(jnp.bfloat16)
        scale = lax.dot_general(pick, weights[block, :], LAST, preferred_element_type=jnp.float32)
        h = g / (1.0 + jnp.exp(-g)) * u * scale
        hidden[lax.rem(step, 2), block, :] = jnp.transpose(h).astype(jnp.bfloat16)

    def down_product(step, block):
        down = downs.at[lax.rem(step, downs.shape[0])]
        total[block, :] += jnp.dot(
            hidden[lax.rem(step, 2), block, :], down[...], preferred_element_type=jnp.float32
        )

    wait(0, 0)
    wait(1, 0)
    each_block(lambda block: activate(0, block, *products(jnp.int32(0), block)))

    @pl.loop(1, steps)
    def _(step):
        @pl.when(step - 1 + slots < steps)
        def _():
            start(step - 1 + slots)

        wait(0, step)
        wait(1, step)
        wait(2, step - 1)

        def both(block):
            g, u = products(step, block)
            down_product(step - 1, block)
            activate(step, block, g, u)

        each_block(both)

    wait(2, steps - 1)
    each_block(lambda block: down_product(jnp.int32(steps - 1), block))
    keep_ref[...] = total[:half, :]
    send_ref[...] = total[half:, :].astype(jnp.bfloat16)


def build(axes):
    def local(tokens, expert_ids, gate_numer, w_gate, w_up, w_down):
        local_count, ff_dev, depth = w_gate.shape
        units = local_count * ff_dev
        top = expert_ids.shape[1]
        step_units = next(n for n in range(256, 0, -16) if units % n == 0)
        weights = [w.reshape(units, depth) for w in (w_gate, w_up, w_down)]
        weights = [pltpu.with_memory_space_constraint(w, pltpu.HBM) for w in weights]
        small = pltpu.CompilerParams(vmem_limit_bytes=2 << 20)
        own = (tokens, expert_ids, gate_numer)
        own = [pltpu.with_memory_space_constraint(a, pltpu.HBM) for a in own]
        rows = pl.pallas_call(
            with_routing,
            out_shape=jax.ShapeDtypeStruct((tokens.shape[0], depth + SIDE), jnp.bfloat16),
            in_specs=[HBM] * 3,
            out_specs=VMEM,
            scratch_shapes=[
                pltpu.VMEM(expert_ids.shape, jnp.int32),
                pltpu.VMEM(gate_numer.shape, jnp.int32),
                pltpu.SemaphoreType.DMA((3,)),
            ],
            compiler_params=small,
            name="with_routing",
        )(*own)
        hops = [None]
        for axis, size in axes:
            by = size // 2
            while by:
                hops.append((axis, size, by))
                by //= 2
        span = lax.axis_size("wide")
        slots = min(SLOTS, units // step_units)
        ring_shapes = [
            pltpu.VMEM((n, step_units, depth), jnp.bfloat16) for n in (slots, slots, slots + 1)
        ]
        ring = []
        early = 0
        for number, hop in enumerate(hops):
            if hop is None:
                theirs = [shift(rows, "wide", span, -by) for by in range(1, span)]
            else:
                theirs = [swap(rows, *hop)]
            steps = EARLY[number] if number < len(EARLY) and units >= 8 * step_units else 0
            ends = []
            if steps:
                *ring, end = pl.pallas_call(
                    functools.partial(bring, early, steps),
                    out_shape=ring_shapes + [jax.ShapeDtypeStruct((8, 128), jnp.float32)],
                    in_specs=[HBM] * 3 + [pl.BlockSpec(memory_space=pl.ANY)] + [VMEM] * len(ring),
                    out_specs=[VMEM] * 4,
                    scratch_shapes=[pltpu.SemaphoreType.DMA((3, steps, 2))],
                    input_output_aliases={4 + i: i for i in range(len(ring))},
                    compiler_params=small,
                    cost_estimate=pl.CostEstimate(
                        flops=0,
                        bytes_accessed=6 * steps * step_units * depth,
                        transcendentals=0,
                    ),
                    name="bring_weights",
                )(*weights, rows, *ring)
                early += steps
                ends = [end]
            if hop is hops[-1]:
                break
            all_rows = [rows] + theirs
            count = sum(part.shape[0] for part in all_rows)
            if count <= 64:
                rows = pl.pallas_call(
                    functools.partial(join, len(all_rows)),
                    out_shape=jax.ShapeDtypeStruct((count, depth + SIDE), jnp.bfloat16),
                    in_specs=[VMEM] * len(all_rows)
                    + [pl.BlockSpec(memory_space=pl.ANY)] * len(ends),
                    out_specs=VMEM,
                    compiler_params=small,
                    name="join",
                )(*all_rows, *ends)
            else:
                rows = jnp.concatenate(all_rows, axis=0)
        half = rows.shape[0]
        count = 2 * half
        row_block = min(count, 64)
        keep, send, *_ = pl.pallas_call(
            functools.partial(layer, top, ff_dev, row_block, step_units, early),
            out_shape=[
                jax.ShapeDtypeStruct((half, depth), jnp.float32),
                jax.ShapeDtypeStruct((half, depth), jnp.bfloat16),
            ]
            + (ring_shapes if early else []),
            in_specs=[VMEM] * 2 + [HBM] * 3 + [VMEM] * len(ring),
            out_specs=[VMEM] * (5 if early else 2),
            scratch_shapes=([] if early else ring_shapes)
            + [
                pltpu.VMEM((count, depth + SIDE), jnp.bfloat16),
                pltpu.VMEM((count, depth), jnp.float32),
                pltpu.VMEM((count, SIDE), jnp.bfloat16),
                pltpu.VMEM((2, count, step_units), jnp.bfloat16),
                pltpu.SemaphoreType.DMA((3, slots + 1)),
            ],
            input_output_aliases={5 + i: 2 + i for i in range(len(ring))},
            compiler_params=pltpu.CompilerParams(
                vmem_limit_bytes=GRANT if early else 60 << 20
            ),
            cost_estimate=pl.CostEstimate(
                flops=6 * count * units * depth,
                bytes_accessed=6 * (units - early * step_units) * depth,
                transcendentals=count * units,
            ),
            name="expert_layer",
        )(rows, *theirs, *weights, *ring)
        total = keep + swap(send, *hops[-1]).astype(jnp.float32)
        for hop in reversed(hops[1:-1]):
            half = total.shape[0] // 2
            theirs = swap(total[half:].astype(jnp.bfloat16), *hop)
            total = total[:half] + theirs.astype(jnp.float32)
        blocks = total.reshape(span, tokens.shape[0], depth)
        total = blocks[0]
        for by in range(1, span):
            theirs = shift(blocks[by].astype(jnp.bfloat16), "wide", span, by)
            total = total + theirs.astype(jnp.float32)
        return total.astype(jnp.bfloat16)

    return local


def solution(mesh):
    rows = P(("grp", "wide", "sec", "sub"), None)
    weights = P("wide", ("sec", "sub"), None)
    axes = [(name, mesh.shape[name]) for name in ("sec", "sub")]
    return jax.shard_map(
        build(axes),
        mesh=mesh,
        in_specs=(rows, rows, rows, weights, weights, weights),
        out_specs=rows,
        check_vma=False,
    )
```

```python
import functools

import jax
import jax.numpy as jnp
from jax import lax
from jax.experimental import pallas as pl
from jax.experimental.pallas import tpu as pltpu
from jax.sharding import PartitionSpec as P

EXPERTS = 32
SIDE = 128
SLOTS = 4
EARLY = ((1, 1, 1), (2, 1, 1), (0, 1, 0))
GRANT = 8 << 20

VMEM = pl.BlockSpec(memory_space=pltpu.VMEM)
HBM = pl.BlockSpec(memory_space=pltpu.HBM)
LAST = (((1,), (1,)), ((), ()))


def swap(x, axis, size, by):
    return lax.ppermute(x, axis, [(i, i ^ by) for i in range(size)])


def shift(x, axis, size, by):
    return lax.ppermute(x, axis, [(i, (i + by) % size) for i in range(size)])


def with_routing(tokens_ref, ids_ref, numer_ref, out_ref, ids, numer, sem):
    rows, depth = tokens_ref.shape
    top = ids_ref.shape[1]
    pairs = [(tokens_ref, out_ref.at[:, pl.ds(0, depth)]), (ids_ref, ids), (numer_ref, numer)]
    started = [pltpu.make_async_copy(a, b, sem.at[i]) for i, (a, b) in enumerate(pairs)]
    for copy in started:
        copy.start()
    for copy in started:
        copy.wait()
    pad = jnp.zeros((rows, SIDE - 3 * top), jnp.int32)
    side = jnp.concatenate([ids[...], numer[...] >> 5, numer[...] & 31, pad], axis=1)
    out_ref[:, depth:] = side.astype(jnp.float32).astype(jnp.bfloat16)


def join(parts, *refs):
    out_ref = refs[-1]
    count = refs[0].shape[0]
    for part in range(parts):
        out_ref[part * count:(part + 1) * count, :] = refs[part][...]


def bring(firsts, counts, gate_ref, up_ref, down_ref, after_ref, *refs):
    gates, ups, downs, end_ref, sem = refs[-5:]
    size = gates.shape[1]
    half = size // 2
    started = []
    for i, (ref, ring) in enumerate([(gate_ref, gates), (up_ref, ups), (down_ref, downs)]):
        for step in range(firsts[i], firsts[i] + counts[i]):
            for part in range(2):
                started.append(
                    pltpu.make_async_copy(
                        ref.at[pl.ds(step * size + part * half, half)],
                        ring.at[step, pl.ds(part * half, half)],
                        sem.at[i, step - firsts[i], part],
                    )
                )
    for copy in started:
        copy.start()
    end_ref[...] = jnp.zeros_like(end_ref)
    for copy in started:
        copy.wait()


def dense_weights(side, top):
    ids = side[:, :top]
    numer = side[:, top:2 * top] * 32.0 + side[:, 2 * top:3 * top]
    weight = numer / jnp.sum(numer, axis=-1, keepdims=True)
    lane = lax.broadcasted_iota(jnp.int32, (side.shape[0], SIDE), 1)
    expert = jnp.where(lane < EXPERTS, lane, lane - EXPERTS).astype(jnp.float32)
    full = jnp.zeros((side.shape[0], SIDE), jnp.float32)
    for k in range(top):
        full = full + jnp.where(expert == ids[:, k:k + 1], weight[:, k:k + 1], 0.0)
    high = full.astype(jnp.bfloat16).astype(jnp.float32)
    return jnp.where(lane < EXPERTS, high, full - high).astype(jnp.bfloat16)


def layer(top, ff_dev, row_block, step_units, early, mine_ref, theirs_ref, gate_ref, up_ref,
          down_ref, *refs):
    if max(early):
        refs = refs[3:]
    keep_ref, send_ref, gates, ups, downs, rows_ref, total, weights, hidden, sem = refs
    units, depth = down_ref.shape
    steps = units // step_units
    count = rows_ref.shape[0]
    half = count // 2
    slots = gates.shape[0]

    def copy_of(i, step):
        src, ring = [(gate_ref, gates), (up_ref, ups), (down_ref, downs)][i]
        slot = lax.rem(step, ring.shape[0])
        span = pl.ds(pl.multiple_of(step * step_units, step_units), step_units)
        return pltpu.make_async_copy(src.at[span], ring.at[slot], sem.at[i, slot])

    def start(step):
        for i in range(3):
            copy_of(i, step).start()

    def wait(i, step):
        if isinstance(step, int):
            if step >= early[i]:
                copy_of(i, jnp.int32(step)).wait()
        else:
            @pl.when(step >= early[i])
            def _():
                copy_of(i, step).wait()

    for step in range(min(slots, steps)):
        for i in range(3):
            if step >= early[i]:
                copy_of(i, jnp.int32(step)).start()

    first = lax.axis_index("wide") * (units // ff_dev)

    def each_block(body):
        if count == row_block:
            body(pl.ds(0, row_block))
        else:
            @pl.loop(0, count // row_block)
            def _(b):
                body(pl.ds(pl.multiple_of(b * row_block, row_block), row_block))

    rows_ref[:half, :] = mine_ref[...]
    rows_ref[half:, :] = theirs_ref[...]

    def prepare(block):
        side = rows_ref[block, depth:depth + SIDE].astype(jnp.float32)
        weights[block, :] = dense_weights(side, top)
        total[block, :] = jnp.zeros((row_block, depth), jnp.float32)

    each_block(prepare)

    def products(step, block):
        x = rows_ref[block, :depth]
        gate, up = [ring.at[lax.rem(step, ring.shape[0])] for ring in (gates, ups)]
        g = lax.dot_general(gate[...], x, LAST, preferred_element_type=jnp.float32)
        u = lax.dot_general(up[...], x, LAST, preferred_element_type=jnp.float32)
        return g, u

    def activate(step, block, g, u):
        expert = lax.broadcasted_iota(jnp.int32, (step_units, SIDE), 1)
        place = jnp.where(expert < EXPERTS, expert, expert - EXPERTS) - first
        unit = step * step_units + lax.broadcasted_iota(jnp.int32, (step_units, SIDE), 0)
        low = place * ff_dev
        pick = (unit >= low) & (unit < low + ff_dev) & (expert < 2 * EXPERTS)
        pick = jnp.where(pick, 1.0, 0.0).astype(jnp.bfloat16)
        scale = lax.dot_general(pick, weights[block, :], LAST, preferred_element_type=jnp.float32)
        h = g / (1.0 + jnp.exp(-g)) * u * scale
        hidden[lax.rem(step, 2), block, :] = jnp.transpose(h).astype(jnp.bfloat16)

    def down_product(step, block):
        down = downs.at[lax.rem(step, downs.shape[0])]
        total[block, :] += jnp.dot(
            hidden[lax.rem(step, 2), block, :], down[...], preferred_element_type=jnp.float32
        )

    wait(0, 0)
    wait(1, 0)
    each_block(lambda block: activate(0, block, *products(jnp.int32(0), block)))

    @pl.loop(1, steps)
    def _(step):
        @pl.when(step - 1 + slots < steps)
        def _():
            start(step - 1 + slots)

        wait(0, step)
        wait(1, step)
        wait(2, step - 1)

        def both(block):
            g, u = products(step, block)
            down_product(step - 1, block)
            activate(step, block, g, u)

        each_block(both)

    wait(2, steps - 1)
    each_block(lambda block: down_product(jnp.int32(steps - 1), block))
    keep_ref[...] = total[:half, :]
    send_ref[...] = total[half:, :].astype(jnp.bfloat16)


def build(axes):
    def local(tokens, expert_ids, gate_numer, w_gate, w_up, w_down):
        local_count, ff_dev, depth = w_gate.shape
        units = local_count * ff_dev
        top = expert_ids.shape[1]
        step_units = next(n for n in range(256, 0, -16) if units % n == 0)
        weights = [w.reshape(units, depth) for w in (w_gate, w_up, w_down)]
        weights = [pltpu.with_memory_space_constraint(w, pltpu.HBM) for w in weights]
        small = pltpu.CompilerParams(vmem_limit_bytes=2 << 20)
        own = (tokens, expert_ids, gate_numer)
        own = [pltpu.with_memory_space_constraint(a, pltpu.HBM) for a in own]
        rows = pl.pallas_call(
            with_routing,
            out_shape=jax.ShapeDtypeStruct((tokens.shape[0], depth + SIDE), jnp.bfloat16),
            in_specs=[HBM] * 3,
            out_specs=VMEM,
            scratch_shapes=[
                pltpu.VMEM(expert_ids.shape, jnp.int32),
                pltpu.VMEM(gate_numer.shape, jnp.int32),
                pltpu.SemaphoreType.DMA((3,)),
            ],
            compiler_params=small,
            name="with_routing",
        )(*own)
        hops = [None]
        for axis, size in axes:
            by = size // 2
            while by:
                hops.append((axis, size, by))
                by //= 2
        span = lax.axis_size("wide")
        slots = min(SLOTS, units // step_units)
        ring_shapes = [
            pltpu.VMEM((n, step_units, depth), jnp.bfloat16) for n in (slots, slots, slots + 1)
        ]
        ring = []
        early = (0, 0, 0)
        for number, hop in enumerate(hops):
            if hop is None:
                theirs = [shift(rows, "wide", span, -by) for by in range(1, span)]
            else:
                theirs = [swap(rows, *hop)]
            more = EARLY[number] if number < len(EARLY) and units >= 8 * step_units else (0, 0, 0)
            ends = []
            if max(more):
                *ring, end = pl.pallas_call(
                    functools.partial(bring, early, more),
                    out_shape=ring_shapes + [jax.ShapeDtypeStruct((8, 128), jnp.float32)],
                    in_specs=[HBM] * 3 + [pl.BlockSpec(memory_space=pl.ANY)] + [VMEM] * len(ring),
                    out_specs=[VMEM] * 4,
                    scratch_shapes=[pltpu.SemaphoreType.DMA((3, max(more), 2))],
                    input_output_aliases={4 + i: i for i in range(len(ring))},
                    compiler_params=small,
                    cost_estimate=pl.CostEstimate(
                        flops=0,
                        bytes_accessed=2 * sum(more) * step_units * depth,
                        transcendentals=0,
                    ),
                    name="bring_weights",
                )(*weights, rows, *ring)
                early = tuple(a + b for a, b in zip(early, more))
                ends = [end]
            if hop is hops[-1]:
                break
            all_rows = [rows] + theirs
            count = sum(part.shape[0] for part in all_rows)
            if count <= 64:
                rows = pl.pallas_call(
                    functools.partial(join, len(all_rows)),
                    out_shape=jax.ShapeDtypeStruct((count, depth + SIDE), jnp.bfloat16),
                    in_specs=[VMEM] * len(all_rows)
                    + [pl.BlockSpec(memory_space=pl.ANY)] * len(ends),
                    out_specs=VMEM,
                    compiler_params=small,
                    name="join",
                )(*all_rows, *ends)
            else:
                rows = jnp.concatenate(all_rows, axis=0)
        half = rows.shape[0]
        count = 2 * half
        row_block = min(count, 64)
        keep, send, *_ = pl.pallas_call(
            functools.partial(layer, top, ff_dev, row_block, step_units, early),
            out_shape=[
                jax.ShapeDtypeStruct((half, depth), jnp.float32),
                jax.ShapeDtypeStruct((half, depth), jnp.bfloat16),
            ]
            + (ring_shapes if ring else []),
            in_specs=[VMEM] * 2 + [HBM] * 3 + [VMEM] * len(ring),
            out_specs=[VMEM] * (5 if ring else 2),
            scratch_shapes=([] if ring else ring_shapes)
            + [
                pltpu.VMEM((count, depth + SIDE), jnp.bfloat16),
                pltpu.VMEM((count, depth), jnp.float32),
                pltpu.VMEM((count, SIDE), jnp.bfloat16),
                pltpu.VMEM((2, count, step_units), jnp.bfloat16),
                pltpu.SemaphoreType.DMA((3, slots + 1)),
            ],
            input_output_aliases={5 + i: 2 + i for i in range(len(ring))},
            compiler_params=pltpu.CompilerParams(
                vmem_limit_bytes=GRANT if ring else 60 << 20
            ),
            cost_estimate=pl.CostEstimate(
                flops=6 * count * units * depth,
                bytes_accessed=2 * (3 * units - sum(early) * step_units) * depth,
                transcendentals=count * units,
            ),
            name="expert_layer",
        )(rows, *theirs, *weights, *ring)
        total = keep + swap(send, *hops[-1]).astype(jnp.float32)
        for hop in reversed(hops[1:-1]):
            half = total.shape[0] // 2
            theirs = swap(total[half:].astype(jnp.bfloat16), *hop)
            total = total[:half] + theirs.astype(jnp.float32)
        blocks = total.reshape(span, tokens.shape[0], depth)
        total = blocks[0]
        for by in range(1, span):
            theirs = shift(blocks[by].astype(jnp.bfloat16), "wide", span, by)
            total = total + theirs.astype(jnp.float32)
        return total.astype(jnp.bfloat16)

    return local


def solution(mesh):
    rows = P(("grp", "wide", "sec", "sub"), None)
    weights = P("wide", ("sec", "sub"), None)
    axes = [(name, mesh.shape[name]) for name in ("sec", "sub")]
    return jax.shard_map(
        build(axes),
        mesh=mesh,
        in_specs=(rows, rows, rows, weights, weights, weights),
        out_specs=rows,
        check_vma=False,
    )
```

```python
import functools

import jax
import jax.numpy as jnp
from jax import lax
from jax.experimental import pallas as pl
from jax.experimental.pallas import tpu as pltpu
from jax.sharding import PartitionSpec as P

EXPERTS = 32
SIDE = 128
SLOTS = 4
EARLY = ((1, 1, 1), (2, 1, 1))
GRANT = 8 << 20

VMEM = pl.BlockSpec(memory_space=pltpu.VMEM)
HBM = pl.BlockSpec(memory_space=pltpu.HBM)
LAST = (((1,), (1,)), ((), ()))


def swap(x, axis, size, by):
    return lax.ppermute(x, axis, [(i, i ^ by) for i in range(size)])


def shift(x, axis, size, by):
    return lax.ppermute(x, axis, [(i, (i + by) % size) for i in range(size)])


def with_routing(tokens_ref, ids_ref, numer_ref, out_ref, ids, numer, sem):
    rows, depth = tokens_ref.shape
    top = ids_ref.shape[1]
    pairs = [(tokens_ref, out_ref.at[:, pl.ds(0, depth)]), (ids_ref, ids), (numer_ref, numer)]
    started = [pltpu.make_async_copy(a, b, sem.at[i]) for i, (a, b) in enumerate(pairs)]
    for copy in started:
        copy.start()
    for copy in started:
        copy.wait()
    pad = jnp.zeros((rows, SIDE - 3 * top), jnp.int32)
    side = jnp.concatenate([ids[...], numer[...] >> 5, numer[...] & 31, pad], axis=1)
    out_ref[:, depth:] = side.astype(jnp.float32).astype(jnp.bfloat16)


def join(parts, *refs):
    out_ref = refs[-1]
    count = refs[0].shape[0]
    for part in range(parts):
        out_ref[part * count:(part + 1) * count, :] = refs[part][...]


def slot_of(i, step, pairs, downs):
    if i == 2:
        return downs.at[lax.rem(step, downs.shape[0])]
    size = pairs.shape[1] // 2
    return pairs.at[lax.rem(step, pairs.shape[0]), pl.ds(i * size, size)]


def bring(firsts, counts, gate_ref, up_ref, down_ref, after_ref, *refs):
    pairs, downs, end_ref, sem = refs[-4:]
    size = downs.shape[1]
    half = size // 2
    started = []
    for i, ref in enumerate([gate_ref, up_ref, down_ref]):
        for step in range(firsts[i], firsts[i] + counts[i]):
            slot = slot_of(i, jnp.int32(step), pairs, downs)
            for part in range(2):
                started.append(
                    pltpu.make_async_copy(
                        ref.at[pl.ds(step * size + part * half, half)],
                        slot.at[pl.ds(part * half, half)],
                        sem.at[i, step - firsts[i], part],
                    )
                )
    for copy in started:
        copy.start()
    end_ref[...] = jnp.zeros_like(end_ref)
    for copy in started:
        copy.wait()


def dense_weights(side, top):
    ids = side[:, :top]
    numer = side[:, top:2 * top] * 32.0 + side[:, 2 * top:3 * top]
    weight = numer / jnp.sum(numer, axis=-1, keepdims=True)
    lane = lax.broadcasted_iota(jnp.int32, (side.shape[0], SIDE), 1)
    expert = jnp.where(lane < EXPERTS, lane, lane - EXPERTS).astype(jnp.float32)
    full = jnp.zeros((side.shape[0], SIDE), jnp.float32)
    for k in range(top):
        full = full + jnp.where(expert == ids[:, k:k + 1], weight[:, k:k + 1], 0.0)
    high = full.astype(jnp.bfloat16).astype(jnp.float32)
    return jnp.where(lane < EXPERTS, high, full - high).astype(jnp.bfloat16)


def layer(top, ff_dev, row_block, step_units, early, mine_ref, theirs_ref, gate_ref, up_ref,
          down_ref, *refs):
    if max(early):
        refs = refs[2:]
    keep_ref, send_ref, pairs, downs, rows_ref, total, weights, hidden, sem = refs
    units, depth = down_ref.shape
    steps = units // step_units
    count = rows_ref.shape[0]
    half = count // 2
    slots = pairs.shape[0]

    def copy_of(i, step):
        src = [gate_ref, up_ref, down_ref][i]
        span = pl.ds(pl.multiple_of(step * step_units, step_units), step_units)
        return pltpu.make_async_copy(
            src.at[span],
            slot_of(i, step, pairs, downs),
            sem.at[i, lax.rem(step, downs.shape[0] if i == 2 else slots)],
        )

    def start(step):
        for i in range(3):
            copy_of(i, step).start()

    def wait(i, step):
        if isinstance(step, int):
            if step >= early[i]:
                copy_of(i, jnp.int32(step)).wait()
        else:
            @pl.when(step >= early[i])
            def _():
                copy_of(i, step).wait()

    for step in range(min(slots, steps)):
        for i in range(3):
            if step >= early[i]:
                copy_of(i, jnp.int32(step)).start()

    first = lax.axis_index("wide") * (units // ff_dev)

    def each_block(body):
        if count == row_block:
            body(pl.ds(0, row_block))
        else:
            @pl.loop(0, count // row_block)
            def _(b):
                body(pl.ds(pl.multiple_of(b * row_block, row_block), row_block))

    rows_ref[:half, :] = mine_ref[...]
    rows_ref[half:, :] = theirs_ref[...]

    def prepare(block):
        side = rows_ref[block, depth:depth + SIDE].astype(jnp.float32)
        weights[block, :] = dense_weights(side, top)
        total[block, :] = jnp.zeros((row_block, depth), jnp.float32)

    each_block(prepare)

    def products(step, block):
        x = rows_ref[block, :depth]
        pair = pairs[lax.rem(step, slots)]
        both = lax.dot_general(pair, x, LAST, preferred_element_type=jnp.float32)
        return both[:step_units], both[step_units:]

    def activate(step, block, g, u):
        expert = lax.broadcasted_iota(jnp.int32, (step_units, SIDE), 1)
        place = jnp.where(expert < EXPERTS, expert, expert - EXPERTS) - first
        unit = step * step_units + lax.broadcasted_iota(jnp.int32, (step_units, SIDE), 0)
        low = place * ff_dev
        pick = (unit >= low) & (unit < low + ff_dev) & (expert < 2 * EXPERTS)
        pick = jnp.where(pick, 1.0, 0.0).astype(jnp.bfloat16)
        scale = lax.dot_general(pick, weights[block, :], LAST, preferred_element_type=jnp.float32)
        h = g / (1.0 + jnp.exp(-g)) * u * scale
        hidden[lax.rem(step, 2), block, :] = jnp.transpose(h).astype(jnp.bfloat16)

    def down_product(step, block):
        down = downs.at[lax.rem(step, downs.shape[0])]
        total[block, :] += jnp.dot(
            hidden[lax.rem(step, 2), block, :], down[...], preferred_element_type=jnp.float32
        )

    wait(0, 0)
    wait(1, 0)
    each_block(lambda block: activate(0, block, *products(jnp.int32(0), block)))

    @pl.loop(1, steps)
    def _(step):
        @pl.when(step - 1 + slots < steps)
        def _():
            start(step - 1 + slots)

        wait(0, step)
        wait(1, step)
        wait(2, step - 1)

        def both(block):
            g, u = products(step, block)
            down_product(step - 1, block)
            activate(step, block, g, u)

        each_block(both)

    wait(2, steps - 1)
    each_block(lambda block: down_product(jnp.int32(steps - 1), block))
    keep_ref[...] = total[:half, :]
    send_ref[...] = total[half:, :].astype(jnp.bfloat16)


def build(axes):
    def local(tokens, expert_ids, gate_numer, w_gate, w_up, w_down):
        local_count, ff_dev, depth = w_gate.shape
        units = local_count * ff_dev
        top = expert_ids.shape[1]
        step_units = next(n for n in range(256, 0, -16) if units % n == 0)
        weights = [w.reshape(units, depth) for w in (w_gate, w_up, w_down)]
        weights = [pltpu.with_memory_space_constraint(w, pltpu.HBM) for w in weights]
        small = pltpu.CompilerParams(vmem_limit_bytes=2 << 20)
        own = (tokens, expert_ids, gate_numer)
        own = [pltpu.with_memory_space_constraint(a, pltpu.HBM) for a in own]
        rows = pl.pallas_call(
            with_routing,
            out_shape=jax.ShapeDtypeStruct((tokens.shape[0], depth + SIDE), jnp.bfloat16),
            in_specs=[HBM] * 3,
            out_specs=VMEM,
            scratch_shapes=[
                pltpu.VMEM(expert_ids.shape, jnp.int32),
                pltpu.VMEM(gate_numer.shape, jnp.int32),
                pltpu.SemaphoreType.DMA((3,)),
            ],
            compiler_params=small,
            name="with_routing",
        )(*own)
        hops = [None]
        for axis, size in axes:
            by = size // 2
            while by:
                hops.append((axis, size, by))
                by //= 2
        span = lax.axis_size("wide")
        slots = min(SLOTS, units // step_units)
        ring_shapes = [
            pltpu.VMEM((slots, 2 * step_units, depth), jnp.bfloat16),
            pltpu.VMEM((slots + 1, step_units, depth), jnp.bfloat16),
        ]
        ring = []
        early = (0, 0, 0)
        for number, hop in enumerate(hops):
            if hop is None:
                theirs = [shift(rows, "wide", span, -by) for by in range(1, span)]
            else:
                theirs = [swap(rows, *hop)]
            more = EARLY[number] if number < len(EARLY) and units >= 8 * step_units else (0, 0, 0)
            ends = []
            if max(more):
                *ring, end = pl.pallas_call(
                    functools.partial(bring, early, more),
                    out_shape=ring_shapes + [jax.ShapeDtypeStruct((8, 128), jnp.float32)],
                    in_specs=[HBM] * 3 + [pl.BlockSpec(memory_space=pl.ANY)] + [VMEM] * len(ring),
                    out_specs=[VMEM] * 3,
                    scratch_shapes=[pltpu.SemaphoreType.DMA((3, max(more), 2))],
                    input_output_aliases={4 + i: i for i in range(len(ring))},
                    compiler_params=small,
                    cost_estimate=pl.CostEstimate(
                        flops=0,
                        bytes_accessed=2 * sum(more) * step_units * depth,
                        transcendentals=0,
                    ),
                    name="bring_weights",
                )(*weights, rows, *ring)
                early = tuple(a + b for a, b in zip(early, more))
                ends = [end]
            if hop is hops[-1]:
                break
            all_rows = [rows] + theirs
            count = sum(part.shape[0] for part in all_rows)
            if count <= 64:
                rows = pl.pallas_call(
                    functools.partial(join, len(all_rows)),
                    out_shape=jax.ShapeDtypeStruct((count, depth + SIDE), jnp.bfloat16),
                    in_specs=[VMEM] * len(all_rows)
                    + [pl.BlockSpec(memory_space=pl.ANY)] * len(ends),
                    out_specs=VMEM,
                    compiler_params=small,
                    name="join",
                )(*all_rows, *ends)
            else:
                rows = jnp.concatenate(all_rows, axis=0)
        half = rows.shape[0]
        count = 2 * half
        row_block = min(count, 64)
        keep, send, *_ = pl.pallas_call(
            functools.partial(layer, top, ff_dev, row_block, step_units, early),
            out_shape=[
                jax.ShapeDtypeStruct((half, depth), jnp.float32),
                jax.ShapeDtypeStruct((half, depth), jnp.bfloat16),
            ]
            + (ring_shapes if ring else []),
            in_specs=[VMEM] * 2 + [HBM] * 3 + [VMEM] * len(ring),
            out_specs=[VMEM] * (4 if ring else 2),
            scratch_shapes=([] if ring else ring_shapes)
            + [
                pltpu.VMEM((count, depth + SIDE), jnp.bfloat16),
                pltpu.VMEM((count, depth), jnp.float32),
                pltpu.VMEM((count, SIDE), jnp.bfloat16),
                pltpu.VMEM((2, count, step_units), jnp.bfloat16),
                pltpu.SemaphoreType.DMA((3, slots + 1)),
            ],
            input_output_aliases={5 + i: 2 + i for i in range(len(ring))},
            compiler_params=pltpu.CompilerParams(
                vmem_limit_bytes=GRANT if ring else 60 << 20
            ),
            cost_estimate=pl.CostEstimate(
                flops=6 * count * units * depth,
                bytes_accessed=2 * (3 * units - sum(early) * step_units) * depth,
                transcendentals=count * units,
            ),
            name="expert_layer",
        )(rows, *theirs, *weights, *ring)
        total = keep + swap(send, *hops[-1]).astype(jnp.float32)
        for hop in reversed(hops[1:-1]):
            half = total.shape[0] // 2
            theirs = swap(total[half:].astype(jnp.bfloat16), *hop)
            total = total[:half] + theirs.astype(jnp.float32)
        blocks = total.reshape(span, tokens.shape[0], depth)
        total = blocks[0]
        for by in range(1, span):
            theirs = shift(blocks[by].astype(jnp.bfloat16), "wide", span, by)
            total = total + theirs.astype(jnp.float32)
        return total.astype(jnp.bfloat16)

    return local


def solution(mesh):
    rows = P(("grp", "wide", "sec", "sub"), None)
    weights = P("wide", ("sec", "sub"), None)
    axes = [(name, mesh.shape[name]) for name in ("sec", "sub")]
    return jax.shard_map(
        build(axes),
        mesh=mesh,
        in_specs=(rows, rows, rows, weights, weights, weights),
        out_specs=rows,
        check_vma=False,
    )
```

```python
import functools

import jax
import jax.numpy as jnp
from jax import lax
from jax.experimental import pallas as pl
from jax.experimental.pallas import tpu as pltpu
from jax.sharding import PartitionSpec as P

EXPERTS = 32
SIDE = 128
SLOTS = 4
EARLY = ((1, 1, 1), (2, 1, 1))
GRANT = 8 << 20

VMEM = pl.BlockSpec(memory_space=pltpu.VMEM)
HBM = pl.BlockSpec(memory_space=pltpu.HBM)
LAST = (((1,), (1,)), ((), ()))


def swap(x, axis, size, by):
    return lax.ppermute(x, axis, [(i, i ^ by) for i in range(size)])


def shift(x, axis, size, by):
    return lax.ppermute(x, axis, [(i, (i + by) % size) for i in range(size)])


def with_routing(tokens_ref, ids_ref, numer_ref, out_ref, ids, numer, sem):
    rows, depth = tokens_ref.shape
    top = ids_ref.shape[1]
    pairs = [(tokens_ref, out_ref.at[:, pl.ds(0, depth)]), (ids_ref, ids), (numer_ref, numer)]
    started = [pltpu.make_async_copy(a, b, sem.at[i]) for i, (a, b) in enumerate(pairs)]
    for copy in started:
        copy.start()
    for copy in started:
        copy.wait()
    pad = jnp.zeros((rows, SIDE - 3 * top), jnp.int32)
    side = jnp.concatenate([ids[...], numer[...] >> 5, numer[...] & 31, pad], axis=1)
    out_ref[:, depth:] = side.astype(jnp.float32).astype(jnp.bfloat16)


def join(parts, *refs):
    out_ref = refs[-1]
    count = refs[0].shape[0]
    for part in range(parts):
        out_ref[part * count:(part + 1) * count, :] = refs[part][...]


def bring(firsts, counts, gate_ref, up_ref, down_ref, after_ref, *refs):
    gates, ups, downs, end_ref, sem = refs[-5:]
    size = gates.shape[1]
    half = size // 2
    started = []
    for i, (ref, ring) in enumerate([(gate_ref, gates), (up_ref, ups), (down_ref, downs)]):
        for step in range(firsts[i], firsts[i] + counts[i]):
            for part in range(2):
                started.append(
                    pltpu.make_async_copy(
                        ref.at[pl.ds(step * size + part * half, half)],
                        ring.at[step, pl.ds(part * half, half)],
                        sem.at[i, step - firsts[i], part],
                    )
                )
    for copy in started:
        copy.start()
    end_ref[...] = jnp.zeros_like(end_ref)
    for copy in started:
        copy.wait()


def dense_weights(side, top):
    ids = side[:, :top]
    numer = side[:, top:2 * top] * 32.0 + side[:, 2 * top:3 * top]
    weight = numer / jnp.sum(numer, axis=-1, keepdims=True)
    lane = lax.broadcasted_iota(jnp.int32, (side.shape[0], SIDE), 1)
    expert = jnp.where(lane < EXPERTS, lane, lane - EXPERTS).astype(jnp.float32)
    full = jnp.zeros((side.shape[0], SIDE), jnp.float32)
    for k in range(top):
        full = full + jnp.where(expert == ids[:, k:k + 1], weight[:, k:k + 1], 0.0)
    high = full.astype(jnp.bfloat16).astype(jnp.float32)
    return jnp.where(lane < EXPERTS, high, full - high).astype(jnp.bfloat16)


def layer(top, ff_dev, row_block, step_units, early, mine_ref, theirs_ref, gate_ref, up_ref,
          down_ref, *refs):
    if max(early):
        refs = refs[3:]
    keep_ref, send_ref, gates, ups, downs, rows_ref, total, weights, hidden, sem = refs
    units, depth = down_ref.shape
    steps = units // step_units
    count = rows_ref.shape[0]
    half = count // 2
    slots = gates.shape[0]

    def copy_of(i, step):
        src, ring = [(gate_ref, gates), (up_ref, ups), (down_ref, downs)][i]
        slot = lax.rem(step, ring.shape[0])
        span = pl.ds(pl.multiple_of(step * step_units, step_units), step_units)
        return pltpu.make_async_copy(src.at[span], ring.at[slot], sem.at[i, slot])

    def start(step):
        for i in range(3):
            copy_of(i, step).start()

    def wait(i, step):
        if isinstance(step, int):
            if step >= early[i]:
                copy_of(i, jnp.int32(step)).wait()
        else:
            @pl.when(step >= early[i])
            def _():
                copy_of(i, step).wait()

    for step in range(min(slots, steps)):
        for i in range(3):
            if step >= early[i]:
                copy_of(i, jnp.int32(step)).start()

    first = lax.axis_index("wide") * (units // ff_dev)

    def each_block(body):
        if count == row_block:
            body(pl.ds(0, row_block))
        else:
            @pl.loop(0, count // row_block)
            def _(b):
                body(pl.ds(pl.multiple_of(b * row_block, row_block), row_block))

    rows_ref[:half, :] = mine_ref[...]
    rows_ref[half:, :] = theirs_ref[...]

    def prepare(block):
        side = rows_ref[block, depth:depth + SIDE].astype(jnp.float32)
        weights[block, :] = dense_weights(side, top)
        total[block, :] = jnp.zeros((row_block, depth), jnp.float32)

    each_block(prepare)

    def products(step, block):
        x = rows_ref[block, :depth]
        gate, up = [ring.at[lax.rem(step, ring.shape[0])] for ring in (gates, ups)]
        g = lax.dot_general(gate[...], x, LAST, preferred_element_type=jnp.float32)
        u = lax.dot_general(up[...], x, LAST, preferred_element_type=jnp.float32)
        return g, u

    def activate(step, block, g, u):
        expert = lax.broadcasted_iota(jnp.int32, (step_units, SIDE), 1)
        place = jnp.where(expert < EXPERTS, expert, expert - EXPERTS) - first
        unit = step * step_units + lax.broadcasted_iota(jnp.int32, (step_units, SIDE), 0)
        low = place * ff_dev
        pick = (unit >= low) & (unit < low + ff_dev) & (expert < 2 * EXPERTS)
        pick = jnp.where(pick, 1.0, 0.0).astype(jnp.bfloat16)
        scale = lax.dot_general(pick, weights[block, :], LAST, preferred_element_type=jnp.float32)
        h = g / (1.0 + jnp.exp(-g)) * u * scale
        hidden[lax.rem(step, 2), block, :] = jnp.transpose(h).astype(jnp.bfloat16)

    def down_product(step, block):
        down = downs.at[lax.rem(step, downs.shape[0])]
        total[block, :] += jnp.dot(
            hidden[lax.rem(step, 2), block, :], down[...], preferred_element_type=jnp.float32
        )

    wait(0, 0)
    wait(1, 0)
    each_block(lambda block: activate(0, block, *products(jnp.int32(0), block)))

    @pl.loop(1, steps)
    def _(step):
        @pl.when(step - 1 + slots < steps)
        def _():
            start(step - 1 + slots)

        wait(0, step)
        wait(1, step)
        wait(2, step - 1)

        def both(block):
            g, u = products(step, block)
            down_product(step - 1, block)
            activate(step, block, g, u)

        each_block(both)

    wait(2, steps - 1)
    each_block(lambda block: down_product(jnp.int32(steps - 1), block))
    keep_ref[...] = total[:half, :]
    send_ref[...] = total[half:, :].astype(jnp.bfloat16)


def build(axes):
    def local(tokens, expert_ids, gate_numer, w_gate, w_up, w_down):
        local_count, ff_dev, depth = w_gate.shape
        units = local_count * ff_dev
        top = expert_ids.shape[1]
        step_units = next(n for n in range(256, 0, -16) if units % n == 0)
        weights = [w.reshape(units, depth) for w in (w_gate, w_up, w_down)]
        weights = [pltpu.with_memory_space_constraint(w, pltpu.HBM) for w in weights]
        small = pltpu.CompilerParams(vmem_limit_bytes=2 << 20)
        own = (tokens, expert_ids, gate_numer)
        own = [pltpu.with_memory_space_constraint(a, pltpu.HBM) for a in own]
        rows = pl.pallas_call(
            with_routing,
            out_shape=jax.ShapeDtypeStruct((tokens.shape[0], depth + SIDE), jnp.bfloat16),
            in_specs=[HBM] * 3,
            out_specs=VMEM,
            scratch_shapes=[
                pltpu.VMEM(expert_ids.shape, jnp.int32),
                pltpu.VMEM(gate_numer.shape, jnp.int32),
                pltpu.SemaphoreType.DMA((3,)),
            ],
            compiler_params=small,
            name="with_routing",
        )(*own)
        hops = [None]
        for axis, size in axes:
            by = size // 2
            while by:
                hops.append((axis, size, by))
                by //= 2
        span = lax.axis_size("wide")
        slots = min(SLOTS, units // step_units)
        ring_shapes = [
            pltpu.VMEM((n, step_units, depth), jnp.bfloat16) for n in (slots, slots, slots + 1)
        ]
        ring = []
        early = (0, 0, 0)
        for number, hop in enumerate(hops):
            if hop is None:
                theirs = [shift(rows, "wide", span, -by) for by in range(1, span)]
            else:
                theirs = [swap(rows, *hop)]
            more = EARLY[number] if number < len(EARLY) and units >= 8 * step_units else (0, 0, 0)
            ends = []
            if max(more):
                *ring, end = pl.pallas_call(
                    functools.partial(bring, early, more),
                    out_shape=ring_shapes + [jax.ShapeDtypeStruct((8, 128), jnp.float32)],
                    in_specs=[HBM] * 3 + [pl.BlockSpec(memory_space=pl.ANY)] + [VMEM] * len(ring),
                    out_specs=[VMEM] * 4,
                    scratch_shapes=[pltpu.SemaphoreType.DMA((3, max(more), 2))],
                    input_output_aliases={4 + i: i for i in range(len(ring))},
                    compiler_params=small,
                    cost_estimate=pl.CostEstimate(
                        flops=0,
                        bytes_accessed=2 * sum(more) * step_units * depth,
                        transcendentals=0,
                    ),
                    name="bring_weights",
                )(*weights, rows, *ring)
                early = tuple(a + b for a, b in zip(early, more))
                ends = [end]
            if hop is hops[-1]:
                break
            all_rows = [rows] + theirs
            count = sum(part.shape[0] for part in all_rows)
            if count <= 64:
                rows = pl.pallas_call(
                    functools.partial(join, len(all_rows)),
                    out_shape=jax.ShapeDtypeStruct((count, depth + SIDE), jnp.bfloat16),
                    in_specs=[VMEM] * len(all_rows)
                    + [pl.BlockSpec(memory_space=pl.ANY)] * len(ends),
                    out_specs=VMEM,
                    compiler_params=small,
                    name="join",
                )(*all_rows, *ends)
            else:
                rows = jnp.concatenate(all_rows, axis=0)
        half = rows.shape[0]
        count = 2 * half
        row_block = min(count, 64)
        keep, send, *_ = pl.pallas_call(
            functools.partial(layer, top, ff_dev, row_block, step_units, early),
            out_shape=[
                jax.ShapeDtypeStruct((half, depth), jnp.float32),
                jax.ShapeDtypeStruct((half, depth), jnp.bfloat16),
            ]
            + (ring_shapes if ring else []),
            in_specs=[VMEM] * 2 + [HBM] * 3 + [VMEM] * len(ring),
            out_specs=[VMEM] * (5 if ring else 2),
            scratch_shapes=([] if ring else ring_shapes)
            + [
                pltpu.VMEM((count, depth + SIDE), jnp.bfloat16),
                pltpu.VMEM((count, depth), jnp.float32),
                pltpu.VMEM((count, SIDE), jnp.bfloat16),
                pltpu.VMEM((2, count, step_units), jnp.bfloat16),
                pltpu.SemaphoreType.DMA((3, slots + 1)),
            ],
            input_output_aliases={5 + i: 2 + i for i in range(len(ring))},
            compiler_params=pltpu.CompilerParams(
                vmem_limit_bytes=GRANT if ring else 60 << 20
            ),
            cost_estimate=pl.CostEstimate(
                flops=6 * count * units * depth,
                bytes_accessed=2 * (3 * units - sum(early) * step_units) * depth,
                transcendentals=count * units,
            ),
            name="expert_layer",
        )(rows, *theirs, *weights, *ring)
        total = keep + swap(send, *hops[-1]).astype(jnp.float32)
        for hop in reversed(hops[1:-1]):
            half = total.shape[0] // 2
            theirs = swap(total[half:].astype(jnp.bfloat16), *hop)
            total = total[:half] + theirs.astype(jnp.float32)
        blocks = total.reshape(span, tokens.shape[0], depth)
        total = blocks[0]
        for by in range(1, span):
            theirs = shift(blocks[by].astype(jnp.bfloat16), "wide", span, by)
            total = total + theirs.astype(jnp.float32)
        return total.astype(jnp.bfloat16)

    return local


def solution(mesh):
    rows = P(("grp", "wide", "sec", "sub"), None)
    weights = P("wide", ("sec", "sub"), None)
    axes = [(name, mesh.shape[name]) for name in ("sec", "sub")]
    return jax.shard_map(
        build(axes),
        mesh=mesh,
        in_specs=(rows, rows, rows, weights, weights, weights),
        out_specs=rows,
        check_vma=False,
    )
```

```python
import functools
import math

import jax
import jax.numpy as jnp
from jax import lax
from jax.experimental import pallas as pl
from jax.experimental.pallas import tpu as pltpu
from jax.sharding import PartitionSpec as P

EXPERTS = 32
SIDE = 128
SLOTS = 4
EARLY = ((1, 1, 1), (2, 1, 1))
GRANT = 8 << 20

VMEM = pl.BlockSpec(memory_space=pltpu.VMEM)
HBM = pl.BlockSpec(memory_space=pltpu.HBM)
LAST = (((1,), (1,)), ((), ()))


def swap(x, axis, size, by):
    return lax.ppermute(x, axis, [(i, i ^ by) for i in range(size)])


def shift(x, axis, size, by):
    return lax.ppermute(x, axis, [(i, (i + by) % size) for i in range(size)])


def with_routing(tokens_ref, ids_ref, numer_ref, out_ref, ids, numer, sem):
    rows, depth = tokens_ref.shape
    top = ids_ref.shape[1]
    pairs = [(tokens_ref, out_ref.at[:, pl.ds(0, depth)]), (ids_ref, ids), (numer_ref, numer)]
    started = [pltpu.make_async_copy(a, b, sem.at[i]) for i, (a, b) in enumerate(pairs)]
    for copy in started:
        copy.start()
    for copy in started:
        copy.wait()
    pad = jnp.zeros((rows, SIDE - 3 * top), jnp.int32)
    side = jnp.concatenate([ids[...], numer[...] >> 5, numer[...] & 31, pad], axis=1)
    out_ref[:, depth:] = side.astype(jnp.float32).astype(jnp.bfloat16)


def join(parts, *refs):
    out_ref = refs[-1]
    count = refs[0].shape[0]
    for part in range(parts):
        out_ref[part * count:(part + 1) * count, :] = refs[part][...]


def bring(firsts, counts, gate_ref, up_ref, down_ref, after_ref, *refs):
    gates, ups, downs, end_ref, sem = refs[-5:]
    size = gates.shape[1]
    half = size // 2
    started = []
    for i, (ref, ring) in enumerate([(gate_ref, gates), (up_ref, ups), (down_ref, downs)]):
        for step in range(firsts[i], firsts[i] + counts[i]):
            for part in range(2):
                started.append(
                    pltpu.make_async_copy(
                        ref.at[pl.ds(step * size + part * half, half)],
                        ring.at[step, pl.ds(part * half, half)],
                        sem.at[i, step - firsts[i], part],
                    )
                )
    for copy in started:
        copy.start()
    end_ref[...] = jnp.zeros_like(end_ref)
    for copy in started:
        copy.wait()


def dense_weights(side, top):
    ids = side[:, :top]
    numer = side[:, top:2 * top] * 32.0 + side[:, 2 * top:3 * top]
    weight = numer / jnp.sum(numer, axis=-1, keepdims=True)
    expert = lax.broadcasted_iota(jnp.int32, (side.shape[0], SIDE), 1).astype(jnp.float32)
    full = jnp.zeros((side.shape[0], SIDE), jnp.float32)
    for k in range(top):
        full = full + jnp.where(expert == ids[:, k:k + 1], weight[:, k:k + 1], 0.0)
    return jnp.transpose(full)


def layer(top, ff_dev, row_block, step_units, early, mine_ref, theirs_ref, gate_ref, up_ref,
          down_ref, *refs):
    if max(early):
        refs = refs[3:]
    keep_ref, send_ref, gates, ups, downs, rows_ref, total, weights, hidden, sem = refs
    units, depth = down_ref.shape
    steps = units // step_units
    count = rows_ref.shape[0]
    half = count // 2
    slots = gates.shape[0]

    def copy_of(i, step):
        src, ring = [(gate_ref, gates), (up_ref, ups), (down_ref, downs)][i]
        slot = lax.rem(step, ring.shape[0])
        span = pl.ds(pl.multiple_of(step * step_units, step_units), step_units)
        return pltpu.make_async_copy(src.at[span], ring.at[slot], sem.at[i, slot])

    def start(step):
        for i in range(3):
            copy_of(i, step).start()

    def wait(i, step):
        if isinstance(step, int):
            if step >= early[i]:
                copy_of(i, jnp.int32(step)).wait()
        else:
            @pl.when(step >= early[i])
            def _():
                copy_of(i, step).wait()

    for step in range(min(slots, steps)):
        for i in range(3):
            if step >= early[i]:
                copy_of(i, jnp.int32(step)).start()

    first = lax.axis_index("wide") * (units // ff_dev)

    def each_block(body):
        if count == row_block:
            body(0, pl.ds(0, row_block))
        else:
            @pl.loop(0, count // row_block)
            def _(b):
                body(b, pl.ds(pl.multiple_of(b * row_block, row_block), row_block))

    rows_ref[:half, :] = mine_ref[...]
    rows_ref[half:, :] = theirs_ref[...]

    def prepare(b, block):
        side = rows_ref[block, depth:depth + SIDE].astype(jnp.float32)
        weights[b] = dense_weights(side, top)
        total[block, :] = jnp.zeros((row_block, depth), jnp.float32)

    each_block(prepare)

    def products(step, block):
        x = rows_ref[block, :depth]
        gate, up = [ring.at[lax.rem(step, ring.shape[0])] for ring in (gates, ups)]
        g = lax.dot_general(gate[...], x, LAST, preferred_element_type=jnp.float32)
        u = lax.dot_general(up[...], x, LAST, preferred_element_type=jnp.float32)
        return g, u

    def activate(step, b, block, g, u):
        run = math.gcd(step_units, ff_dev)
        h = g / (1.0 + jnp.exp(-g)) * u
        scaled = []
        for low in range(0, step_units, run):
            expert = first + lax.div(step * step_units + low, jnp.int32(ff_dev))
            scaled.append(h[low:low + run, :] * weights[b, pl.ds(expert, 1), :])
        h = jnp.concatenate(scaled, axis=0)
        hidden[lax.rem(step, 2), block, :] = jnp.transpose(h).astype(jnp.bfloat16)

    def down_product(step, block):
        down = downs.at[lax.rem(step, downs.shape[0])]
        total[block, :] += jnp.dot(
            hidden[lax.rem(step, 2), block, :], down[...], preferred_element_type=jnp.float32
        )

    wait(0, 0)
    wait(1, 0)
    each_block(lambda b, block: activate(jnp.int32(0), b, block, *products(jnp.int32(0), block)))

    @pl.loop(1, steps)
    def _(step):
        @pl.when(step - 1 + slots < steps)
        def _():
            start(step - 1 + slots)

        wait(0, step)
        wait(1, step)
        wait(2, step - 1)

        def both(b, block):
            g, u = products(step, block)
            down_product(step - 1, block)
            activate(step, b, block, g, u)

        each_block(both)

    wait(2, steps - 1)
    each_block(lambda b, block: down_product(jnp.int32(steps - 1), block))
    keep_ref[...] = total[:half, :]
    send_ref[...] = total[half:, :].astype(jnp.bfloat16)


def build(axes):
    def local(tokens, expert_ids, gate_numer, w_gate, w_up, w_down):
        local_count, ff_dev, depth = w_gate.shape
        units = local_count * ff_dev
        top = expert_ids.shape[1]
        step_units = next(n for n in range(256, 0, -16) if units % n == 0)
        weights = [w.reshape(units, depth) for w in (w_gate, w_up, w_down)]
        weights = [pltpu.with_memory_space_constraint(w, pltpu.HBM) for w in weights]
        small = pltpu.CompilerParams(vmem_limit_bytes=2 << 20)
        own = (tokens, expert_ids, gate_numer)
        own = [pltpu.with_memory_space_constraint(a, pltpu.HBM) for a in own]
        rows = pl.pallas_call(
            with_routing,
            out_shape=jax.ShapeDtypeStruct((tokens.shape[0], depth + SIDE), jnp.bfloat16),
            in_specs=[HBM] * 3,
            out_specs=VMEM,
            scratch_shapes=[
                pltpu.VMEM(expert_ids.shape, jnp.int32),
                pltpu.VMEM(gate_numer.shape, jnp.int32),
                pltpu.SemaphoreType.DMA((3,)),
            ],
            compiler_params=small,
            name="with_routing",
        )(*own)
        hops = [None]
        for axis, size in axes:
            by = size // 2
            while by:
                hops.append((axis, size, by))
                by //= 2
        span = lax.axis_size("wide")
        slots = min(SLOTS, units // step_units)
        ring_shapes = [
            pltpu.VMEM((n, step_units, depth), jnp.bfloat16) for n in (slots, slots, slots + 1)
        ]
        ring = []
        early = (0, 0, 0)
        for number, hop in enumerate(hops):
            if hop is None:
                theirs = [shift(rows, "wide", span, -by) for by in range(1, span)]
            else:
                theirs = [swap(rows, *hop)]
            more = EARLY[number] if number < len(EARLY) and units >= 8 * step_units else (0, 0, 0)
            ends = []
            if max(more):
                *ring, end = pl.pallas_call(
                    functools.partial(bring, early, more),
                    out_shape=ring_shapes + [jax.ShapeDtypeStruct((8, 128), jnp.float32)],
                    in_specs=[HBM] * 3 + [pl.BlockSpec(memory_space=pl.ANY)] + [VMEM] * len(ring),
                    out_specs=[VMEM] * 4,
                    scratch_shapes=[pltpu.SemaphoreType.DMA((3, max(more), 2))],
                    input_output_aliases={4 + i: i for i in range(len(ring))},
                    compiler_params=small,
                    cost_estimate=pl.CostEstimate(
                        flops=0,
                        bytes_accessed=2 * sum(more) * step_units * depth,
                        transcendentals=0,
                    ),
                    name="bring_weights",
                )(*weights, rows, *ring)
                early = tuple(a + b for a, b in zip(early, more))
                ends = [end]
            if hop is hops[-1]:
                break
            all_rows = [rows] + theirs
            count = sum(part.shape[0] for part in all_rows)
            if count <= 64:
                rows = pl.pallas_call(
                    functools.partial(join, len(all_rows)),
                    out_shape=jax.ShapeDtypeStruct((count, depth + SIDE), jnp.bfloat16),
                    in_specs=[VMEM] * len(all_rows)
                    + [pl.BlockSpec(memory_space=pl.ANY)] * len(ends),
                    out_specs=VMEM,
                    compiler_params=small,
                    name="join",
                )(*all_rows, *ends)
            else:
                rows = jnp.concatenate(all_rows, axis=0)
        half = rows.shape[0]
        count = 2 * half
        row_block = min(count, 64)
        keep, send, *_ = pl.pallas_call(
            functools.partial(layer, top, ff_dev, row_block, step_units, early),
            out_shape=[
                jax.ShapeDtypeStruct((half, depth), jnp.float32),
                jax.ShapeDtypeStruct((half, depth), jnp.bfloat16),
            ]
            + (ring_shapes if ring else []),
            in_specs=[VMEM] * 2 + [HBM] * 3 + [VMEM] * len(ring),
            out_specs=[VMEM] * (5 if ring else 2),
            scratch_shapes=([] if ring else ring_shapes)
            + [
                pltpu.VMEM((count, depth + SIDE), jnp.bfloat16),
                pltpu.VMEM((count, depth), jnp.float32),
                pltpu.VMEM((count // row_block, SIDE, row_block), jnp.float32),
                pltpu.VMEM((2, count, step_units), jnp.bfloat16),
                pltpu.SemaphoreType.DMA((3, slots + 1)),
            ],
            input_output_aliases={5 + i: 2 + i for i in range(len(ring))},
            compiler_params=pltpu.CompilerParams(
                vmem_limit_bytes=GRANT if ring else 60 << 20
            ),
            cost_estimate=pl.CostEstimate(
                flops=6 * count * units * depth,
                bytes_accessed=2 * (3 * units - sum(early) * step_units) * depth,
                transcendentals=count * units,
            ),
            name="expert_layer",
        )(rows, *theirs, *weights, *ring)
        total = keep + swap(send, *hops[-1]).astype(jnp.float32)
        for hop in reversed(hops[1:-1]):
            half = total.shape[0] // 2
            theirs = swap(total[half:].astype(jnp.bfloat16), *hop)
            total = total[:half] + theirs.astype(jnp.float32)
        blocks = total.reshape(span, tokens.shape[0], depth)
        total = blocks[0]
        for by in range(1, span):
            theirs = shift(blocks[by].astype(jnp.bfloat16), "wide", span, by)
            total = total + theirs.astype(jnp.float32)
        return total.astype(jnp.bfloat16)

    return local


def solution(mesh):
    rows = P(("grp", "wide", "sec", "sub"), None)
    weights = P("wide", ("sec", "sub"), None)
    axes = [(name, mesh.shape[name]) for name in ("sec", "sub")]
    return jax.shard_map(
        build(axes),
        mesh=mesh,
        in_specs=(rows, rows, rows, weights, weights, weights),
        out_specs=rows,
        check_vma=False,
    )
```

```python
import functools
import math

import jax
import jax.numpy as jnp
from jax import lax
from jax.experimental import pallas as pl
from jax.experimental.pallas import tpu as pltpu
from jax.sharding import PartitionSpec as P

EXPERTS = 32
SIDE = 128
SLOTS = 4
EARLY = ((1, 1, 1), (2, 1, 1))
GRANT = 8 << 20

VMEM = pl.BlockSpec(memory_space=pltpu.VMEM)
HBM = pl.BlockSpec(memory_space=pltpu.HBM)
LAST = (((1,), (1,)), ((), ()))


def swap(x, axis, size, by):
    return lax.ppermute(x, axis, [(i, i ^ by) for i in range(size)])


def shift(x, axis, size, by):
    return lax.ppermute(x, axis, [(i, (i + by) % size) for i in range(size)])


def with_routing(tokens_ref, ids_ref, numer_ref, out_ref, ids, numer, sem):
    rows, depth = tokens_ref.shape
    top = ids_ref.shape[1]
    pairs = [(tokens_ref, out_ref.at[:, pl.ds(0, depth)]), (ids_ref, ids), (numer_ref, numer)]
    started = [pltpu.make_async_copy(a, b, sem.at[i]) for i, (a, b) in enumerate(pairs)]
    for copy in started:
        copy.start()
    for copy in started:
        copy.wait()
    pad = jnp.zeros((rows, SIDE - 3 * top), jnp.int32)
    side = jnp.concatenate([ids[...], numer[...] >> 5, numer[...] & 31, pad], axis=1)
    out_ref[:, depth:] = side.astype(jnp.float32).astype(jnp.bfloat16)


def join(parts, *refs):
    out_ref = refs[-1]
    count = refs[0].shape[0]
    for part in range(parts):
        out_ref[part * count:(part + 1) * count, :] = refs[part][...]


def bring(firsts, counts, gate_ref, up_ref, down_ref, after_ref, *refs):
    gates, ups, downs, end_ref, sem = refs[-5:]
    size = gates.shape[1]
    half = size // 2
    started = []
    for i, (ref, ring) in enumerate([(gate_ref, gates), (up_ref, ups), (down_ref, downs)]):
        for step in range(firsts[i], firsts[i] + counts[i]):
            for part in range(2):
                started.append(
                    pltpu.make_async_copy(
                        ref.at[pl.ds(step * size + part * half, half)],
                        ring.at[step, pl.ds(part * half, half)],
                        sem.at[i, step - firsts[i], part],
                    )
                )
    for copy in started:
        copy.start()
    end_ref[...] = jnp.zeros_like(end_ref)
    for copy in started:
        copy.wait()


def dense_weights(side, top):
    ids = side[:, :top]
    numer = side[:, top:2 * top] * 32.0 + side[:, 2 * top:3 * top]
    weight = numer / jnp.sum(numer, axis=-1, keepdims=True)
    expert = lax.broadcasted_iota(jnp.int32, (side.shape[0], SIDE), 1).astype(jnp.float32)
    full = jnp.zeros((side.shape[0], SIDE), jnp.float32)
    for k in range(top):
        full = full + jnp.where(expert == ids[:, k:k + 1], weight[:, k:k + 1], 0.0)
    return jnp.transpose(full)


def layer(top, ff_dev, row_block, step_units, early, mine_ref, theirs_ref, gate_ref, up_ref,
          down_ref, *refs):
    if max(early):
        refs = refs[3:]
    keep_ref, send_ref, gates, ups, downs, rows_ref, total, weights, hidden, sem = refs
    units, depth = down_ref.shape
    steps = units // step_units
    count = rows_ref.shape[0]
    half = count // 2
    slots = gates.shape[0]

    def copy_of(i, step):
        src, ring = [(gate_ref, gates), (up_ref, ups), (down_ref, downs)][i]
        slot = lax.rem(step, ring.shape[0])
        span = pl.ds(pl.multiple_of(step * step_units, step_units), step_units)
        return pltpu.make_async_copy(src.at[span], ring.at[slot], sem.at[i, slot])

    ahead = (slots, slots, max(1, slots - 2))

    def wait(i, step):
        if isinstance(step, int):
            if step >= early[i]:
                copy_of(i, jnp.int32(step)).wait()
        else:
            @pl.when(step >= early[i])
            def _():
                copy_of(i, step).wait()

    for step in range(min(slots, steps)):
        for i in range(3):
            if early[i] <= step < ahead[i]:
                copy_of(i, jnp.int32(step)).start()

    first = lax.axis_index("wide") * (units // ff_dev)

    def each_block(body):
        if count == row_block:
            body(0, pl.ds(0, row_block))
        else:
            @pl.loop(0, count // row_block)
            def _(b):
                body(b, pl.ds(pl.multiple_of(b * row_block, row_block), row_block))

    rows_ref[:half, :] = mine_ref[...]
    rows_ref[half:, :] = theirs_ref[...]

    def prepare(b, block):
        side = rows_ref[block, depth:depth + SIDE].astype(jnp.float32)
        weights[b] = dense_weights(side, top)
        total[block, :] = jnp.zeros((row_block, depth), jnp.float32)

    each_block(prepare)

    def products(step, block):
        x = rows_ref[block, :depth]
        gate, up = [ring.at[lax.rem(step, ring.shape[0])] for ring in (gates, ups)]
        g = lax.dot_general(gate[...], x, LAST, preferred_element_type=jnp.float32)
        u = lax.dot_general(up[...], x, LAST, preferred_element_type=jnp.float32)
        return g, u

    def activate(step, b, block, g, u):
        run = math.gcd(step_units, ff_dev)
        h = g / (1.0 + jnp.exp(-g)) * u
        scaled = []
        for low in range(0, step_units, run):
            expert = first + lax.div(step * step_units + low, jnp.int32(ff_dev))
            scaled.append(h[low:low + run, :] * weights[b, pl.ds(expert, 1), :])
        h = jnp.concatenate(scaled, axis=0)
        hidden[lax.rem(step, 2), block, :] = jnp.transpose(h).astype(jnp.bfloat16)

    def down_product(step, block):
        down = downs.at[lax.rem(step, downs.shape[0])]
        total[block, :] += jnp.dot(
            hidden[lax.rem(step, 2), block, :], down[...], preferred_element_type=jnp.float32
        )

    wait(0, 0)
    wait(1, 0)
    each_block(lambda b, block: activate(jnp.int32(0), b, block, *products(jnp.int32(0), block)))

    @pl.loop(1, steps)
    def _(step):
        @pl.when(step - 1 + ahead[0] < steps)
        def _():
            copy_of(0, step - 1 + ahead[0]).start()
            copy_of(1, step - 1 + ahead[1]).start()

        @pl.when(step - 1 + ahead[2] < steps)
        def _():
            copy_of(2, step - 1 + ahead[2]).start()

        wait(0, step)
        wait(1, step)
        wait(2, step - 1)

        def both(b, block):
            g, u = products(step, block)
            down_product(step - 1, block)
            activate(step, b, block, g, u)

        each_block(both)

    wait(2, steps - 1)
    each_block(lambda b, block: down_product(jnp.int32(steps - 1), block))
    keep_ref[...] = total[:half, :]
    send_ref[...] = total[half:, :].astype(jnp.bfloat16)


def build(axes):
    def local(tokens, expert_ids, gate_numer, w_gate, w_up, w_down):
        local_count, ff_dev, depth = w_gate.shape
        units = local_count * ff_dev
        top = expert_ids.shape[1]
        step_units = next(n for n in range(256, 0, -16) if units % n == 0)
        weights = [w.reshape(units, depth) for w in (w_gate, w_up, w_down)]
        weights = [pltpu.with_memory_space_constraint(w, pltpu.HBM) for w in weights]
        small = pltpu.CompilerParams(vmem_limit_bytes=2 << 20)
        own = (tokens, expert_ids, gate_numer)
        own = [pltpu.with_memory_space_constraint(a, pltpu.HBM) for a in own]
        rows = pl.pallas_call(
            with_routing,
            out_shape=jax.ShapeDtypeStruct((tokens.shape[0], depth + SIDE), jnp.bfloat16),
            in_specs=[HBM] * 3,
            out_specs=VMEM,
            scratch_shapes=[
                pltpu.VMEM(expert_ids.shape, jnp.int32),
                pltpu.VMEM(gate_numer.shape, jnp.int32),
                pltpu.SemaphoreType.DMA((3,)),
            ],
            compiler_params=small,
            name="with_routing",
        )(*own)
        hops = [None]
        for axis, size in axes:
            by = size // 2
            while by:
                hops.append((axis, size, by))
                by //= 2
        span = lax.axis_size("wide")
        slots = min(SLOTS, units // step_units)
        ring_shapes = [
            pltpu.VMEM((n, step_units, depth), jnp.bfloat16) for n in (slots, slots, slots + 1)
        ]
        ring = []
        early = (0, 0, 0)
        for number, hop in enumerate(hops):
            if hop is None:
                theirs = [shift(rows, "wide", span, -by) for by in range(1, span)]
            else:
                theirs = [swap(rows, *hop)]
            more = EARLY[number] if number < len(EARLY) and units >= 8 * step_units else (0, 0, 0)
            ends = []
            if max(more):
                *ring, end = pl.pallas_call(
                    functools.partial(bring, early, more),
                    out_shape=ring_shapes + [jax.ShapeDtypeStruct((8, 128), jnp.float32)],
                    in_specs=[HBM] * 3 + [pl.BlockSpec(memory_space=pl.ANY)] + [VMEM] * len(ring),
                    out_specs=[VMEM] * 4,
                    scratch_shapes=[pltpu.SemaphoreType.DMA((3, max(more), 2))],
                    input_output_aliases={4 + i: i for i in range(len(ring))},
                    compiler_params=small,
                    cost_estimate=pl.CostEstimate(
                        flops=0,
                        bytes_accessed=2 * sum(more) * step_units * depth,
                        transcendentals=0,
                    ),
                    name="bring_weights",
                )(*weights, rows, *ring)
                early = tuple(a + b for a, b in zip(early, more))
                ends = [end]
            if hop is hops[-1]:
                break
            all_rows = [rows] + theirs
            count = sum(part.shape[0] for part in all_rows)
            if count <= 64:
                rows = pl.pallas_call(
                    functools.partial(join, len(all_rows)),
                    out_shape=jax.ShapeDtypeStruct((count, depth + SIDE), jnp.bfloat16),
                    in_specs=[VMEM] * len(all_rows)
                    + [pl.BlockSpec(memory_space=pl.ANY)] * len(ends),
                    out_specs=VMEM,
                    compiler_params=small,
                    name="join",
                )(*all_rows, *ends)
            else:
                rows = jnp.concatenate(all_rows, axis=0)
        half = rows.shape[0]
        count = 2 * half
        row_block = min(count, 64)
        keep, send, *_ = pl.pallas_call(
            functools.partial(layer, top, ff_dev, row_block, step_units, early),
            out_shape=[
                jax.ShapeDtypeStruct((half, depth), jnp.float32),
                jax.ShapeDtypeStruct((half, depth), jnp.bfloat16),
            ]
            + (ring_shapes if ring else []),
            in_specs=[VMEM] * 2 + [HBM] * 3 + [VMEM] * len(ring),
            out_specs=[VMEM] * (5 if ring else 2),
            scratch_shapes=([] if ring else ring_shapes)
            + [
                pltpu.VMEM((count, depth + SIDE), jnp.bfloat16),
                pltpu.VMEM((count, depth), jnp.float32),
                pltpu.VMEM((count // row_block, SIDE, row_block), jnp.float32),
                pltpu.VMEM((2, count, step_units), jnp.bfloat16),
                pltpu.SemaphoreType.DMA((3, slots + 1)),
            ],
            input_output_aliases={5 + i: 2 + i for i in range(len(ring))},
            compiler_params=pltpu.CompilerParams(
                vmem_limit_bytes=GRANT if ring else 60 << 20
            ),
            cost_estimate=pl.CostEstimate(
                flops=6 * count * units * depth,
                bytes_accessed=2 * (3 * units - sum(early) * step_units) * depth,
                transcendentals=count * units,
            ),
            name="expert_layer",
        )(rows, *theirs, *weights, *ring)
        total = keep + swap(send, *hops[-1]).astype(jnp.float32)
        for hop in reversed(hops[1:-1]):
            half = total.shape[0] // 2
            theirs = swap(total[half:].astype(jnp.bfloat16), *hop)
            total = total[:half] + theirs.astype(jnp.float32)
        blocks = total.reshape(span, tokens.shape[0], depth)
        total = blocks[0]
        for by in range(1, span):
            theirs = shift(blocks[by].astype(jnp.bfloat16), "wide", span, by)
            total = total + theirs.astype(jnp.float32)
        return total.astype(jnp.bfloat16)

    return local


def solution(mesh):
    rows = P(("grp", "wide", "sec", "sub"), None)
    weights = P("wide", ("sec", "sub"), None)
    axes = [(name, mesh.shape[name]) for name in ("sec", "sub")]
    return jax.shard_map(
        build(axes),
        mesh=mesh,
        in_specs=(rows, rows, rows, weights, weights, weights),
        out_specs=rows,
        check_vma=False,
    )
```

```python
import functools
import math

import jax
import jax.numpy as jnp
from jax import lax
from jax.experimental import pallas as pl
from jax.experimental.pallas import tpu as pltpu
from jax.sharding import PartitionSpec as P

EXPERTS = 32
SIDE = 128
SLOTS = 6
EARLY = ((1, 1, 1), (2, 1, 1))
GRANT = 8 << 20

VMEM = pl.BlockSpec(memory_space=pltpu.VMEM)
HBM = pl.BlockSpec(memory_space=pltpu.HBM)
LAST = (((1,), (1,)), ((), ()))


def swap(x, axis, size, by):
    return lax.ppermute(x, axis, [(i, i ^ by) for i in range(size)])


def shift(x, axis, size, by):
    return lax.ppermute(x, axis, [(i, (i + by) % size) for i in range(size)])


def with_routing(tokens_ref, ids_ref, numer_ref, out_ref, ids, numer, sem):
    rows, depth = tokens_ref.shape
    top = ids_ref.shape[1]
    pairs = [(tokens_ref, out_ref.at[:, pl.ds(0, depth)]), (ids_ref, ids), (numer_ref, numer)]
    started = [pltpu.make_async_copy(a, b, sem.at[i]) for i, (a, b) in enumerate(pairs)]
    for copy in started:
        copy.start()
    for copy in started:
        copy.wait()
    pad = jnp.zeros((rows, SIDE - 3 * top), jnp.int32)
    side = jnp.concatenate([ids[...], numer[...] >> 5, numer[...] & 31, pad], axis=1)
    out_ref[:, depth:] = side.astype(jnp.float32).astype(jnp.bfloat16)


def join(parts, *refs):
    out_ref = refs[-1]
    count = refs[0].shape[0]
    for part in range(parts):
        out_ref[part * count:(part + 1) * count, :] = refs[part][...]


def bring(firsts, counts, gate_ref, up_ref, down_ref, after_ref, *refs):
    gates, ups, downs, end_ref, sem = refs[-5:]
    size = gates.shape[1]
    half = size // 2
    started = []
    for i, (ref, ring) in enumerate([(gate_ref, gates), (up_ref, ups), (down_ref, downs)]):
        for step in range(firsts[i], firsts[i] + counts[i]):
            for part in range(2):
                started.append(
                    pltpu.make_async_copy(
                        ref.at[pl.ds(step * size + part * half, half)],
                        ring.at[step, pl.ds(part * half, half)],
                        sem.at[i, step - firsts[i], part],
                    )
                )
    for copy in started:
        copy.start()
    end_ref[...] = jnp.zeros_like(end_ref)
    for copy in started:
        copy.wait()


def dense_weights(side, top):
    ids = side[:, :top]
    numer = side[:, top:2 * top] * 32.0 + side[:, 2 * top:3 * top]
    weight = numer / jnp.sum(numer, axis=-1, keepdims=True)
    expert = lax.broadcasted_iota(jnp.int32, (side.shape[0], SIDE), 1).astype(jnp.float32)
    full = jnp.zeros((side.shape[0], SIDE), jnp.float32)
    for k in range(top):
        full = full + jnp.where(expert == ids[:, k:k + 1], weight[:, k:k + 1], 0.0)
    return jnp.transpose(full)


def layer(top, ff_dev, row_block, step_units, early, mine_ref, theirs_ref, gate_ref, up_ref,
          down_ref, *refs):
    if max(early):
        refs = refs[3:]
    keep_ref, send_ref, gates, ups, downs, rows_ref, total, weights, hidden, sem = refs
    units, depth = down_ref.shape
    steps = units // step_units
    count = rows_ref.shape[0]
    half = count // 2
    slots = gates.shape[0]

    def copy_of(i, step):
        src, ring = [(gate_ref, gates), (up_ref, ups), (down_ref, downs)][i]
        slot = lax.rem(step, ring.shape[0])
        span = pl.ds(pl.multiple_of(step * step_units, step_units), step_units)
        return pltpu.make_async_copy(src.at[span], ring.at[slot], sem.at[i, slot])

    def start(step):
        for i in range(3):
            copy_of(i, step).start()

    def wait(i, step):
        if isinstance(step, int):
            if step >= early[i]:
                copy_of(i, jnp.int32(step)).wait()
        else:
            @pl.when(step >= early[i])
            def _():
                copy_of(i, step).wait()

    for step in range(min(slots, steps)):
        for i in range(3):
            if step >= early[i]:
                copy_of(i, jnp.int32(step)).start()

    first = lax.axis_index("wide") * (units // ff_dev)

    def each_block(body):
        if count == row_block:
            body(0, pl.ds(0, row_block))
        else:
            @pl.loop(0, count // row_block)
            def _(b):
                body(b, pl.ds(pl.multiple_of(b * row_block, row_block), row_block))

    rows_ref[:half, :] = mine_ref[...]
    rows_ref[half:, :] = theirs_ref[...]

    def prepare(b, block):
        side = rows_ref[block, depth:depth + SIDE].astype(jnp.float32)
        weights[b] = dense_weights(side, top)
        total[block, :] = jnp.zeros((row_block, depth), jnp.float32)

    each_block(prepare)

    def products(step, block):
        x = rows_ref[block, :depth]
        gate, up = [ring.at[lax.rem(step, ring.shape[0])] for ring in (gates, ups)]
        g = lax.dot_general(gate[...], x, LAST, preferred_element_type=jnp.float32)
        u = lax.dot_general(up[...], x, LAST, preferred_element_type=jnp.float32)
        return g, u

    def activate(step, b, block, g, u):
        run = math.gcd(step_units, ff_dev)
        h = g / (1.0 + jnp.exp(-g)) * u
        scaled = []
        for low in range(0, step_units, run):
            expert = first + lax.div(step * step_units + low, jnp.int32(ff_dev))
            scaled.append(h[low:low + run, :] * weights[b, pl.ds(expert, 1), :])
        h = jnp.concatenate(scaled, axis=0)
        hidden[lax.rem(step, 2), block, :] = jnp.transpose(h).astype(jnp.bfloat16)

    def down_product(step, block):
        down = downs.at[lax.rem(step, downs.shape[0])]
        total[block, :] += jnp.dot(
            hidden[lax.rem(step, 2), block, :], down[...], preferred_element_type=jnp.float32
        )

    wait(0, 0)
    wait(1, 0)
    each_block(lambda b, block: activate(jnp.int32(0), b, block, *products(jnp.int32(0), block)))

    @pl.loop(1, steps)
    def _(step):
        @pl.when(step - 1 + slots < steps)
        def _():
            start(step - 1 + slots)

        wait(0, step)
        wait(1, step)
        wait(2, step - 1)

        def both(b, block):
            g, u = products(step, block)
            down_product(step - 1, block)
            activate(step, b, block, g, u)

        each_block(both)

    wait(2, steps - 1)
    each_block(lambda b, block: down_product(jnp.int32(steps - 1), block))
    keep_ref[...] = total[:half, :]
    send_ref[...] = total[half:, :].astype(jnp.bfloat16)


def build(axes):
    def local(tokens, expert_ids, gate_numer, w_gate, w_up, w_down):
        local_count, ff_dev, depth = w_gate.shape
        units = local_count * ff_dev
        top = expert_ids.shape[1]
        step_units = next(n for n in range(256, 0, -16) if units % n == 0)
        weights = [w.reshape(units, depth) for w in (w_gate, w_up, w_down)]
        weights = [pltpu.with_memory_space_constraint(w, pltpu.HBM) for w in weights]
        small = pltpu.CompilerParams(vmem_limit_bytes=2 << 20)
        own = (tokens, expert_ids, gate_numer)
        own = [pltpu.with_memory_space_constraint(a, pltpu.HBM) for a in own]
        rows = pl.pallas_call(
            with_routing,
            out_shape=jax.ShapeDtypeStruct((tokens.shape[0], depth + SIDE), jnp.bfloat16),
            in_specs=[HBM] * 3,
            out_specs=VMEM,
            scratch_shapes=[
                pltpu.VMEM(expert_ids.shape, jnp.int32),
                pltpu.VMEM(gate_numer.shape, jnp.int32),
                pltpu.SemaphoreType.DMA((3,)),
            ],
            compiler_params=small,
            name="with_routing",
        )(*own)
        hops = [None]
        for axis, size in axes:
            by = size // 2
            while by:
                hops.append((axis, size, by))
                by //= 2
        span = lax.axis_size("wide")
        slots = min(SLOTS, units // step_units)
        ring_shapes = [
            pltpu.VMEM((n, step_units, depth), jnp.bfloat16) for n in (slots, slots, slots + 1)
        ]
        ring = []
        early = (0, 0, 0)
        for number, hop in enumerate(hops):
            if hop is None:
                theirs = [shift(rows, "wide", span, -by) for by in range(1, span)]
            else:
                theirs = [swap(rows, *hop)]
            more = EARLY[number] if number < len(EARLY) and units >= 8 * step_units else (0, 0, 0)
            ends = []
            if max(more):
                *ring, end = pl.pallas_call(
                    functools.partial(bring, early, more),
                    out_shape=ring_shapes + [jax.ShapeDtypeStruct((8, 128), jnp.float32)],
                    in_specs=[HBM] * 3 + [pl.BlockSpec(memory_space=pl.ANY)] + [VMEM] * len(ring),
                    out_specs=[VMEM] * 4,
                    scratch_shapes=[pltpu.SemaphoreType.DMA((3, max(more), 2))],
                    input_output_aliases={4 + i: i for i in range(len(ring))},
                    compiler_params=small,
                    cost_estimate=pl.CostEstimate(
                        flops=0,
                        bytes_accessed=2 * sum(more) * step_units * depth,
                        transcendentals=0,
                    ),
                    name="bring_weights",
                )(*weights, rows, *ring)
                early = tuple(a + b for a, b in zip(early, more))
                ends = [end]
            if hop is hops[-1]:
                break
            all_rows = [rows] + theirs
            count = sum(part.shape[0] for part in all_rows)
            if count <= 64:
                rows = pl.pallas_call(
                    functools.partial(join, len(all_rows)),
                    out_shape=jax.ShapeDtypeStruct((count, depth + SIDE), jnp.bfloat16),
                    in_specs=[VMEM] * len(all_rows)
                    + [pl.BlockSpec(memory_space=pl.ANY)] * len(ends),
                    out_specs=VMEM,
                    compiler_params=small,
                    name="join",
                )(*all_rows, *ends)
            else:
                rows = jnp.concatenate(all_rows, axis=0)
        half = rows.shape[0]
        count = 2 * half
        row_block = min(count, 64)
        keep, send, *_ = pl.pallas_call(
            functools.partial(layer, top, ff_dev, row_block, step_units, early),
            out_shape=[
                jax.ShapeDtypeStruct((half, depth), jnp.float32),
                jax.ShapeDtypeStruct((half, depth), jnp.bfloat16),
            ]
            + (ring_shapes if ring else []),
            in_specs=[VMEM] * 2 + [HBM] * 3 + [VMEM] * len(ring),
            out_specs=[VMEM] * (5 if ring else 2),
            scratch_shapes=([] if ring else ring_shapes)
            + [
                pltpu.VMEM((count, depth + SIDE), jnp.bfloat16),
                pltpu.VMEM((count, depth), jnp.float32),
                pltpu.VMEM((count // row_block, SIDE, row_block), jnp.float32),
                pltpu.VMEM((2, count, step_units), jnp.bfloat16),
                pltpu.SemaphoreType.DMA((3, slots + 1)),
            ],
            input_output_aliases={5 + i: 2 + i for i in range(len(ring))},
            compiler_params=pltpu.CompilerParams(
                vmem_limit_bytes=GRANT if ring else 60 << 20
            ),
            cost_estimate=pl.CostEstimate(
                flops=6 * count * units * depth,
                bytes_accessed=2 * (3 * units - sum(early) * step_units) * depth,
                transcendentals=count * units,
            ),
            name="expert_layer",
        )(rows, *theirs, *weights, *ring)
        total = keep + swap(send, *hops[-1]).astype(jnp.float32)
        for hop in reversed(hops[1:-1]):
            half = total.shape[0] // 2
            theirs = swap(total[half:].astype(jnp.bfloat16), *hop)
            total = total[:half] + theirs.astype(jnp.float32)
        blocks = total.reshape(span, tokens.shape[0], depth)
        total = blocks[0]
        for by in range(1, span):
            theirs = shift(blocks[by].astype(jnp.bfloat16), "wide", span, by)
            total = total + theirs.astype(jnp.float32)
        return total.astype(jnp.bfloat16)

    return local


def solution(mesh):
    rows = P(("grp", "wide", "sec", "sub"), None)
    weights = P("wide", ("sec", "sub"), None)
    axes = [(name, mesh.shape[name]) for name in ("sec", "sub")]
    return jax.shard_map(
        build(axes),
        mesh=mesh,
        in_specs=(rows, rows, rows, weights, weights, weights),
        out_specs=rows,
        check_vma=False,
    )
```

```python
import functools
import math

import jax
import jax.numpy as jnp
from jax import lax
from jax.experimental import pallas as pl
from jax.experimental.pallas import tpu as pltpu
from jax.sharding import PartitionSpec as P

EXPERTS = 32
SIDE = 128
SLOTS = 4
EARLY = ((1, 1, 1), (2, 1, 1))
GRANT = 8 << 20

VMEM = pl.BlockSpec(memory_space=pltpu.VMEM)
HBM = pl.BlockSpec(memory_space=pltpu.HBM)
LAST = (((1,), (1,)), ((), ()))


def swap(x, axis, size, by):
    return lax.ppermute(x, axis, [(i, i ^ by) for i in range(size)])


def shift(x, axis, size, by):
    return lax.ppermute(x, axis, [(i, (i + by) % size) for i in range(size)])


def with_routing(tokens_ref, ids_ref, numer_ref, out_ref, ids, numer, sem):
    rows, depth = tokens_ref.shape
    top = ids_ref.shape[1]
    pairs = [(tokens_ref, out_ref.at[:, pl.ds(0, depth)]), (ids_ref, ids), (numer_ref, numer)]
    started = [pltpu.make_async_copy(a, b, sem.at[i]) for i, (a, b) in enumerate(pairs)]
    for copy in started:
        copy.start()
    for copy in started:
        copy.wait()
    pad = jnp.zeros((rows, SIDE - 3 * top), jnp.int32)
    side = jnp.concatenate([ids[...], numer[...] >> 5, numer[...] & 31, pad], axis=1)
    out_ref[:, depth:] = side.astype(jnp.float32).astype(jnp.bfloat16)


def join(parts, *refs):
    out_ref = refs[-1]
    count = refs[0].shape[0]
    for part in range(parts):
        out_ref[part * count:(part + 1) * count, :] = refs[part][...]


def bring(firsts, counts, gate_ref, up_ref, down_ref, after_ref, *refs):
    gates, ups, downs, end_ref, sem = refs[-5:]
    size = gates.shape[1]
    half = size // 2
    started = []
    for i, (ref, ring) in enumerate([(gate_ref, gates), (up_ref, ups), (down_ref, downs)]):
        for step in range(firsts[i], firsts[i] + counts[i]):
            for part in range(2):
                started.append(
                    pltpu.make_async_copy(
                        ref.at[pl.ds(step * size + part * half, half)],
                        ring.at[step, pl.ds(part * half, half)],
                        sem.at[i, step - firsts[i], part],
                    )
                )
    for copy in started:
        copy.start()
    end_ref[...] = jnp.zeros_like(end_ref)
    for copy in started:
        copy.wait()


def dense_weights(side, top):
    ids = side[:, :top]
    numer = side[:, top:2 * top] * 32.0 + side[:, 2 * top:3 * top]
    weight = numer / jnp.sum(numer, axis=-1, keepdims=True)
    expert = lax.broadcasted_iota(jnp.int32, (side.shape[0], SIDE), 1).astype(jnp.float32)
    full = jnp.zeros((side.shape[0], SIDE), jnp.float32)
    for k in range(top):
        full = full + jnp.where(expert == ids[:, k:k + 1], weight[:, k:k + 1], 0.0)
    return jnp.transpose(full)


def layer(top, ff_dev, row_block, step_units, early, mine_ref, theirs_ref, gate_ref, up_ref,
          down_ref, *refs):
    if max(early):
        refs = refs[3:]
    keep_ref, send_ref, gates, ups, downs, rows_ref, total, weights, hidden, sem = refs
    units, depth = down_ref.shape
    steps = units // step_units
    count = rows_ref.shape[0]
    half = count // 2
    slots = gates.shape[0]

    def copy_of(i, step):
        src, ring = [(gate_ref, gates), (up_ref, ups), (down_ref, downs)][i]
        slot = lax.rem(step, ring.shape[0])
        span = pl.ds(pl.multiple_of(step * step_units, step_units), step_units)
        return pltpu.make_async_copy(src.at[span], ring.at[slot], sem.at[i, slot])

    def start(step):
        for i in range(3):
            copy_of(i, step).start()

    def wait(i, step):
        if isinstance(step, int):
            if step >= early[i]:
                copy_of(i, jnp.int32(step)).wait()
        else:
            @pl.when(step >= early[i])
            def _():
                copy_of(i, step).wait()

    for step in range(min(slots, steps)):
        for i in range(3):
            if step >= early[i]:
                copy_of(i, jnp.int32(step)).start()

    first = lax.axis_index("wide") * (units // ff_dev)

    def each_block(body):
        if count == row_block:
            body(0, pl.ds(0, row_block))
        else:
            @pl.loop(0, count // row_block)
            def _(b):
                body(b, pl.ds(pl.multiple_of(b * row_block, row_block), row_block))

    rows_ref[:half, :] = mine_ref[...]
    rows_ref[half:, :] = theirs_ref[...]

    def prepare(b, block):
        side = rows_ref[block, depth:depth + SIDE].astype(jnp.float32)
        weights[b] = dense_weights(side, top)
        total[block, :] = jnp.zeros((row_block, depth), jnp.float32)

    each_block(prepare)

    def products(step, block):
        x = rows_ref[block, :depth]
        gate, up = [ring.at[lax.rem(step, ring.shape[0])] for ring in (gates, ups)]
        g = lax.dot_general(gate[...], x, LAST, preferred_element_type=jnp.float32)
        u = lax.dot_general(up[...], x, LAST, preferred_element_type=jnp.float32)
        return g, u

    def activate(step, b, block, g, u):
        run = math.gcd(step_units, ff_dev)
        h = g / (1.0 + jnp.exp(-g)) * u
        scaled = []
        for low in range(0, step_units, run):
            expert = first + lax.div(step * step_units + low, jnp.int32(ff_dev))
            scaled.append(h[low:low + run, :] * weights[b, pl.ds(expert, 1), :])
        h = jnp.concatenate(scaled, axis=0)
        hidden[lax.rem(step, 2), block, :] = jnp.transpose(h).astype(jnp.bfloat16)

    def down_product(step, block):
        down = downs.at[lax.rem(step, downs.shape[0])]
        total[block, :] += jnp.dot(
            hidden[lax.rem(step, 2), block, :], down[...], preferred_element_type=jnp.float32
        )

    wait(0, 0)
    wait(1, 0)
    each_block(lambda b, block: activate(jnp.int32(0), b, block, *products(jnp.int32(0), block)))

    @pl.loop(1, steps)
    def _(step):
        @pl.when(step - 1 + slots < steps)
        def _():
            start(step - 1 + slots)

        wait(0, step)
        wait(1, step)
        wait(2, step - 1)

        def both(b, block):
            g, u = products(step, block)
            down_product(step - 1, block)
            activate(step, b, block, g, u)

        each_block(both)

    wait(2, steps - 1)
    each_block(lambda b, block: down_product(jnp.int32(steps - 1), block))
    keep_ref[...] = total[:half, :]
    send_ref[...] = total[half:, :].astype(jnp.bfloat16)


def build(axes):
    def local(tokens, expert_ids, gate_numer, w_gate, w_up, w_down):
        local_count, ff_dev, depth = w_gate.shape
        units = local_count * ff_dev
        top = expert_ids.shape[1]
        step_units = next(n for n in range(256, 0, -16) if units % n == 0)
        weights = [w.reshape(units, depth) for w in (w_gate, w_up, w_down)]
        weights = [pltpu.with_memory_space_constraint(w, pltpu.HBM) for w in weights]
        small = pltpu.CompilerParams(vmem_limit_bytes=2 << 20)
        own = (tokens, expert_ids, gate_numer)
        own = [pltpu.with_memory_space_constraint(a, pltpu.HBM) for a in own]
        rows = pl.pallas_call(
            with_routing,
            out_shape=jax.ShapeDtypeStruct((tokens.shape[0], depth + SIDE), jnp.bfloat16),
            in_specs=[HBM] * 3,
            out_specs=VMEM,
            scratch_shapes=[
                pltpu.VMEM(expert_ids.shape, jnp.int32),
                pltpu.VMEM(gate_numer.shape, jnp.int32),
                pltpu.SemaphoreType.DMA((3,)),
            ],
            compiler_params=small,
            name="with_routing",
        )(*own)
        hops = [None]
        for axis, size in axes:
            by = size // 2
            while by:
                hops.append((axis, size, by))
                by //= 2
        span = lax.axis_size("wide")
        slots = min(SLOTS, units // step_units)
        ring_shapes = [
            pltpu.VMEM((n, step_units, depth), jnp.bfloat16) for n in (slots, slots, slots + 1)
        ]
        ring = []
        early = (0, 0, 0)
        for number, hop in enumerate(hops):
            if hop is None:
                theirs = [shift(rows, "wide", span, -by) for by in range(1, span)]
            else:
                theirs = [swap(rows, *hop)]
            more = EARLY[number] if number < len(EARLY) and units >= 8 * step_units else (0, 0, 0)
            ends = []
            if max(more):
                *ring, end = pl.pallas_call(
                    functools.partial(bring, early, more),
                    out_shape=ring_shapes + [jax.ShapeDtypeStruct((8, 128), jnp.float32)],
                    in_specs=[HBM] * 3 + [pl.BlockSpec(memory_space=pl.ANY)] + [VMEM] * len(ring),
                    out_specs=[VMEM] * 4,
                    scratch_shapes=[pltpu.SemaphoreType.DMA((3, max(more), 2))],
                    input_output_aliases={4 + i: i for i in range(len(ring))},
                    compiler_params=small,
                    cost_estimate=pl.CostEstimate(
                        flops=0,
                        bytes_accessed=2 * sum(more) * step_units * depth,
                        transcendentals=0,
                    ),
                    name="bring_weights",
                )(*weights, rows, *ring)
                early = tuple(a + b for a, b in zip(early, more))
                ends = [end]
            if hop is hops[-1]:
                break
            all_rows = [rows] + theirs
            count = sum(part.shape[0] for part in all_rows)
            if count <= 64:
                rows = pl.pallas_call(
                    functools.partial(join, len(all_rows)),
                    out_shape=jax.ShapeDtypeStruct((count, depth + SIDE), jnp.bfloat16),
                    in_specs=[VMEM] * len(all_rows)
                    + [pl.BlockSpec(memory_space=pl.ANY)] * len(ends),
                    out_specs=VMEM,
                    compiler_params=small,
                    name="join",
                )(*all_rows, *ends)
            else:
                rows = jnp.concatenate(all_rows, axis=0)
        half = rows.shape[0]
        count = 2 * half
        row_block = min(count, 64)
        keep, send, *_ = pl.pallas_call(
            functools.partial(layer, top, ff_dev, row_block, step_units, early),
            out_shape=[
                jax.ShapeDtypeStruct((half, depth), jnp.float32),
                jax.ShapeDtypeStruct((half, depth), jnp.bfloat16),
            ]
            + (ring_shapes if ring else []),
            in_specs=[VMEM] * 2 + [HBM] * 3 + [VMEM] * len(ring),
            out_specs=[VMEM] * (5 if ring else 2),
            scratch_shapes=([] if ring else ring_shapes)
            + [
                pltpu.VMEM((count, depth + SIDE), jnp.bfloat16),
                pltpu.VMEM((count, depth), jnp.float32),
                pltpu.VMEM((count // row_block, SIDE, row_block), jnp.float32),
                pltpu.VMEM((2, count, step_units), jnp.bfloat16),
                pltpu.SemaphoreType.DMA((3, slots + 1)),
            ],
            input_output_aliases={5 + i: 2 + i for i in range(len(ring))},
            compiler_params=pltpu.CompilerParams(
                vmem_limit_bytes=GRANT if ring else 60 << 20
            ),
            cost_estimate=pl.CostEstimate(
                flops=6 * count * units * depth,
                bytes_accessed=2 * (3 * units - sum(early) * step_units) * depth,
                transcendentals=count * units,
            ),
            name="expert_layer",
        )(rows, *theirs, *weights, *ring)
        total = keep + swap(send, *hops[-1]).astype(jnp.float32)
        for hop in reversed(hops[1:-1]):
            half = total.shape[0] // 2
            theirs = swap(total[half:].astype(jnp.bfloat16), *hop)
            total = total[:half] + theirs.astype(jnp.float32)
        blocks = total.reshape(span, tokens.shape[0], depth)
        total = blocks[0]
        for by in reversed(range(1, span)):
            theirs = shift(blocks[by].astype(jnp.bfloat16), "wide", span, by)
            total = total + theirs.astype(jnp.float32)
        return total.astype(jnp.bfloat16)

    return local


def solution(mesh):
    rows = P(("grp", "wide", "sec", "sub"), None)
    weights = P("wide", ("sec", "sub"), None)
    axes = [(name, mesh.shape[name]) for name in ("sec", "sub")]
    return jax.shard_map(
        build(axes),
        mesh=mesh,
        in_specs=(rows, rows, rows, weights, weights, weights),
        out_specs=rows,
        check_vma=False,
    )
```
